32 devices in a mesh: dp: 8 (over y, x, core), tensor: 4 (over z).
Axes of the slice: x: 2, y: 2, z: 4, core: 2. Of those that a mesh axis runs over, the one named last changes fastest.
Arguments:
- inputs: bfloat16 [2, 8, 1024, 1024], P(None, 'dp', 'tensor'), may hold values from -6 to 6
- segment_ids: int32 [2, 8, 1024], P(None, 'dp'), may hold values from 0 to 2, never falling along the last dimension, each value on 1 to 512 neighbouring positions
- norm1_gain: bfloat16 [2, 1024], P(None, 'dp'), may hold values from 0.099609375 to 1.8984375
- norm1_shift: bfloat16 [2, 1024], P(None, 'dp'), may hold values from -1.25 to 1.25
- w_query: bfloat16 [2, 1024, 1024], P(None, 'dp', 'tensor'), may hold values from -0.1875 to 0.1875
- w_key: bfloat16 [2, 1024, 1024], P(None, 'dp', 'tensor'), may hold values from -0.1875 to 0.1875
- w_value: bfloat16 [2, 1024, 1024], P(None, 'dp', 'tensor'), may hold values from -0.1875 to 0.1875
- w_output: bfloat16 [2, 1024, 1024], P(None, 'tensor', 'dp'), may hold values from -2.5 to 2.5
- norm2_gain: bfloat16 [2, 1024], P(None, 'dp'), may hold values from 0.099609375 to 1.8984375
- norm2_shift: bfloat16 [2, 1024], P(None, 'dp'), may hold values from -1.25 to 1.25
- w_fc_in: bfloat16 [2, 1024, 4096], P(None, 'dp', 'tensor'), may hold values from -0.1875 to 0.1875
- w_fc_out: bfloat16 [2, 4096, 1024], P(None, 'tensor', 'dp'), may hold values from -0.09375 to 0.09375
- cotangent: bfloat16 [2, 8, 1024, 1024], P(None, 'dp', 'tensor'), may hold values from -6 to 6
Outputs:
- block_output: float32 [2, 8, 1024, 1024], P(None, 'dp', 'tensor')
- input_grad: float32 [2, 8, 1024, 1024], P(None, 'dp', 'tensor')
- grad_norm1_gain: float32 [2, 1024], P(None, 'dp')
- grad_norm1_shift: float32 [2, 1024], P(None, 'dp')
- grad_w_query: float32 [2, 1024, 1024], P(None, 'dp', 'tensor')
- grad_w_key: float32 [2, 1024, 1024], P(None, 'dp', 'tensor')
- grad_w_value: float32 [2, 1024, 1024], P(None, 'dp', 'tensor')
- grad_w_output: float32 [2, 1024, 1024], P(None, 'tensor', 'dp')
- grad_norm2_gain: float32 [2, 1024], P(None, 'dp')
- grad_norm2_shift: float32 [2, 1024], P(None, 'dp')
- grad_w_fc_in: float32 [2, 1024, 4096], P(None, 'dp', 'tensor')
- grad_w_fc_out: float32 [2, 4096, 1024], P(None, 'tensor', 'dp')
The draws below stay inside these ranges and needn't reach their ends.
Inputs may be any that keep to these rules, and one draw needn't show every extreme that they name: `segment_ids`: along each sequence the ids never fall; each of the three scenes of a sequence is one run of 1 to 512 tokens.
All inputs are finite; a program needn't handle non-finite values.
Results may differ from the reference program's by a relative error of at most 0.023.
Values may be sent and summed in bfloat16 or wider, within the bound.
A program may use at most 320 MiB of HBM per device.

```python
import math
import jax
import jax.numpy as jnp
import numpy as np
from jax import lax

D = 1024
HEADS = 16
FF = 4096
SEQ = 1024
MB = 2
LAYERS = 2
SEQS = 8


def block_levels(stream_key, dims, cuts, smallest, largest):
    gain, own = 1.0, jax.random.fold_in(stream_key, 6)
    for position, parts in cuts:
        draws = jnp.exp(jax.random.uniform(jax.random.fold_in(own, position), (parts,), jnp.float32, smallest / len(cuts), largest / len(cuts)))
        gain = gain * jnp.repeat(draws, dims[position] // parts).reshape([-1 if axis == position else 1 for axis in range(len(dims))])
    return gain


def split_up(number_of, total, reach, lean):
    portions = [(1 << 20) // math.isqrt(standing ** lean) + 1 for standing in range(2, number_of + 1)]
    rest, holding = total - reach - (number_of - 1), [1] * (number_of - 1)
    while rest > 0:
        candidates = [i for i in range(number_of - 1) if holding[i] < reach]
        mass, remaining = sum([portions[i] for i in candidates]), rest
        for i in candidates:
            addition = min(reach - holding[i], max(1, remaining * portions[i] // mass), rest)
            holding[i] = holding[i] + addition
            rest = rest - addition
    return np.array([reach] + holding)


def ragged(stream_key, number_of, total, reach, slope):
    if number_of == 2:
        one = jax.random.randint(stream_key, (), max(1, total - reach), min(reach, total - 1) + 1)
        return jnp.stack([one, total - one])
    tallies = jnp.asarray(split_up(number_of, total, reach, slope), jnp.int32)
    couples = (number_of - 1) // 2
    source_of, sink = tallies[1:1 + 2 * couples:2], tallies[2:2 + 2 * couples:2]
    margin = jnp.minimum(source_of - 1, reach - sink)
    passed = jax.random.randint(jax.random.fold_in(stream_key, 1), (couples,), 0, 1 << 20) % (margin + 1)
    tallies = tallies.at[1:1 + 2 * couples:2].set(source_of - passed).at[2:2 + 2 * couples:2].set(sink + passed)
    return tallies[jax.random.permutation(jax.random.fold_in(stream_key, 2), number_of)]


def gaussian(own_key, extent, scale, reach, shards=(), dtype=jnp.bfloat16):
    gain = block_levels(own_key, extent, shards, -0.22, 0.18) if shards else 1.0
    result = jax.random.normal(own_key, extent, jnp.float32) * scale * gain
    return jnp.minimum(jnp.maximum(result, -reach), reach).astype(dtype)


def setup_inputs(seed: int = 0) -> dict:
    keys = jax.random.split(jax.random.key(seed), 14)
    return {
        "inputs": gaussian(keys[0], (MB, SEQS, SEQ, D), 1.0, 6.0, ((1, 8), (2, 4))),
        "segment_ids": jax.vmap(lambda own: jnp.searchsorted(jnp.cumsum(ragged(own, 3, SEQ, SEQ // 2, 1)), jnp.arange(SEQ), side="right"))(jax.random.split(keys[1], MB * SEQS)).reshape((MB, SEQS, SEQ)).astype(jnp.int32),
        "norm1_gain": jnp.clip(1.0 + 0.18 * jax.random.normal(keys[2], (LAYERS, D), jnp.float32), 0.099609375, 1.8984375).astype(jnp.bfloat16),
        "norm1_shift": gaussian(keys[3], (LAYERS, D), 0.2, 1.25, ((1, 8),)),
        "w_query": gaussian(keys[4], (LAYERS, D, D), D ** -0.5, 0.1875, ((1, 8), (2, 4))),
        "w_key": gaussian(keys[5], (LAYERS, D, D), D ** -0.5, 0.1875, ((1, 8), (2, 4))),
        "w_value": gaussian(keys[6], (LAYERS, D, D), D ** -0.5, 0.1875, ((1, 8), (2, 4))),
        "w_output": gaussian(keys[7], (LAYERS, D, D), (max(1, 6 * D // SEQ)) ** -0.5, 2.5, ((1, 4), (2, 8))),
        "norm2_gain": jnp.clip(1.0 + 0.18 * jax.random.normal(keys[8], (LAYERS, D), jnp.float32), 0.099609375, 1.8984375).astype(jnp.bfloat16),
        "norm2_shift": gaussian(keys[9], (LAYERS, D), 0.2, 1.25, ((1, 8),)),
        "w_fc_in": gaussian(keys[10], (LAYERS, D, FF), D ** -0.5, 0.1875, ((1, 8), (2, 4))),
        "w_fc_out": gaussian(keys[11], (LAYERS, FF, D), FF ** -0.5, 0.09375, ((1, 4), (2, 8))),
        "cotangent": gaussian(keys[12], (MB, SEQS, SEQ, D), 1.0, 6.0, ((1, 8), (2, 4))),
    }


@jax.custom_vjp
def low(v):
    return lax.optimization_barrier(v.astype(jnp.bfloat16)).astype(jnp.float32)

@jax.custom_vjp
def low_back(v):
    return v

def low_keep(v):
    return (low(v), None)

def low_pass(kept, grad):
    return (grad,)

def back_keep(v):
    return (v, None)

def back_low(kept, grad):
    return (low(grad),)
low.defvjp(low_keep, low_pass)
low_back.defvjp(back_keep, back_low)
highest = lax.Precision.HIGHEST

def layer_norm(token_rows, gain_vec, shift_vec):
    center = token_rows - lax.optimization_barrier(jnp.mean(token_rows, axis=-1, keepdims=True))
    spread = lax.optimization_barrier(jnp.mean(center * center, axis=-1, keepdims=True))
    return center * lax.rsqrt(spread + 1e-05) * gain_vec + shift_vec

def scene_attention(queries, key_heads, values, segment):
    head_width = D // HEADS
    block_rows = min(512, SEQ)
    score_scale = 1.0 / math.sqrt(head_width)
    query_blocks = queries.reshape(SEQ // block_rows, block_rows, HEADS, head_width)
    segment_blocks = segment.reshape(SEQ // block_rows, block_rows)

    def one_block(block_pair):
        query_part, segment_part = block_pair
        raw_scores = low_back(jnp.einsum('qhd,khd->hqk', query_part, key_heads, precision=highest))
        same_scene = segment_part[:, None] == segment[None, :]
        scores = jnp.where(same_scene[None], raw_scores * score_scale, -1e+30)
        exp_scores = jnp.exp(scores - lax.optimization_barrier(jnp.max(scores, axis=-1, keepdims=True)))
        probabilities = exp_scores / lax.optimization_barrier(jnp.sum(exp_scores, axis=-1, keepdims=True))
        return jnp.einsum('hqk,khd->qhd', low(probabilities), values, precision=highest)
    block_out = lax.map(jax.checkpoint(one_block), (query_blocks, segment_blocks))
    return block_out.reshape(SEQ, D)

def one_layer(token_rows, segment, layer_weights):
    gain_one, shift_one, query_w, key_w, value_w, output_w, gain_two, shift_two, fc_in_w, fc_out_w = layer_weights
    head_width = D // HEADS
    normed = low(layer_norm(token_rows, gain_one, shift_one))

    def project(weight_matrix):
        return low_back(low(jnp.dot(normed, weight_matrix, precision=highest))).reshape(SEQ, HEADS, head_width)
    attended = low_back(low(scene_attention(project(query_w), project(key_w), project(value_w), segment)))
    mid_rows = token_rows + low_back(jnp.dot(attended, output_w, precision=highest))
    normed_two = low(layer_norm(mid_rows, gain_two, shift_two))
    pre_act = low_back(jnp.dot(normed_two, fc_in_w, precision=highest))
    hidden = low(jax.nn.gelu(pre_act, approximate=False))
    return mid_rows + low_back(jnp.dot(hidden, fc_out_w, precision=highest))

def reference(inputs, segment_ids, norm1_gain, norm1_shift, w_query, w_key, w_value, w_output, norm2_gain, norm2_shift, w_fc_in, w_fc_out, cotangent):
    params = (norm1_gain.astype(jnp.float32), norm1_shift.astype(jnp.float32), w_query.astype(jnp.float32), w_key.astype(jnp.float32), w_value.astype(jnp.float32), w_output.astype(jnp.float32), norm2_gain.astype(jnp.float32), norm2_shift.astype(jnp.float32), w_fc_in.astype(jnp.float32), w_fc_out.astype(jnp.float32))
    sequences = inputs.astype(jnp.float32).reshape(MB * SEQS, SEQ, D)
    scene_ids = segment_ids.reshape(MB * SEQS, SEQ)

    def forward(seq_rows, layer_params):

        def per_sequence(seq_pair):
            token_rows, segment = seq_pair
            for layer_index in range(LAYERS):
                token_rows = one_layer(token_rows, segment, tuple((parameter[layer_index] for parameter in layer_params)))
            return token_rows
        return lax.map(jax.checkpoint(per_sequence), (seq_rows, scene_ids))
    block_output, pull_back = jax.vjp(forward, sequences, params)
    input_grad, param_grads = pull_back(cotangent.astype(jnp.float32).reshape(MB * SEQS, SEQ, D))
    shape_full = (MB, SEQS, SEQ, D)
    return (block_output.reshape(shape_full), input_grad.reshape(shape_full), param_grads[0], param_grads[1], param_grads[2], param_grads[3], param_grads[4], param_grads[5], param_grads[6], param_grads[7], param_grads[8], param_grads[9])
```

```python
from functools import partial
import math

import jax
import jax.numpy as jnp
from jax import lax
from jax.experimental import pallas as pl
from jax.experimental.pallas import tpu as pltpu
from jax.sharding import PartitionSpec as P

D = 1024
HEADS = 16
float_type = jnp.float32
brain_type = jnp.bfloat16
CORE, XBIT, YBIT = 1, 2, 4
ZLOW, ZHIGH = 1, 2


def swap(block, axis_name, bit):
    size = lax.axis_size(axis_name)
    return lax.ppermute(block, axis_name, [(i, i ^ bit) for i in range(size)])


def after(block, earlier):
    return lax.optimization_barrier((block, earlier))[0]


def pick(flag, when_zero, when_one):
    return jnp.where(flag == 0, when_zero, when_one)


def tn_low(left, right):
    return tn(left, right).astype(brain_type)


def nt(left, right):
    return lax.dot_general(left, right, (((1,), (1,)), ((), ())), preferred_element_type=float_type)


def nn(left, right):
    return lax.dot_general(left, right, (((1,), (0,)), ((), ())), preferred_element_type=float_type)


def tn(left, right):
    return lax.dot_general(left, right, (((0,), (0,)), ((), ())), preferred_element_type=float_type)


def attend_kernel(score_scale, qkv_ref, seg_col_ref, seg_row_ref, out_ref):
    seq_len = qkv_ref.shape[0]
    rows = 256
    keys = qkv_ref[:, 128:256]
    values = qkv_ref[:, 256:384]
    low_lane = lax.broadcasted_iota(jnp.int32, (rows, 128), 1) < 64
    for part in range(seq_len // rows):
        span = slice(part * rows, (part + 1) * rows)
        query = qkv_ref[span, :128]
        same = seg_col_ref[span, :] == seg_row_ref[...]
        outs = []
        for head in range(2):
            mine = low_lane if head == 0 else jnp.logical_not(low_lane)
            masked = jnp.where(mine, query, jnp.zeros_like(query))
            scores = jnp.where(same, nt(masked, keys) * score_scale, -1e30)
            top = jnp.max(scores, axis=1, keepdims=True)
            weight = jnp.exp(scores - top)
            total = jnp.sum(weight, axis=1, keepdims=True)
            probs = (weight * (1.0 / total)).astype(brain_type)
            outs.append(nn(probs, values))
        out_ref[span, :] = jnp.where(low_lane, outs[0], outs[1]).astype(brain_type)


def attend(qkv, segment, score_scale):
    seq_len, width = qkv.shape
    blocks = width // 384
    return pl.pallas_call(
        partial(attend_kernel, score_scale),
        grid=(blocks,),
        in_specs=[
            pl.BlockSpec((seq_len, 384), lambda i: (0, i)),
            pl.BlockSpec((seq_len, 1), lambda i: (0, 0)),
            pl.BlockSpec((1, seq_len), lambda i: (0, 0)),
        ],
        out_specs=pl.BlockSpec((seq_len, 128), lambda i: (0, i)),
        out_shape=jax.ShapeDtypeStruct((seq_len, blocks * 128), brain_type),
        compiler_params=pltpu.CompilerParams(vmem_limit_bytes=48 * 1024 * 1024),
        cost_estimate=pl.CostEstimate(
            flops=blocks * 2 * 2 * 4 * seq_len * seq_len * 64 * 2,
            bytes_accessed=seq_len * width * 2,
            transcendentals=blocks * 2 * seq_len * seq_len,
        ),
        name="attend",
    )(qkv, segment[:, None], segment[None, :])


def attend_back_kernel(score_scale, qkv_ref, grad_ref, seg_col_ref, seg_row_ref, out_ref, gk_ref, gv_ref):
    seq_len = qkv_ref.shape[0]
    rows = 256
    keys = qkv_ref[:, 128:256]
    values = qkv_ref[:, 256:384]
    low_lane = lax.broadcasted_iota(jnp.int32, (rows, 128), 1) < 64
    for part in range(seq_len // rows):
        span = slice(part * rows, (part + 1) * rows)
        query = qkv_ref[span, :128]
        grad = grad_ref[span, :]
        same = seg_col_ref[...] == seg_row_ref[:, span]
        grad_queries = []
        for head in range(2):
            mine = low_lane if head == 0 else jnp.logical_not(low_lane)
            masked = jnp.where(mine, query, jnp.zeros_like(query))
            grad_masked = jnp.where(mine, grad, jnp.zeros_like(grad))
            scores = jnp.where(same, nt(keys, masked) * score_scale, -1e30)
            top = jnp.max(scores, axis=0, keepdims=True)
            weight = jnp.exp(scores - top)
            total = jnp.sum(weight, axis=0, keepdims=True)
            probs = weight * (1.0 / total)
            grad_probs = nt(values, grad_masked)
            inner = jnp.sum(probs * grad_probs, axis=0, keepdims=True)
            grad_raw = (probs * (grad_probs - inner) * score_scale).astype(brain_type)
            gv_part = nn(probs.astype(brain_type), grad_masked)
            gk_part = nn(grad_raw, masked)
            if part == 0 and head == 0:
                gv_ref[...] = gv_part
                gk_ref[...] = gk_part
            else:
                gv_ref[...] += gv_part
                gk_ref[...] += gk_part
            grad_queries.append(tn(grad_raw, keys))
        out_ref[span, :128] = jnp.where(low_lane, grad_queries[0], grad_queries[1]).astype(brain_type)
    out_ref[:, 128:256] = gk_ref[...].astype(brain_type)
    out_ref[:, 256:384] = gv_ref[...].astype(brain_type)


def attend_back(qkv, grad, segment, score_scale):
    seq_len, width = qkv.shape
    blocks = width // 384
    return pl.pallas_call(
        partial(attend_back_kernel, score_scale),
        grid=(blocks,),
        in_specs=[
            pl.BlockSpec((seq_len, 384), lambda i: (0, i)),
            pl.BlockSpec((seq_len, 128), lambda i: (0, i)),
            pl.BlockSpec((seq_len, 1), lambda i: (0, 0)),
            pl.BlockSpec((1, seq_len), lambda i: (0, 0)),
        ],
        out_specs=pl.BlockSpec((seq_len, 384), lambda i: (0, i)),
        out_shape=jax.ShapeDtypeStruct((seq_len, width), brain_type),
        scratch_shapes=[
            pltpu.VMEM((seq_len, 128), float_type),
            pltpu.VMEM((seq_len, 128), float_type),
        ],
        compiler_params=pltpu.CompilerParams(vmem_limit_bytes=48 * 1024 * 1024),
        cost_estimate=pl.CostEstimate(
            flops=blocks * 2 * 5 * 4 * seq_len * seq_len * 64 * 2,
            bytes_accessed=seq_len * width * 5,
            transcendentals=blocks * 2 * seq_len * seq_len,
        ),
        name="attend_back",
    )(qkv, grad, segment[:, None], segment[None, :])


def center_of(rows):
    center = rows - jnp.mean(rows, axis=-1, keepdims=True)
    scale = lax.rsqrt(jnp.mean(center * center, axis=-1, keepdims=True) + 1e-05)
    return center * scale, scale


def normed(rows, gain, shift):
    return (center_of(rows)[0] * gain + shift).astype(brain_type)


def normed_back(rows, gain, grad):
    unit, scale = center_of(rows)
    grad_unit = grad * gain
    below = scale * (
        grad_unit
        - jnp.mean(grad_unit, axis=-1, keepdims=True)
        - unit * jnp.mean(grad_unit * unit, axis=-1, keepdims=True)
    )
    return below, jnp.sum(grad * unit, axis=0), jnp.sum(grad, axis=0)


def gelu_pair(pre):
    cdf = 0.5 * (1.0 + lax.erf(pre * math.sqrt(0.5)))
    density = jnp.exp(-0.5 * pre * pre) * (1.0 / math.sqrt(2.0 * math.pi))
    return (pre * cdf).astype(brain_type), (cdf + pre * density).astype(brain_type)


class Mover:
    def __init__(self, send_sems, recv_sems, local_sems):
        self.send_sems, self.recv_sems, self.local_sems = send_sems, recv_sems, local_sems
        self.remote, self.local = 0, 0
        self.place = lax.axis_index("dp")
        self.height = lax.axis_index("tensor")
        self.core = lax.rem(self.place, 2)
        self.x_bit = lax.rem(self.place // 2, 2)
        self.y_bit = lax.rem(self.place // 4, 2)
        self.z_low = lax.rem(self.height, 2)
        self.z_high = self.height // 2
        self.sibling = {"dp": self.place + 1 - 2 * self.core}
        self.x_side = {"dp": self.place + 2 - 4 * self.x_bit}
        self.y_side = {"dp": self.place + 4 - 8 * self.y_bit}
        self.z_near = {"tensor": self.height + 1 - 2 * self.z_low}
        self.z_far = {"tensor": self.height + 2 - 4 * self.z_high}

    def make(self, source, target, device, send_index, recv_index):
        return pltpu.make_async_remote_copy(
            src_ref=source,
            dst_ref=target,
            send_sem=self.send_sems.at[send_index],
            recv_sem=self.recv_sems.at[recv_index],
            device_id=device,
            device_id_type=pl.DeviceIdType.MESH,
        )

    def send(self, source, target, device):
        copy = self.make(source, target, device, self.remote, self.remote)
        self.remote += 1
        copy.start()
        return copy

    def keep(self, source, target):
        copy = pltpu.make_async_copy(source, target, self.local_sems.at[self.local])
        self.local += 1
        copy.start()
        return copy

    def greet(self):
        barrier = pltpu.get_barrier_semaphore()
        plane = self.place - self.core
        devices = [self.x_side, self.y_side]
        for step in range(1, 8):
            other = lax.rem(self.core * 4 + self.height + step, 8)
            devices.append({"dp": plane + other // 4, "tensor": lax.rem(other, 4)})
        for device in devices:
            pl.semaphore_signal(
                barrier, inc=1, device_id=device, device_id_type=pl.DeviceIdType.MESH
            )
        pl.semaphore_wait(barrier, len(devices))

    def column(self, y, x, half):
        y_off = lax.rem(y + self.y_bit, 2)
        x_off = lax.rem(x + self.x_bit, 2)
        spot = 2 * y_off + x_off if half == 0 else y_off + 2 * x_off
        return pl.multiple_of((half * 4 + spot) * 128, 128)


BLOCKS = [(y, x, half) for y in range(2) for x in range(2) for half in range(2)]


def move_tokens(move, ways, origins):
    base, local = move.remote, move.local
    move.remote += 2
    move.local += 2
    closing = []
    for i, (to_core, to_z, copies, whole, slot) in enumerate(ways):
        stays = jnp.logical_and(to_core == move.core, to_z == move.height)
        device = {"dp": move.place - move.core + to_core, "tensor": to_z}

        @pl.when(stays)
        def _():
            for source, target in copies:
                pltpu.make_async_copy(source, target, move.local_sems.at[local + i]).start()

        @pl.when(jnp.logical_not(stays))
        def _():
            for source, target in copies:
                move.make(source, target, device, base + i, base + slot).start()

        closing.append((stays, device, whole, i))

    def finish():
        for stays, device, (source, target), i in closing:
            @pl.when(stays)
            def _():
                pltpu.make_async_copy(source, target, move.local_sems.at[local + i]).wait()

            @pl.when(jnp.logical_not(stays))
            def _():
                move.make(source, target, device, base + i, base + i).wait_send()

        for slot, (from_core, from_z, (source, target)) in enumerate(origins):
            comes = jnp.logical_not(
                jnp.logical_and(from_core == move.core, from_z == move.height)
            )

            @pl.when(comes)
            def _():
                move.make(source, target, move.sibling, base + slot, base + slot).wait_recv()

    return finish


def fetch_tokens(move, source, target):
    rows = source.shape[1]
    here = pl.ds(pl.multiple_of(move.z_low * rows, rows), rows)
    ways, origins = [], []
    for micro in range(2):
        copies = [
            (
                source.at[micro, :, pl.ds(i * 128, 128)],
                target.at[here, pl.ds(move.column(*block), 128)],
            )
            for i, block in enumerate(BLOCKS)
        ]
        whole = (source.at[micro], target.at[here])
        ways.append((move.z_high, 2 * micro + move.core, copies, whole, move.z_low))
    for slot in range(2):
        whole = (source.at[slot], target.at[pl.ds(slot * rows, rows)])
        origins.append((move.z_low, 2 * move.core + slot, whole))
    return move_tokens(move, ways, origins)


def return_tokens(move, source, target):
    rows = target.shape[1]
    ways, origins = [], []
    for slot in range(2):
        copies = [
            (
                source.at[pl.ds(slot * rows, rows), pl.ds(move.column(*block), 128)],
                target.at[move.z_high, :, pl.ds(i * 128, 128)],
            )
            for i, block in enumerate(BLOCKS)
        ]
        whole = (source.at[pl.ds(slot * rows, rows)], target.at[move.z_high])
        ways.append((move.z_low, 2 * move.core + slot, copies, whole, move.z_high))
    for micro in range(2):
        whole = (source.at[pl.ds(micro * rows, rows)], target.at[micro])
        origins.append((move.z_high, 2 * micro + move.core, whole))
    return move_tokens(move, ways, origins)


def spread_stages(move, mine, other, whole, start=None):
    rows, units = mine.shape
    half = whole.shape[0] // 2
    own = pl.ds(pl.multiple_of(move.core * half, half), rows)

    def part(first, spot, lane, lanes):
        return whole.at[pl.ds(first * half + spot * rows, rows), pl.ds(lane * units, lanes * units)]

    copies = [
        move.send(other, whole.at[own, pl.ds(0, units)], move.sibling),
        move.keep(mine, whole.at[own, pl.ds(0, units)]),
    ]
    done = []

    def go(first, spot, lane, lanes, to_spot, to_lane, device):
        copy = move.send(part(first, spot, lane, lanes), part(first, to_spot, to_lane, lanes), device)
        done.append(copy)
        return copy

    def plane(lane, lanes):
        one = go(0, 0, lane, lanes, 1, lane, move.x_side)
        two = go(1, 0, lane, lanes, 1, lane, move.y_side)
        last = [
            go(0, 0, lane, lanes, 2, lane, move.y_side),
            go(1, 0, lane, lanes, 2, lane, move.x_side),
        ]
        return one, two, last, lane, lanes

    def relay(one, two, last, lane, lanes):
        one.wait_recv()
        last.append(go(0, 1, lane, lanes, 3, lane, move.y_side))
        two.wait_recv()
        last.append(go(1, 1, lane, lanes, 3, lane, move.x_side))
        return last

    yield
    copies[0].wait_send()
    copies[0].wait_recv()
    copies[1].wait()
    near = [go(first, 0, 0, 1, 0, 1, move.z_near) for first in range(2)]
    far = [go(first, 0, 0, 1, 0, 2, move.z_far) for first in range(2)]
    planes = [plane(0, 1)]
    yield
    for copy in near:
        copy.wait_recv()
    far += [go(first, 0, 1, 1, 0, 3, move.z_far) for first in range(2)]
    planes.append(plane(1, 1))
    yield
    lasts = relay(*planes[0])
    for copy in far:
        copy.wait_recv()
    planes.append(plane(2, 2))
    yield
    lasts += relay(*planes[1])
    yield
    lasts += relay(*planes[2])
    yield
    for copy in lasts:
        copy.wait_recv()
    for copy in done:
        copy.wait_send()


SPREAD_STEPS = 6


def vector_stages(move, vectors, out):
    own = move.core * 4
    keep = move.keep(vectors, out.at[own])
    copy = move.send(vectors, out.at[own], move.sibling)
    yield
    keep.wait()
    copy.wait()
    over_x = [move.send(out.at[i], out.at[j], move.x_side) for i, j in ((0, 1), (4, 6))]
    yield
    for copy in over_x:
        copy.wait()
    over_y = [
        move.send(out.at[i], out.at[j], move.y_side) for i, j in ((0, 2), (1, 3), (4, 5), (6, 7))
    ]
    yield
    for copy in over_y:
        copy.wait()


def spread_kernel(groups, *refs):
    count = 2 * groups
    inputs, cotangent, vectors, ids = refs[:4]
    pieces = refs[4 : 4 + count]
    rows_out, grad_out, vectors_out, ids_out = refs[4 + count : 8 + count]
    wholes = refs[8 + count : 8 + count + groups]
    move = Mover(*refs[8 + count + groups :])
    move.greet()
    tasks = [
        spread_stages(move, pieces[2 * i], pieces[2 * i + 1], wholes[i]) for i in range(groups)
    ]
    for task in tasks:
        next(task)
    finish_rows = fetch_tokens(move, inputs, rows_out)
    small = vector_stages(move, vectors, vectors_out)
    next(small)
    ids_copy = move.send(ids, ids_out, move.sibling)
    finish_grad = None
    for tick in range(groups + SPREAD_STEPS - 1):
        for i in range(groups - 1, -1, -1):
            if 0 <= tick - i < SPREAD_STEPS:
                next(tasks[i], None)
        next(small, None)
        if tick == 2:
            finish_grad = fetch_tokens(move, cotangent, grad_out)
    ids_copy.wait()
    finish_rows()
    finish_grad()


def hbm(count):
    return [pl.BlockSpec(memory_space=pl.ANY)] * count


def spread_all(inputs, cotangent, vectors, ids, pieces):
    groups = len(pieces)
    tokens = 2 * inputs.shape[1]
    width = inputs.shape[2]
    flat = [block for piece in pieces for block in piece]
    remote = 27 * groups + 16
    outs = pl.pallas_call(
        partial(spread_kernel, groups),
        out_shape=[
            jax.ShapeDtypeStruct((tokens, width), inputs.dtype),
            jax.ShapeDtypeStruct((tokens, width), inputs.dtype),
            jax.ShapeDtypeStruct((8, *vectors.shape), vectors.dtype),
            jax.ShapeDtypeStruct(ids.shape, ids.dtype),
        ]
        + [jax.ShapeDtypeStruct((8 * p.shape[0], 4 * p.shape[1]), p.dtype) for p, _ in pieces],
        in_specs=hbm(4 + 2 * groups),
        out_specs=hbm(4 + groups),
        scratch_shapes=[
            pltpu.SemaphoreType.DMA((remote,)),
            pltpu.SemaphoreType.DMA((remote,)),
            pltpu.SemaphoreType.DMA((groups + 5,)),
        ],
        compiler_params=pltpu.CompilerParams(collective_id=0, has_side_effects=True),
        name="spread",
    )(inputs, cotangent, vectors, ids, *flat)
    return outs[0], outs[1], outs[2], outs[3], outs[4:]


def collect_stages(move, grads, out, loaded, first_got, second_got, far_got, near_got):
    quarter = grads.shape[0] // 4
    rows, units = quarter // 2, grads.shape[1] // 4
    sides = ((move.y_side, move.x_side), (move.x_side, move.y_side))
    done = []

    def go(source, target, device):
        copy = move.send(source, target, device)
        done.append(copy)
        return copy

    def total(target, source, height, width):
        step = 32

        def body(i, carry):
            span = (pl.ds(pl.multiple_of(i * step, step), step), pl.ds(0, width))
            target[span] = (
                target[span].astype(float_type) + source[span].astype(float_type)
            ).astype(brain_type)
            return carry

        lax.fori_loop(0, height // step, body, 0)

    first = [
        go(grads.at[pl.ds((2 * i + 1) * quarter, quarter)], first_got.at[i], sides[i][0])
        for i in range(2)
    ]
    loads = [
        move.keep(grads.at[pl.ds(2 * i * quarter, quarter)], loaded.at[i]) for i in range(2)
    ]
    yield
    second = []
    for i in range(2):
        loads[i].wait()
        first[i].wait_recv()
        total(loaded.at[i], first_got.at[i], quarter, 4 * units)
        second.append(go(loaded.at[i, pl.ds(rows, rows)], second_got.at[i], sides[i][1]))
    yield
    far = []
    for i in range(2):
        second[i].wait_recv()
        total(loaded.at[i], second_got.at[i], rows, 4 * units)
        far.append(
            go(loaded.at[i, pl.ds(0, rows), pl.ds(2 * units, 2 * units)], far_got.at[i], move.z_far)
        )
    yield
    near = []
    for i in range(2):
        far[i].wait_recv()
        total(loaded.at[i], far_got.at[i], rows, 2 * units)
        near.append(
            go(loaded.at[i, pl.ds(0, rows), pl.ds(units, units)], near_got.at[i], move.z_near)
        )
    yield
    for i in range(2):
        near[i].wait_recv()
        total(loaded.at[i], near_got.at[i], rows, units)
    ready = pl.ds(0, rows), pl.ds(0, units)
    last = go(loaded.at[(1 - move.core, *ready)], out.at[1], move.sibling)
    stay = move.keep(loaded.at[(move.core, *ready)], out.at[0])
    yield
    last.wait_recv()
    stay.wait()
    for copy in done:
        copy.wait_send()


COLLECT_STEPS = 6


def vector_sum_stages(move, vectors, out, sums, by_core, by_y, by_x, by_near, by_far):
    keep = move.keep(vectors.at[move.core], sums)
    copy = move.send(vectors.at[1 - move.core], by_core, move.sibling)
    yield
    keep.wait()
    copy.wait()
    sums[...] += by_core[...]
    copy = move.send(sums.at[pl.ds(2, 2)], by_y, move.y_side)
    yield
    copy.wait()
    sums[:2] += by_y[...]
    copy = move.send(sums.at[1], by_x, move.x_side)
    yield
    copy.wait()
    sums[0] += by_x[...]
    copy = move.send(sums.at[0], by_near, move.z_near)
    yield
    copy.wait()
    sums[1] = sums[0] + by_near[...]
    copy = move.send(sums.at[1], by_far, move.z_far)
    yield
    copy.wait()
    out[...] = sums[1] + by_far[...]


def collect_kernel(groups, *refs):
    above, below, vectors = refs[:3]
    grads = refs[3 : 3 + groups]
    above_out, below_out, vectors_out = refs[3 + groups : 6 + groups]
    outs = refs[6 + groups : 6 + 2 * groups]
    buffers = refs[6 + 2 * groups : 6 + 7 * groups]
    small_buffers = refs[6 + 7 * groups : 12 + 7 * groups]
    move = Mover(*refs[12 + 7 * groups :])
    move.greet()
    tasks = [
        collect_stages(move, grads[i], outs[i], *buffers[5 * i : 5 * i + 5]) for i in range(groups)
    ]
    for task in tasks:
        next(task)
    finish_above = return_tokens(move, above, above_out)
    finish_below = return_tokens(move, below, below_out)
    small = vector_sum_stages(move, vectors, vectors_out, *small_buffers)
    next(small)
    for tick in range(groups + COLLECT_STEPS - 1):
        for i in range(groups):
            if 0 <= tick - i < COLLECT_STEPS:
                next(tasks[i], None)
        next(small, None)
    finish_above()
    finish_below()


def collect_all(tokens, vectors, grads):
    groups = len(grads)
    width = tokens[0].shape[1]
    buffers = []
    for grad in grads:
        rows, units = grad.shape[0] // 8, grad.shape[1] // 4
        for height, lanes in ((2 * rows, 4), (2 * rows, 4), (rows, 4), (rows, 2), (rows, 1)):
            buffers.append(pltpu.VMEM((2, height, lanes * units), grad.dtype))
    for shape in ((4, 8, 128), (4, 8, 128), (2, 8, 128), (8, 128), (8, 128), (8, 128)):
        buffers.append(pltpu.VMEM(shape, vectors.dtype))
    remote = 9 * groups + 9
    outs = pl.pallas_call(
        partial(collect_kernel, groups),
        out_shape=[
            jax.ShapeDtypeStruct((2, tokens[0].shape[0] // 2, width), tokens[0].dtype)
            for _ in tokens
        ]
        + [
            jax.ShapeDtypeStruct(vectors.shape[2:], vectors.dtype),
        ]
        + [
            jax.ShapeDtypeStruct((2, g.shape[0] // 8, g.shape[1] // 4), g.dtype) for g in grads
        ],
        in_specs=hbm(3 + groups),
        out_specs=hbm(2) + [pl.BlockSpec(memory_space=pltpu.VMEM)] + hbm(groups),
        scratch_shapes=buffers
        + [
            pltpu.SemaphoreType.DMA((remote,)),
            pltpu.SemaphoreType.DMA((remote,)),
            pltpu.SemaphoreType.DMA((3 * groups + 5,)),
        ],
        compiler_params=pltpu.CompilerParams(
            collective_id=1, has_side_effects=True, vmem_limit_bytes=60 * 1024 * 1024
        ),
        name="collect",
    )(*tokens, vectors, *grads)
    return outs[:2], outs[2], outs[3:]


def per_chip(
    inputs,
    segment_ids,
    norm1_gain,
    norm1_shift,
    w_query,
    w_key,
    w_value,
    w_output,
    norm2_gain,
    norm2_shift,
    w_fc_in,
    w_fc_out,
    cotangent,
):
    layers = norm1_gain.shape[0]
    head_width = inputs.shape[3] // HEADS
    score_scale = 1.0 / math.sqrt(head_width)
    place = lax.axis_index("dp")
    height = lax.axis_index("tensor")
    core, x_bit, y_bit = place & 1, (place >> 1) & 1, (place >> 2) & 1
    z_low, z_high = height & 1, (height >> 1) & 1

    def halves(columns):
        wide = columns.shape[1] // 2
        low, high = columns[:, :wide], columns[:, wide:]
        return pick(core, low, high), pick(core, high, low)

    pieces = []
    for layer in range(layers):
        both = [halves(w[layer]) for w in (w_query, w_key, w_value)]
        pieces += [
            tuple(jnp.concatenate([b[side] for b in both], axis=1) for side in range(2)),
            halves(w_output[layer].T),
            halves(w_fc_in[layer]),
            halves(w_fc_out[layer].T),
        ]
    vectors = jnp.concatenate([norm1_gain, norm1_shift, norm2_gain, norm2_shift], axis=0)
    rows, grad, vectors, other_ids, weights = spread_all(
        inputs[:, 0], cotangent[:, 0], vectors.astype(float_type), segment_ids, pieces
    )
    rows, grad = rows.astype(float_type), grad.astype(float_type)
    vectors = vectors.transpose(1, 0, 2).reshape(4 * layers, -1)

    ids = pick(z_low ^ core, segment_ids, other_ids)
    ids = pick(z_high, ids[0, 0], ids[1, 0])
    half_len = ids.shape[0] // 2
    ids = pick(core, ids, jnp.concatenate([ids[half_len:], ids[:half_len]]))

    def whole_tokens(half):
        return jnp.concatenate([half, swap(half, "dp", CORE)], axis=0)

    def summed(product, left):
        rows_here = left.shape[0] // 2
        got = swap(product(left[rows_here:]).astype(brain_type), "dp", CORE)
        return product(left[:rows_here]) + got.astype(float_type)

    saved = []
    for layer in range(layers):
        qkv_w, output_w, fc_in_w, fc_out_w = weights[4 * layer : 4 * layer + 4]
        gain_one, shift_one, gain_two, shift_two = (vectors[i * layers + layer] for i in range(4))
        normed_one = whole_tokens(normed(rows, gain_one, shift_one))
        qkv = nn(normed_one, qkv_w).astype(brain_type)
        attended = attend(qkv, ids, score_scale)
        mid = rows + summed(lambda left: nt(left, output_w), attended)
        normed_two = whole_tokens(normed(mid, gain_two, shift_two))
        hidden, slope = gelu_pair(nn(normed_two, fc_in_w))
        above = mid + summed(lambda left: nt(left, fc_out_w), hidden)
        saved.append((rows, normed_one, qkv, attended, mid, normed_two, hidden, slope))
        rows = above
    block_output = rows

    totals = [None] * (4 * layers)
    vector_grads = [None] * (4 * layers)
    for layer in reversed(range(layers)):
        rows, normed_one, qkv, attended, mid, normed_two, hidden, slope = saved[layer]
        qkv_w, output_w, fc_in_w, fc_out_w = weights[4 * layer : 4 * layer + 4]
        gain_one, shift_one, gain_two, shift_two = (vectors[i * layers + layer] for i in range(4))
        branch = whole_tokens(grad.astype(brain_type))
        totals[4 * layer + 3] = tn_low(branch, hidden)
        grad_pre = (nn(branch, fc_out_w) * slope.astype(float_type)).astype(brain_type)
        totals[4 * layer + 2] = tn_low(normed_two, grad_pre)
        grad_normed = summed(lambda left: nt(left, fc_in_w), grad_pre)
        below, vector_grads[2 * layers + layer], vector_grads[3 * layers + layer] = normed_back(
            mid, gain_two, grad_normed
        )
        grad = grad + below
        branch = whole_tokens(grad.astype(brain_type))
        totals[4 * layer + 1] = tn_low(branch, attended)
        grad_attended = nn(branch, output_w).astype(brain_type)
        grad_qkv = attend_back(qkv, grad_attended, ids, score_scale)
        totals[4 * layer] = tn_low(normed_one, grad_qkv)
        grad_normed = summed(lambda left: nt(left, qkv_w), grad_qkv)
        below, vector_grads[layer], vector_grads[layers + layer] = normed_back(
            rows, gain_one, grad_normed
        )
        grad = grad + below
    vector_grads = jnp.stack(vector_grads).reshape(4 * layers, 2, 4, -1)
    second = vector_grads[:, 1]
    second = jnp.stack([second[:, i] for i in (0, 2, 1, 3)], axis=1)
    vector_grads = jnp.stack([vector_grads[:, 0], second])
    order = [4 * layer + kind for layer in reversed(range(layers)) for kind in (3, 2, 1, 0)]
    block_output, vector_grads, outs = collect_all(
        (block_output.astype(brain_type), grad.astype(brain_type)),
        vector_grads.transpose(0, 2, 1, 3),
        [totals[i] for i in order],
    )
    outs = [(pick(core, out[0], out[1]), pick(core, out[1], out[0])) for out in outs]
    outs = [outs[order.index(i)] for i in range(4 * layers)]
    block_output, input_grad = (tokens.astype(float_type) for tokens in block_output)

    def joined(kind, columns=None):
        per_layer = []
        for layer in range(layers):
            low, high = outs[4 * layer + kind]
            if columns is not None:
                low, high = low[:, columns], high[:, columns]
            per_layer.append(jnp.concatenate([low, high], axis=1))
        return jnp.stack(per_layer)

    width = w_query.shape[2] // 2
    grad_query, grad_key, grad_value = (joined(0, slice(i * width, (i + 1) * width)) for i in range(3))
    grad_output = joined(1).transpose(0, 2, 1)
    grad_fc_in = joined(2)
    grad_fc_out = joined(3).transpose(0, 2, 1)

    gain_one, shift_one, gain_two, shift_two = (
        vector_grads[i * layers : (i + 1) * layers] for i in range(4)
    )
    return (
        block_output[:, None],
        input_grad[:, None],
        gain_one,
        shift_one,
        grad_query.astype(float_type),
        grad_key.astype(float_type),
        grad_value.astype(float_type),
        grad_output.astype(float_type),
        gain_two,
        shift_two,
        grad_fc_in.astype(float_type),
        grad_fc_out.astype(float_type),
    )


def layer_norm(token_rows, gain_vec, shift_vec):
    center = token_rows - jnp.mean(token_rows, axis=-1, keepdims=True)
    spread = jnp.mean(center * center, axis=-1, keepdims=True)
    return center * lax.rsqrt(spread + 1e-05) * gain_vec + shift_vec


def normed_local(token_rows, gain_vec, shift_vec):
    return layer_norm(token_rows, gain_vec.astype(float_type), shift_vec.astype(float_type)).astype(
        brain_type
    )


def normed_send(token_rows, gain_vec, shift_vec):
    return lax.all_gather(
        normed_local(token_rows, gain_vec, shift_vec), "tensor", axis=0, tiled=True
    )


def normed_resend(token_rows, gain_vec, shift_vec):
    return lax.all_gather(
        normed_local(token_rows, gain_vec, shift_vec), "tensor", axis=0, tiled=True
    )


def branch_total(partial_sum):
    return lax.psum_scatter(
        partial_sum.astype(jnp.bfloat16), "tensor", scatter_dimension=0, tiled=True
    ).astype(jnp.float32)


def branch_cotangent(grad_rows):
    return lax.all_gather(grad_rows.astype(brain_type), "tensor", axis=0, tiled=True)


def input_total(partial_sum):
    return lax.psum_scatter(
        partial_sum.astype(jnp.bfloat16), "tensor", scatter_dimension=0, tiled=True
    ).astype(jnp.float32)


def norm_backward(token_rows, gain_vec, shift_vec, grad_normed):
    _, norm_pull = jax.vjp(
        layer_norm, token_rows, gain_vec.astype(float_type), shift_vec.astype(float_type)
    )
    return norm_pull(grad_normed)


def masked_scores(query_part, segment_part, key_heads, segment, score_scale):
    raw_scores = jnp.einsum(
        "qhd,khd->hqk", query_part, key_heads, preferred_element_type=float_type
    )
    same_scene = segment_part[:, None] == segment[None, :]
    return jnp.where(same_scene[None], raw_scores * score_scale, -1e30)


def attend_forward(queries, key_heads, values, segment, block_rows):
    seq_len, head_count, head_width = queries.shape
    score_scale = 1.0 / math.sqrt(head_width)
    block_count = seq_len // block_rows

    def one_block(block_pair):
        query_part, segment_part = block_pair
        scores = masked_scores(query_part, segment_part, key_heads, segment, score_scale)
        row_max = jnp.max(scores, axis=-1, keepdims=True)
        exp_scores = jnp.exp(scores - row_max)
        row_total = jnp.sum(exp_scores, axis=-1, keepdims=True)
        probabilities = (exp_scores / row_total).astype(brain_type)
        block_out = jnp.einsum(
            "hqk,khd->qhd", probabilities, values, preferred_element_type=float_type
        )
        log_total = (row_max + jnp.log(row_total))[..., 0]
        return (block_out.astype(brain_type), log_total)

    query_blocks = queries.reshape(block_count, block_rows, head_count, head_width)
    segment_blocks = segment.reshape(block_count, block_rows)
    outputs, log_totals = lax.map(one_block, (query_blocks, segment_blocks))
    return (outputs.reshape(seq_len, head_count * head_width), log_totals)


def attend_backward(queries, key_heads, values, segment, log_totals, grad_out, block_rows):
    seq_len, head_count, head_width = queries.shape
    score_scale = 1.0 / math.sqrt(head_width)
    block_count = seq_len // block_rows

    def one_block(carry_pair, block_items):
        grad_keys, grad_values = carry_pair
        query_part, segment_part, log_part, grad_part = block_items
        scores = masked_scores(query_part, segment_part, key_heads, segment, score_scale)
        probabilities = jnp.exp(scores - log_part[..., None])
        grad_probs = jnp.einsum(
            "qhd,khd->hqk", grad_part, values, preferred_element_type=float_type
        )
        row_inner = jnp.sum(probabilities * grad_probs, axis=-1, keepdims=True)
        grad_raw = (probabilities * (grad_probs - row_inner) * score_scale).astype(brain_type)
        grad_query = jnp.einsum(
            "hqk,khd->qhd", grad_raw, key_heads, preferred_element_type=float_type
        )
        grad_keys = grad_keys + jnp.einsum(
            "hqk,qhd->khd", grad_raw, query_part, preferred_element_type=float_type
        )
        grad_values = grad_values + jnp.einsum(
            "hqk,qhd->khd",
            probabilities.astype(brain_type),
            grad_part,
            preferred_element_type=float_type,
        )
        return ((grad_keys, grad_values), grad_query.astype(brain_type))

    zero_heads = jnp.zeros((seq_len, head_count, head_width), float_type)
    block_items = (
        queries.reshape(block_count, block_rows, head_count, head_width),
        segment.reshape(block_count, block_rows),
        log_totals,
        grad_out.reshape(block_count, block_rows, head_count, head_width),
    )
    (grad_keys, grad_values), grad_queries = lax.scan(
        one_block, (zero_heads, zero_heads), block_items
    )
    flat_shape = (seq_len, head_count * head_width)
    return (
        grad_queries.reshape(flat_shape),
        grad_keys.astype(brain_type).reshape(flat_shape),
        grad_values.astype(brain_type).reshape(flat_shape),
    )


def fresh_totals(layers, attn_width, hidden_width):
    vector_zero = jnp.zeros((layers, D), float_type)
    column_zero = jnp.zeros((layers, D, attn_width), float_type)
    return [
        vector_zero,
        vector_zero,
        column_zero,
        column_zero,
        column_zero,
        jnp.zeros((layers, attn_width, D), float_type),
        vector_zero,
        vector_zero,
        jnp.zeros((layers, D, hidden_width), float_type),
        jnp.zeros((layers, hidden_width, D), float_type),
    ]


def add_into(grad_totals, position, layer_index, term):
    grad_totals[position] = grad_totals[position].at[layer_index].add(term)


def per_device(
    inputs,
    segment_ids,
    norm1_gain,
    norm1_shift,
    w_query,
    w_key,
    w_value,
    w_output,
    norm2_gain,
    norm2_shift,
    w_fc_in,
    w_fc_out,
    cotangent,
):
    micro_count = inputs.shape[0]
    layers = norm1_gain.shape[0]
    seq_len = segment_ids.shape[2]
    block_rows = min(512, seq_len)
    head_width = D // HEADS
    attn_width = w_query.shape[2]
    hidden_width = w_fc_in.shape[2]
    grad_totals = fresh_totals(layers, attn_width, hidden_width)
    reduced = None
    output_list = []
    input_grad_list = []
    for micro_index in range(micro_count):
        token_rows = inputs[micro_index, 0].astype(float_type)
        segment = segment_ids[micro_index, 0]
        saved_state = []
        for layer_index in range(layers):
            weights = (
                lax.all_gather(norm1_gain[layer_index], "dp", axis=0, tiled=True),
                lax.all_gather(norm1_shift[layer_index], "dp", axis=0, tiled=True),
                lax.all_gather(w_query[layer_index], "dp", axis=0, tiled=True),
                lax.all_gather(w_key[layer_index], "dp", axis=0, tiled=True),
                lax.all_gather(w_value[layer_index], "dp", axis=0, tiled=True),
                lax.all_gather(w_output[layer_index], "dp", axis=1, tiled=True),
                lax.all_gather(norm2_gain[layer_index], "dp", axis=0, tiled=True),
                lax.all_gather(norm2_shift[layer_index], "dp", axis=0, tiled=True),
                lax.all_gather(w_fc_in[layer_index], "dp", axis=0, tiled=True),
                lax.all_gather(w_fc_out[layer_index], "dp", axis=1, tiled=True),
            )
            (
                gain_one,
                shift_one,
                query_w,
                key_w,
                value_w,
                output_w,
                gain_two,
                shift_two,
                fc_in_w,
                fc_out_w,
            ) = weights
            whole_weights = None
            normed = normed_send(token_rows, gain_one, shift_one)
            queries = jnp.dot(normed, query_w, preferred_element_type=float_type).astype(brain_type)
            key_heads = jnp.dot(normed, key_w, preferred_element_type=float_type).astype(brain_type)
            values = jnp.dot(normed, value_w, preferred_element_type=float_type).astype(brain_type)
            attended, log_totals = attend_forward(
                queries.reshape(seq_len, -1, head_width),
                key_heads.reshape(seq_len, -1, head_width),
                values.reshape(seq_len, -1, head_width),
                segment,
                block_rows,
            )
            mid_rows = token_rows + branch_total(
                jnp.dot(attended, output_w, preferred_element_type=float_type)
            )
            normed_two = normed_send(mid_rows, gain_two, shift_two)
            pre_act = jnp.dot(normed_two, fc_in_w, preferred_element_type=float_type)
            hidden = jax.nn.gelu(pre_act, approximate=False).astype(brain_type)
            next_rows = mid_rows + branch_total(
                jnp.dot(hidden, fc_out_w, preferred_element_type=float_type)
            )
            saved_state.append(
                (
                    token_rows,
                    mid_rows,
                    weights,
                    normed,
                    normed_two,
                    queries,
                    key_heads,
                    values,
                    attended,
                    log_totals,
                    pre_act,
                    hidden,
                    whole_weights,
                )
            )
            token_rows = next_rows
        output_list.append(token_rows)
        grad_rows = cotangent[micro_index, 0].astype(float_type)
        for layer_index in reversed(range(layers)):
            (
                layer_rows,
                mid_rows,
                weights,
                normed,
                normed_two,
                queries,
                key_heads,
                values,
                attended,
                log_totals,
                pre_act,
                hidden,
                whole_weights,
            ) = saved_state[layer_index]
            weights = (
                lax.all_gather(norm1_gain[layer_index], "dp", axis=0, tiled=True),
                lax.all_gather(norm1_shift[layer_index], "dp", axis=0, tiled=True),
                lax.all_gather(w_query[layer_index], "dp", axis=0, tiled=True),
                lax.all_gather(w_key[layer_index], "dp", axis=0, tiled=True),
                lax.all_gather(w_value[layer_index], "dp", axis=0, tiled=True),
                lax.all_gather(w_output[layer_index], "dp", axis=1, tiled=True),
                lax.all_gather(norm2_gain[layer_index], "dp", axis=0, tiled=True),
                lax.all_gather(norm2_shift[layer_index], "dp", axis=0, tiled=True),
                lax.all_gather(w_fc_in[layer_index], "dp", axis=0, tiled=True),
                lax.all_gather(w_fc_out[layer_index], "dp", axis=1, tiled=True),
            )
            (
                gain_one,
                shift_one,
                query_w,
                key_w,
                value_w,
                output_w,
                gain_two,
                shift_two,
                fc_in_w,
                fc_out_w,
            ) = weights
            normed = normed_resend(layer_rows, gain_one, shift_one)
            normed_two = normed_resend(mid_rows, gain_two, shift_two)
            grad_branch = branch_cotangent(grad_rows)
            add_into(
                grad_totals,
                9,
                layer_index,
                jnp.einsum("sf,sd->fd", hidden, grad_branch, preferred_element_type=float_type),
            )
            grad_hidden = jnp.einsum(
                "sd,fd->sf", grad_branch, fc_out_w, preferred_element_type=float_type
            )
            _, gelu_pull = jax.vjp(partial(jax.nn.gelu, approximate=False), pre_act)
            grad_pre = gelu_pull(grad_hidden)[0].astype(brain_type)
            add_into(
                grad_totals,
                8,
                layer_index,
                jnp.einsum("sd,sf->df", normed_two, grad_pre, preferred_element_type=float_type),
            )
            grad_normed = input_total(
                jnp.einsum("sf,df->sd", grad_pre, fc_in_w, preferred_element_type=float_type)
            )
            grad_mid_part, grad_gain, grad_shift = norm_backward(
                mid_rows, gain_two, shift_two, grad_normed
            )
            add_into(grad_totals, 6, layer_index, grad_gain)
            add_into(grad_totals, 7, layer_index, grad_shift)
            grad_mid = grad_rows + grad_mid_part
            grad_branch = branch_cotangent(grad_mid)
            add_into(
                grad_totals,
                5,
                layer_index,
                jnp.einsum("sa,sd->ad", attended, grad_branch, preferred_element_type=float_type),
            )
            grad_attended = jnp.einsum(
                "sd,ad->sa", grad_branch, output_w, preferred_element_type=float_type
            ).astype(brain_type)
            grad_queries, grad_keys, grad_values = attend_backward(
                queries.reshape(seq_len, -1, head_width),
                key_heads.reshape(seq_len, -1, head_width),
                values.reshape(seq_len, -1, head_width),
                segment,
                log_totals,
                grad_attended.reshape(seq_len, -1, head_width),
                block_rows,
            )
            add_into(
                grad_totals,
                2,
                layer_index,
                jnp.einsum("sd,sa->da", normed, grad_queries, preferred_element_type=float_type),
            )
            add_into(
                grad_totals,
                3,
                layer_index,
                jnp.einsum("sd,sa->da", normed, grad_keys, preferred_element_type=float_type),
            )
            add_into(
                grad_totals,
                4,
                layer_index,
                jnp.einsum("sd,sa->da", normed, grad_values, preferred_element_type=float_type),
            )
            grad_input_part = jnp.einsum(
                "sa,da->sd", grad_queries, query_w, preferred_element_type=float_type
            )
            grad_input_part = grad_input_part + jnp.einsum(
                "sa,da->sd", grad_keys, key_w, preferred_element_type=float_type
            )
            grad_input_part = grad_input_part + jnp.einsum(
                "sa,da->sd", grad_values, value_w, preferred_element_type=float_type
            )
            grad_normed = input_total(grad_input_part)
            grad_below, grad_gain, grad_shift = norm_backward(
                layer_rows, gain_one, shift_one, grad_normed
            )
            add_into(grad_totals, 0, layer_index, grad_gain)
            add_into(grad_totals, 1, layer_index, grad_shift)
            grad_rows = grad_mid + grad_below
        input_grad_list.append(grad_rows)
    reduced = (
        lax.psum_scatter(
            grad_totals[0].astype(jnp.bfloat16), "dp", scatter_dimension=1, tiled=True
        ).astype(jnp.float32),
        lax.psum_scatter(
            grad_totals[1].astype(jnp.bfloat16), "dp", scatter_dimension=1, tiled=True
        ).astype(jnp.float32),
        lax.psum_scatter(
            grad_totals[2].astype(jnp.bfloat16), "dp", scatter_dimension=1, tiled=True
        ).astype(jnp.float32),
        lax.psum_scatter(
            grad_totals[3].astype(jnp.bfloat16), "dp", scatter_dimension=1, tiled=True
        ).astype(jnp.float32),
        lax.psum_scatter(
            grad_totals[4].astype(jnp.bfloat16), "dp", scatter_dimension=1, tiled=True
        ).astype(jnp.float32),
        lax.psum_scatter(
            grad_totals[5].astype(jnp.bfloat16), "dp", scatter_dimension=2, tiled=True
        ).astype(jnp.float32),
        lax.psum_scatter(
            grad_totals[6].astype(jnp.bfloat16), "dp", scatter_dimension=1, tiled=True
        ).astype(jnp.float32),
        lax.psum_scatter(
            grad_totals[7].astype(jnp.bfloat16), "dp", scatter_dimension=1, tiled=True
        ).astype(jnp.float32),
        lax.psum_scatter(
            grad_totals[8].astype(jnp.bfloat16), "dp", scatter_dimension=1, tiled=True
        ).astype(jnp.float32),
        lax.psum_scatter(
            grad_totals[9].astype(jnp.bfloat16), "dp", scatter_dimension=2, tiled=True
        ).astype(jnp.float32),
    )
    norm_sums = lax.psum((reduced[0], reduced[1], reduced[6], reduced[7]), "tensor")
    block_output = jnp.stack(output_list)[:, None]
    input_grad = jnp.stack(input_grad_list)[:, None]
    return (
        block_output,
        input_grad,
        norm_sums[0],
        norm_sums[1],
        reduced[2],
        reduced[3],
        reduced[4],
        reduced[5],
        norm_sums[2],
        norm_sums[3],
        reduced[8],
        reduced[9],
    )


def solution(mesh):
    placed = (
        P(None, "dp", "tensor", None),
        P(None, "dp", None),
        P(None, "dp"),
        P(None, "dp"),
        P(None, "dp", "tensor"),
        P(None, "dp", "tensor"),
        P(None, "dp", "tensor"),
        P(None, "tensor", "dp"),
        P(None, "dp"),
        P(None, "dp"),
        P(None, "dp", "tensor"),
        P(None, "tensor", "dp"),
        P(None, "dp", "tensor", None),
    )
    line, plane = mesh.shape["tensor"], mesh.shape["dp"]
    fits = line == 4 and plane == 8 and 2 * line == plane
    return jax.shard_map(
        per_chip if fits else per_device,
        mesh=mesh,
        in_specs=placed,
        out_specs=(
            P(None, "dp", "tensor", None),
            P(None, "dp", "tensor", None),
            P(None, "dp"),
            P(None, "dp"),
            P(None, "dp", "tensor"),
            P(None, "dp", "tensor"),
            P(None, "dp", "tensor"),
            P(None, "tensor", "dp"),
            P(None, "dp"),
            P(None, "dp"),
            P(None, "dp", "tensor"),
            P(None, "tensor", "dp"),
        ),
        check_vma=False,
    )
```

```python
from functools import partial
import math

import jax
import jax.numpy as jnp
from jax import lax
from jax.experimental import pallas as pl
from jax.experimental.pallas import tpu as pltpu
from jax.sharding import PartitionSpec as P

D = 1024
HEADS = 16
float_type = jnp.float32
brain_type = jnp.bfloat16
CORE, XBIT, YBIT = 1, 2, 4
ZLOW, ZHIGH = 1, 2


def swap(block, axis_name, bit):
    size = lax.axis_size(axis_name)
    return lax.ppermute(block, axis_name, [(i, i ^ bit) for i in range(size)])


def after(block, earlier):
    return lax.optimization_barrier((block, earlier))[0]


def pick(flag, when_zero, when_one):
    return jnp.where(flag == 0, when_zero, when_one)


def tn_low(left, right):
    return tn(left, right).astype(brain_type)


def nt(left, right):
    return lax.dot_general(left, right, (((1,), (1,)), ((), ())), preferred_element_type=float_type)


def nn(left, right):
    return lax.dot_general(left, right, (((1,), (0,)), ((), ())), preferred_element_type=float_type)


def tn(left, right):
    return lax.dot_general(left, right, (((0,), (0,)), ((), ())), preferred_element_type=float_type)


def attend_back_kernel(score_scale, qkv_ref, grad_ref, seg_col_ref, seg_row_ref, out_ref, gk_ref, gv_ref):
    seq_len = qkv_ref.shape[0]
    rows = 256
    keys = qkv_ref[:, 128:256]
    values = qkv_ref[:, 256:384]
    low_lane = lax.broadcasted_iota(jnp.int32, (rows, 128), 1) < 64
    for part in range(seq_len // rows):
        span = slice(part * rows, (part + 1) * rows)
        query = qkv_ref[span, :128]
        grad = grad_ref[span, :]
        same = seg_col_ref[...] == seg_row_ref[:, span]
        grad_queries = []
        for head in range(2):
            mine = low_lane if head == 0 else jnp.logical_not(low_lane)
            masked = jnp.where(mine, query, jnp.zeros_like(query))
            grad_masked = jnp.where(mine, grad, jnp.zeros_like(grad))
            scores = jnp.where(same, nt(keys, masked) * score_scale, -1e30)
            top = jnp.max(scores, axis=0, keepdims=True)
            weight = jnp.exp(scores - top)
            total = jnp.sum(weight, axis=0, keepdims=True)
            probs = weight * (1.0 / total)
            grad_probs = nt(values, grad_masked)
            inner = jnp.sum(probs * grad_probs, axis=0, keepdims=True)
            grad_raw = (probs * (grad_probs - inner) * score_scale).astype(brain_type)
            gv_part = nn(probs.astype(brain_type), grad_masked)
            gk_part = nn(grad_raw, masked)
            if part == 0 and head == 0:
                gv_ref[...] = gv_part
                gk_ref[...] = gk_part
            else:
                gv_ref[...] += gv_part
                gk_ref[...] += gk_part
            grad_queries.append(tn(grad_raw, keys))
        out_ref[span, :128] = jnp.where(low_lane, grad_queries[0], grad_queries[1]).astype(brain_type)
    out_ref[:, 128:256] = gk_ref[...].astype(brain_type)
    out_ref[:, 256:384] = gv_ref[...].astype(brain_type)


def attend_back(qkv, grad, segment, score_scale):
    seq_len, width = qkv.shape
    blocks = width // 384
    return pl.pallas_call(
        partial(attend_back_kernel, score_scale),
        grid=(blocks,),
        in_specs=[
            pl.BlockSpec((seq_len, 384), lambda i: (0, i)),
            pl.BlockSpec((seq_len, 128), lambda i: (0, i)),
            pl.BlockSpec((seq_len, 1), lambda i: (0, 0)),
            pl.BlockSpec((1, seq_len), lambda i: (0, 0)),
        ],
        out_specs=pl.BlockSpec((seq_len, 384), lambda i: (0, i)),
        out_shape=jax.ShapeDtypeStruct((seq_len, width), brain_type),
        scratch_shapes=[
            pltpu.VMEM((seq_len, 128), float_type),
            pltpu.VMEM((seq_len, 128), float_type),
        ],
        compiler_params=pltpu.CompilerParams(vmem_limit_bytes=48 * 1024 * 1024),
        cost_estimate=pl.CostEstimate(
            flops=blocks * 2 * 5 * 4 * seq_len * seq_len * 64 * 2,
            bytes_accessed=seq_len * width * 5,
            transcendentals=blocks * 2 * seq_len * seq_len,
        ),
        name="attend_back",
    )(qkv, grad, segment[:, None], segment[None, :])


def center_of(rows):
    center = rows - jnp.mean(rows, axis=-1, keepdims=True)
    scale = lax.rsqrt(jnp.mean(center * center, axis=-1, keepdims=True) + 1e-05)
    return center * scale, scale


def normed_back(rows, gain, grad):
    unit, scale = center_of(rows)
    grad_unit = grad * gain
    below = scale * (
        grad_unit
        - jnp.mean(grad_unit, axis=-1, keepdims=True)
        - unit * jnp.mean(grad_unit * unit, axis=-1, keepdims=True)
    )
    return below, jnp.sum(grad * unit, axis=0), jnp.sum(grad, axis=0)


class Mover:
    def __init__(self, send_sems, recv_sems, local_sems):
        self.send_sems, self.recv_sems, self.local_sems = send_sems, recv_sems, local_sems
        self.remote, self.local = 0, 0
        self.place = lax.axis_index("dp")
        self.height = lax.axis_index("tensor")
        self.core = lax.rem(self.place, 2)
        self.x_bit = lax.rem(self.place // 2, 2)
        self.y_bit = lax.rem(self.place // 4, 2)
        self.z_low = lax.rem(self.height, 2)
        self.z_high = self.height // 2
        self.sibling = {"dp": self.place + 1 - 2 * self.core}
        self.x_side = {"dp": self.place + 2 - 4 * self.x_bit}
        self.y_side = {"dp": self.place + 4 - 8 * self.y_bit}
        self.z_near = {"tensor": self.height + 1 - 2 * self.z_low}
        self.z_far = {"tensor": self.height + 2 - 4 * self.z_high}

    def make(self, source, target, device, send_index, recv_index):
        return pltpu.make_async_remote_copy(
            src_ref=source,
            dst_ref=target,
            send_sem=self.send_sems.at[send_index],
            recv_sem=self.recv_sems.at[recv_index],
            device_id=device,
            device_id_type=pl.DeviceIdType.MESH,
        )

    def send(self, source, target, device):
        copy = self.make(source, target, device, self.remote, self.remote)
        self.remote += 1
        copy.start()
        return copy

    def keep(self, source, target):
        copy = pltpu.make_async_copy(source, target, self.local_sems.at[self.local])
        self.local += 1
        copy.start()
        return copy

    def greet(self):
        barrier = pltpu.get_barrier_semaphore()
        plane = self.place - self.core
        devices = [self.x_side, self.y_side]
        for step in range(1, 8):
            other = lax.rem(self.core * 4 + self.height + step, 8)
            devices.append({"dp": plane + other // 4, "tensor": lax.rem(other, 4)})
        for device in devices:
            pl.semaphore_signal(
                barrier, inc=1, device_id=device, device_id_type=pl.DeviceIdType.MESH
            )
        pl.semaphore_wait(barrier, len(devices))

    def column(self, y, x, half):
        y_off = lax.rem(y + self.y_bit, 2)
        x_off = lax.rem(x + self.x_bit, 2)
        spot = 2 * y_off + x_off if half == 0 else y_off + 2 * x_off
        return pl.multiple_of((half * 4 + spot) * 128, 128)


BLOCKS = [(y, x, half) for y in range(2) for x in range(2) for half in range(2)]


def move_tokens(move, ways, origins):
    base, local = move.remote, move.local
    move.remote += 2
    move.local += 2
    closing = []
    for i, (to_core, to_z, copies, whole, slot) in enumerate(ways):
        stays = jnp.logical_and(to_core == move.core, to_z == move.height)
        device = {"dp": move.place - move.core + to_core, "tensor": to_z}

        @pl.when(stays)
        def _():
            for source, target in copies:
                pltpu.make_async_copy(source, target, move.local_sems.at[local + i]).start()

        @pl.when(jnp.logical_not(stays))
        def _():
            for source, target in copies:
                move.make(source, target, device, base + i, base + slot).start()

        closing.append((stays, device, whole, i))

    def finish():
        for stays, device, (source, target), i in closing:
            @pl.when(stays)
            def _():
                pltpu.make_async_copy(source, target, move.local_sems.at[local + i]).wait()

            @pl.when(jnp.logical_not(stays))
            def _():
                move.make(source, target, device, base + i, base + i).wait_send()

        for slot, (from_core, from_z, (source, target)) in enumerate(origins):
            comes = jnp.logical_not(
                jnp.logical_and(from_core == move.core, from_z == move.height)
            )

            @pl.when(comes)
            def _():
                move.make(source, target, move.sibling, base + slot, base + slot).wait_recv()

    return finish


def fetch_tokens(move, source, target):
    rows = source.shape[1]
    here = pl.ds(pl.multiple_of(move.z_low * rows, rows), rows)
    ways, origins = [], []
    for micro in range(2):
        copies = [
            (
                source.at[micro, :, pl.ds(i * 128, 128)],
                target.at[here, pl.ds(move.column(*block), 128)],
            )
            for i, block in enumerate(BLOCKS)
        ]
        whole = (source.at[micro], target.at[here])
        ways.append((move.z_high, 2 * micro + move.core, copies, whole, move.z_low))
    for slot in range(2):
        whole = (source.at[slot], target.at[pl.ds(slot * rows, rows)])
        origins.append((move.z_low, 2 * move.core + slot, whole))
    return move_tokens(move, ways, origins)


def return_tokens(move, source, target):
    rows = target.shape[1]
    ways, origins = [], []
    for slot in range(2):
        copies = [
            (
                source.at[pl.ds(slot * rows, rows), pl.ds(move.column(*block), 128)],
                target.at[move.z_high, :, pl.ds(i * 128, 128)],
            )
            for i, block in enumerate(BLOCKS)
        ]
        whole = (source.at[pl.ds(slot * rows, rows)], target.at[move.z_high])
        ways.append((move.z_low, 2 * move.core + slot, copies, whole, move.z_high))
    for micro in range(2):
        whole = (source.at[pl.ds(micro * rows, rows)], target.at[micro])
        origins.append((move.z_high, 2 * micro + move.core, whole))
    return move_tokens(move, ways, origins)


def spread_stages(move, mine, other, whole, start=None):
    rows, units = mine.shape
    half = whole.shape[0] // 2
    own = pl.ds(pl.multiple_of(move.core * half, half), rows)

    def part(first, spot, lane, lanes):
        return whole.at[pl.ds(first * half + spot * rows, rows), pl.ds(lane * units, lanes * units)]

    copies = [
        move.send(other, whole.at[own, pl.ds(0, units)], move.sibling),
        move.keep(mine, whole.at[own, pl.ds(0, units)]),
    ]
    done = []

    def go(first, spot, lane, lanes, to_spot, to_lane, device):
        copy = move.send(part(first, spot, lane, lanes), part(first, to_spot, to_lane, lanes), device)
        done.append(copy)
        return copy

    def plane(lane, lanes):
        one = go(0, 0, lane, lanes, 1, lane, move.x_side)
        two = go(1, 0, lane, lanes, 1, lane, move.y_side)
        last = [
            go(0, 0, lane, lanes, 2, lane, move.y_side),
            go(1, 0, lane, lanes, 2, lane, move.x_side),
        ]
        return one, two, last, lane, lanes

    def relay(one, two, last, lane, lanes):
        one.wait_recv()
        last.append(go(0, 1, lane, lanes, 3, lane, move.y_side))
        two.wait_recv()
        last.append(go(1, 1, lane, lanes, 3, lane, move.x_side))
        return last

    yield
    copies[0].wait_send()
    copies[0].wait_recv()
    copies[1].wait()
    near = [go(first, 0, 0, 1, 0, 1, move.z_near) for first in range(2)]
    far = [go(first, 0, 0, 1, 0, 2, move.z_far) for first in range(2)]
    planes = [plane(0, 1)]
    yield
    for copy in near:
        copy.wait_recv()
    far += [go(first, 0, 1, 1, 0, 3, move.z_far) for first in range(2)]
    planes.append(plane(1, 1))
    yield
    lasts = relay(*planes[0])
    for copy in far:
        copy.wait_recv()
    planes.append(plane(2, 2))
    yield
    lasts += relay(*planes[1])
    yield
    lasts += relay(*planes[2])
    yield
    for copy in lasts:
        copy.wait_recv()
    for copy in done:
        copy.wait_send()


SPREAD_STEPS = 6


def vector_stages(move, vectors, out):
    own = move.core * 4
    keep = move.keep(vectors, out.at[own])
    copy = move.send(vectors, out.at[own], move.sibling)
    yield
    keep.wait()
    copy.wait()
    over_x = [move.send(out.at[i], out.at[j], move.x_side) for i, j in ((0, 1), (4, 6))]
    yield
    for copy in over_x:
        copy.wait()
    over_y = [
        move.send(out.at[i], out.at[j], move.y_side) for i, j in ((0, 2), (1, 3), (4, 5), (6, 7))
    ]
    yield
    for copy in over_y:
        copy.wait()


def hbm(count):
    return [pl.BlockSpec(memory_space=pl.ANY)] * count


def loop(count, body):
    def step(i, carry):
        body(i)
        return carry

    lax.fori_loop(0, count, step, 0)


def at(i, size):
    return pl.ds(pl.multiple_of(i * size, size), size)


def vector_row(vectors, index):
    return jnp.concatenate([vectors[spot, index : index + 1, :] for spot in range(8)], axis=1)


def segment_rows(move, own_ids, other_ids, seg_row, seg_col):
    own, other = own_ids[move.z_high], other_ids[move.z_high]
    ids = jnp.where(move.z_low == move.core, own, other).astype(float_type)
    half = ids.shape[1] // 2
    turned = jnp.concatenate([ids[:, half:], ids[:, :half]], axis=1)
    ids = jnp.where(move.core == 0, ids, turned)
    seg_row[...] = ids
    seg_col[...] = jnp.transpose(jnp.broadcast_to(ids, (128, 2 * half)))


def forward_steps(move, score_scale, layers, box):
    half = box["x"].shape[0]
    tile = 256
    vectors = box["vectors"]
    send, got = box["send"], box["got"]
    saves = {}

    def save(name, layer):
        source = box[name]
        copy = move.keep(source, box["saved"][layer][name])
        saves[name] = copy

    def before(*names):
        for name in names:
            if name in saves:
                saves.pop(name).wait()

    def norm(source, target, gain, shift):
        gain_row, shift_row = vector_row(vectors, gain), vector_row(vectors, shift)

        def body(i):
            rows = at(i, 64)
            target[rows, :] = (center_of(source[rows, :])[0] * gain_row + shift_row).astype(
                brain_type
            )

        loop(half // 64, body)
        return move.send(target.at[pl.ds(0, half)], target.at[pl.ds(half, half)], move.sibling)

    def partial_sums(left, weight, first):
        def body(i):
            columns = at(i, tile)
            send[:, columns] = nt(left[pl.ds(half, half), :], weight[columns, :]).astype(brain_type)

        loop(weight.shape[0] // tile, body)
        return move.send(send, got, move.sibling)

    def whole_sums(left, weight, base, target, copy):
        copy.wait()

        def body(i):
            columns = at(i, tile)
            target[:, columns] = (
                base[:, columns]
                + nt(left[pl.ds(0, half), :], weight[columns, :])
                + got[:, columns].astype(float_type)
            )

        loop(weight.shape[0] // tile, body)

    for layer in range(layers):
        x, mid, n1, n2 = box["x"], box["mid"], box["n1"], box["n2"]
        qkv, att, hid, slope = box["qkv"], box["att"], box["hid"], box["slope"]
        base = 4 * layer
        before("n1", "qkv")
        sent = norm(x, n1, layer, layers + layer)
        yield base
        box["load"](base)

        def project(first):
            def body(i):
                columns = at(i, tile)
                rows = pl.ds(first * half, half)
                qkv[rows, columns] = nn(n1[rows, :], box["w0"][:, columns]).astype(brain_type)

            loop(qkv.shape[1] // tile, body)

        project(0)
        yield None
        sent.wait()
        project(1)
        save("n1", layer)
        save("qkv", layer)
        before("att")
        yield None
        for pair in range(qkv.shape[1] // 384):

            def body(part, pair=pair):
                rows = at(part, tile)
                low_lane = lax.broadcasted_iota(jnp.int32, (tile, 128), 1) < 64
                query = qkv[rows, pl.ds(pair * 384, 128)] * jnp.asarray(score_scale, brain_type)
                keys = qkv[:, pl.ds(pair * 384 + 128, 128)]
                values = qkv[:, pl.ds(pair * 384 + 256, 128)]
                same = box["seg_col"][rows, :1] == box["seg_row"][...]
                outs = []
                for head in range(2):
                    mine = low_lane if head == 0 else jnp.logical_not(low_lane)
                    scores = nt(jnp.where(mine, query, jnp.zeros_like(query)), keys)
                    scores = jnp.where(same, scores, -1e30)
                    weight = jnp.exp(scores - jnp.max(scores, axis=1, keepdims=True))
                    inverse = 1.0 / jnp.sum(weight, axis=1, keepdims=True)
                    outs.append(nn((weight * inverse).astype(brain_type), values))
                att[rows, pl.ds(pair * 128, 128)] = jnp.where(low_lane, outs[0], outs[1]).astype(
                    brain_type
                )

            loop(2 * half // tile, body)
            yield None
        yield base + 1
        box["load"](base + 1)
        sent = partial_sums(att, box["w1"], half)
        save("att", layer)
        yield None
        before("mid", "n2")
        whole_sums(att, box["w1"], x, mid, sent)
        sent = norm(mid, n2, 2 * layers + layer, 3 * layers + layer)
        save("mid", layer)
        before("hid", "slope")
        yield base + 2
        box["load"](base + 2)
        for first in range(2):
            if first == 1:
                sent.wait()
                save("n2", layer)
            rows = pl.ds(first * half, half)
            count = hid.shape[1] // tile
            for part in range(2):

                def body(i, rows=rows, part=part):
                    columns = at(part * (count // 2) + i, tile)
                    pre = nn(n2[rows, :], box["w2"][:, columns])
                    cdf = 0.5 * (1.0 + lax.erf(pre * math.sqrt(0.5)))
                    density = jnp.exp(-0.5 * pre * pre) * (1.0 / math.sqrt(2.0 * math.pi))
                    hid[rows, columns] = (pre * cdf).astype(brain_type)
                    slope[rows, columns] = (cdf + pre * density).astype(brain_type)

                loop(count // 2, body)
                yield None
        save("slope", layer)
        yield base + 3
        box["load"](base + 3)
        before("n1", "qkv", "att", "n2")
        sent = partial_sums(hid, box["w3"], half)
        save("hid", layer)
        yield None
        before("x")
        whole_sums(hid, box["w3"], mid, x, sent)
        save("x", layer)
    before(*list(saves))


def forward_kernel(groups, layers, score_scale, *refs):
    refs = list(refs)

    def take(count):
        taken, refs[:count] = refs[:count], []
        return taken

    inputs, cotangent, vectors, ids = take(4)
    pieces = take(2 * groups)
    rows_out, grad_out, vectors_out, ids_out = take(4)
    wholes = take(groups)
    names = ("n1", "qkv", "att", "mid", "n2", "hid", "slope", "x")
    saved = [dict(zip(names, take(8))) for _ in range(layers)]
    box = dict(zip(names, take(8)))
    box["saved"] = saved
    weights = take(4)
    for i in range(4):
        box[f"w{i}"] = weights[i]
    box["send"], box["got"], x_in, box["vectors"] = take(4)
    own_ids, other_ids, box["seg_row"], box["seg_col"] = take(4)
    move = Mover(*refs)
    move.greet()
    finish_rows = fetch_tokens(move, inputs, rows_out)
    tasks = [
        spread_stages(move, pieces[2 * i], pieces[2 * i + 1], wholes[i]) for i in range(groups)
    ]
    for task in tasks:
        next(task)
    small = vector_stages(move, vectors, vectors_out)
    next(small)
    ids_copy = move.send(ids, other_ids, move.sibling)
    ids_here = move.keep(ids, own_ids)

    loads = {}
    complete = set()

    def load(group):
        loads.pop(group).wait()

    def start_load(group):
        loads[group] = move.keep(wholes[group], weights[group % 4])

    box["load"] = load
    compute = forward_steps(move, score_scale, layers, box)
    state = {"need": None, "begun": False, "over": False, "loaded": -1}

    def ready():
        return state["need"] is None or state["need"] in complete

    def prefetch():
        group = state["loaded"] + 1
        while group < groups and group in complete and (group < 4 or state["used"] > group - 4):
            start_load(group)
            state["loaded"] = group
            group += 1

    state["used"] = 0

    def advance(count):
        for _ in range(count):
            if state["over"] or not ready():
                return
            if state["need"] is not None:
                state["used"] = state["need"]
                prefetch()
            if state["need"] is not None and state["need"] not in loads:
                return
            try:
                state["need"] = next(compute)
            except StopIteration:
                state["over"] = True

    for tick in range(groups + SPREAD_STEPS - 1):
        for i in range(groups - 1, -1, -1):
            if 0 <= tick - i < SPREAD_STEPS:
                next(tasks[i], None)
                if tick - i == SPREAD_STEPS - 1:
                    complete.add(i)
                    prefetch()
                if state["begun"]:
                    advance(PACE)
        next(small, None)
        if tick == 2:
            ids_copy.wait()
            ids_here.wait()
            ids_kept = move.keep(other_ids, ids_out)
            segment_rows(move, own_ids, other_ids, box["seg_row"], box["seg_col"])
            finish_grad = fetch_tokens(move, cotangent, grad_out)
        if tick == 3:
            finish_rows()
            copies = [move.keep(rows_out, x_in), move.keep(vectors_out, box["vectors"])]
            for copy in copies:
                copy.wait()

            def body(i):
                rows = at(i, 64)
                box["x"][rows, :] = x_in[rows, :].astype(float_type)

            loop(x_in.shape[0] // 64, body)
            state["begun"] = True
            state["need"] = None
    while not state["over"]:
        advance(1)
    ids_kept.wait()
    finish_grad()


PACE = 1


def forward_all(inputs, cotangent, vectors, ids, pieces, layers, score_scale):
    groups = len(pieces)
    tokens, width = 2 * inputs.shape[1], inputs.shape[2]
    units = [p.shape[1] for p, _ in pieces[:4]]
    flat = [block for piece in pieces for block in piece]
    remote = 27 * groups + 16 + 4 * layers
    kept = [
        ((2 * tokens, width), brain_type),
        ((2 * tokens, 4 * units[0]), brain_type),
        ((2 * tokens, 4 * units[1]), brain_type),
        ((tokens, width), float_type),
        ((2 * tokens, width), brain_type),
        ((2 * tokens, 4 * units[2]), brain_type),
        ((2 * tokens, 4 * units[2]), brain_type),
        ((tokens, width), float_type),
    ]
    outs = pl.pallas_call(
        partial(forward_kernel, groups, layers, score_scale),
        out_shape=[
            jax.ShapeDtypeStruct((tokens, width), inputs.dtype),
            jax.ShapeDtypeStruct((tokens, width), inputs.dtype),
            jax.ShapeDtypeStruct((8, *vectors.shape), vectors.dtype),
            jax.ShapeDtypeStruct(ids.shape, ids.dtype),
        ]
        + [jax.ShapeDtypeStruct((8 * p.shape[0], 4 * p.shape[1]), p.dtype) for p, _ in pieces]
        + [jax.ShapeDtypeStruct(*shape) for _ in range(layers) for shape in kept],
        in_specs=hbm(4 + 2 * groups),
        out_specs=hbm(4 + groups + 8 * layers),
        scratch_shapes=[pltpu.VMEM(*shape) for shape in kept]
        + [pltpu.VMEM((8 * p.shape[0], 4 * p.shape[1]), p.dtype) for p, _ in pieces[:4]]
        + [
            pltpu.VMEM((tokens, width), brain_type),
            pltpu.VMEM((tokens, width), brain_type),
            pltpu.VMEM((tokens, width), brain_type),
            pltpu.VMEM((8, *vectors.shape), vectors.dtype),
            pltpu.VMEM(ids.shape, ids.dtype),
            pltpu.VMEM(ids.shape, ids.dtype),
            pltpu.VMEM((1, 2 * tokens), float_type),
            pltpu.VMEM((2 * tokens, 128), float_type),
            pltpu.SemaphoreType.DMA((remote,)),
            pltpu.SemaphoreType.DMA((remote,)),
            pltpu.SemaphoreType.DMA((2 * groups + 10 + 8 * layers,)),
        ],
        compiler_params=pltpu.CompilerParams(
            collective_id=0, has_side_effects=True, vmem_limit_bytes=60 * 1024 * 1024
        ),
        name="forward",
    )(inputs, cotangent, vectors, ids, *flat)
    saved = [outs[4 + groups + 8 * i : 12 + groups + 8 * i] for i in range(layers)]
    return outs[0], outs[1], outs[2], outs[3], outs[4 : 4 + groups], saved


def collect_stages(move, grads, out, loaded, first_got, second_got, far_got, near_got):
    quarter = grads.shape[0] // 4
    rows, units = quarter // 2, grads.shape[1] // 4
    sides = ((move.y_side, move.x_side), (move.x_side, move.y_side))
    done = []

    def go(source, target, device):
        copy = move.send(source, target, device)
        done.append(copy)
        return copy

    def total(target, source, height, width):
        step = 32

        def body(i, carry):
            span = (pl.ds(pl.multiple_of(i * step, step), step), pl.ds(0, width))
            target[span] = (
                target[span].astype(float_type) + source[span].astype(float_type)
            ).astype(brain_type)
            return carry

        lax.fori_loop(0, height // step, body, 0)

    first = [
        go(grads.at[pl.ds((2 * i + 1) * quarter, quarter)], first_got.at[i], sides[i][0])
        for i in range(2)
    ]
    loads = [
        move.keep(grads.at[pl.ds(2 * i * quarter, quarter)], loaded.at[i]) for i in range(2)
    ]
    yield
    second = []
    for i in range(2):
        loads[i].wait()
        first[i].wait_recv()
        total(loaded.at[i], first_got.at[i], quarter, 4 * units)
        second.append(go(loaded.at[i, pl.ds(rows, rows)], second_got.at[i], sides[i][1]))
    yield
    far = []
    for i in range(2):
        second[i].wait_recv()
        total(loaded.at[i], second_got.at[i], rows, 4 * units)
        far.append(
            go(loaded.at[i, pl.ds(0, rows), pl.ds(2 * units, 2 * units)], far_got.at[i], move.z_far)
        )
    yield
    near = []
    for i in range(2):
        far[i].wait_recv()
        total(loaded.at[i], far_got.at[i], rows, 2 * units)
        near.append(
            go(loaded.at[i, pl.ds(0, rows), pl.ds(units, units)], near_got.at[i], move.z_near)
        )
    yield
    for i in range(2):
        near[i].wait_recv()
        total(loaded.at[i], near_got.at[i], rows, units)
    ready = pl.ds(0, rows), pl.ds(0, units)
    last = go(loaded.at[(1 - move.core, *ready)], out.at[1], move.sibling)
    stay = move.keep(loaded.at[(move.core, *ready)], out.at[0])
    yield
    last.wait_recv()
    stay.wait()
    for copy in done:
        copy.wait_send()


COLLECT_STEPS = 6


def vector_sum_stages(move, vectors, out, sums, by_core, by_y, by_x, by_near, by_far):
    keep = move.keep(vectors.at[move.core], sums)
    copy = move.send(vectors.at[1 - move.core], by_core, move.sibling)
    yield
    keep.wait()
    copy.wait()
    sums[...] += by_core[...]
    copy = move.send(sums.at[pl.ds(2, 2)], by_y, move.y_side)
    yield
    copy.wait()
    sums[:2] += by_y[...]
    copy = move.send(sums.at[1], by_x, move.x_side)
    yield
    copy.wait()
    sums[0] += by_x[...]
    copy = move.send(sums.at[0], by_near, move.z_near)
    yield
    copy.wait()
    sums[1] = sums[0] + by_near[...]
    copy = move.send(sums.at[1], by_far, move.z_far)
    yield
    copy.wait()
    out[...] = sums[1] + by_far[...]


def collect_kernel(groups, *refs):
    above, below, vectors = refs[:3]
    grads = refs[3 : 3 + groups]
    above_out, below_out, vectors_out = refs[3 + groups : 6 + groups]
    outs = refs[6 + groups : 6 + 2 * groups]
    buffers = refs[6 + 2 * groups : 6 + 7 * groups]
    small_buffers = refs[6 + 7 * groups : 12 + 7 * groups]
    move = Mover(*refs[12 + 7 * groups :])
    move.greet()
    tasks = [
        collect_stages(move, grads[i], outs[i], *buffers[5 * i : 5 * i + 5]) for i in range(groups)
    ]
    for task in tasks:
        next(task)
    finish_above = return_tokens(move, above, above_out)
    finish_below = return_tokens(move, below, below_out)
    small = vector_sum_stages(move, vectors, vectors_out, *small_buffers)
    next(small)
    for tick in range(groups + COLLECT_STEPS - 1):
        for i in range(groups):
            if 0 <= tick - i < COLLECT_STEPS:
                next(tasks[i], None)
        next(small, None)
    finish_above()
    finish_below()


def collect_all(tokens, vectors, grads):
    groups = len(grads)
    width = tokens[0].shape[1]
    buffers = []
    for grad in grads:
        rows, units = grad.shape[0] // 8, grad.shape[1] // 4
        for height, lanes in ((2 * rows, 4), (2 * rows, 4), (rows, 4), (rows, 2), (rows, 1)):
            buffers.append(pltpu.VMEM((2, height, lanes * units), grad.dtype))
    for shape in ((4, 8, 128), (4, 8, 128), (2, 8, 128), (8, 128), (8, 128), (8, 128)):
        buffers.append(pltpu.VMEM(shape, vectors.dtype))
    remote = 9 * groups + 9
    outs = pl.pallas_call(
        partial(collect_kernel, groups),
        out_shape=[
            jax.ShapeDtypeStruct((2, tokens[0].shape[0] // 2, width), tokens[0].dtype)
            for _ in tokens
        ]
        + [
            jax.ShapeDtypeStruct(vectors.shape[2:], vectors.dtype),
        ]
        + [
            jax.ShapeDtypeStruct((2, g.shape[0] // 8, g.shape[1] // 4), g.dtype) for g in grads
        ],
        in_specs=hbm(3 + groups),
        out_specs=hbm(2) + [pl.BlockSpec(memory_space=pltpu.VMEM)] + hbm(groups),
        scratch_shapes=buffers
        + [
            pltpu.SemaphoreType.DMA((remote,)),
            pltpu.SemaphoreType.DMA((remote,)),
            pltpu.SemaphoreType.DMA((3 * groups + 5,)),
        ],
        compiler_params=pltpu.CompilerParams(
            collective_id=1, has_side_effects=True, vmem_limit_bytes=60 * 1024 * 1024
        ),
        name="collect",
    )(*tokens, vectors, *grads)
    return outs[:2], outs[2], outs[3:]


def per_chip(
    inputs,
    segment_ids,
    norm1_gain,
    norm1_shift,
    w_query,
    w_key,
    w_value,
    w_output,
    norm2_gain,
    norm2_shift,
    w_fc_in,
    w_fc_out,
    cotangent,
):
    layers = norm1_gain.shape[0]
    head_width = inputs.shape[3] // HEADS
    score_scale = 1.0 / math.sqrt(head_width)
    place = lax.axis_index("dp")
    height = lax.axis_index("tensor")
    core, x_bit, y_bit = place & 1, (place >> 1) & 1, (place >> 2) & 1
    z_low, z_high = height & 1, (height >> 1) & 1

    def halves(columns):
        wide = columns.shape[1] // 2
        low, high = columns[:, :wide], columns[:, wide:]
        return pick(core, low, high), pick(core, high, low)

    pieces = []
    for layer in range(layers):
        both = [halves(w[layer]) for w in (w_query, w_key, w_value)]
        pieces += [
            tuple(jnp.concatenate([b[side] for b in both], axis=1) for side in range(2)),
            halves(w_output[layer].T),
            halves(w_fc_in[layer]),
            halves(w_fc_out[layer].T),
        ]
    vectors = jnp.concatenate([norm1_gain, norm1_shift, norm2_gain, norm2_shift], axis=0)
    rows, grad, vectors, other_ids, weights, saved = forward_all(
        inputs[:, 0],
        cotangent[:, 0],
        vectors.astype(float_type),
        segment_ids,
        pieces,
        layers,
        score_scale,
    )
    below_rows = [rows.astype(float_type)] + [kept[7] for kept in saved]
    grad = grad.astype(float_type)
    vectors = vectors.transpose(1, 0, 2).reshape(4 * layers, -1)

    ids = pick(z_low ^ core, segment_ids, other_ids)
    ids = pick(z_high, ids[0, 0], ids[1, 0])
    half_len = ids.shape[0] // 2
    ids = pick(core, ids, jnp.concatenate([ids[half_len:], ids[:half_len]]))

    def whole_tokens(half):
        return jnp.concatenate([half, swap(half, "dp", CORE)], axis=0)

    def summed(product, left):
        rows_here = left.shape[0] // 2
        got = swap(product(left[rows_here:]).astype(brain_type), "dp", CORE)
        return product(left[:rows_here]) + got.astype(float_type)

    block_output = below_rows[layers]

    totals = [None] * (4 * layers)
    vector_grads = [None] * (4 * layers)
    for layer in reversed(range(layers)):
        normed_one, qkv, attended, mid, normed_two, hidden, slope, _ = saved[layer]
        rows = below_rows[layer]
        qkv_w, output_w, fc_in_w, fc_out_w = weights[4 * layer : 4 * layer + 4]
        gain_one, shift_one, gain_two, shift_two = (vectors[i * layers + layer] for i in range(4))
        branch = whole_tokens(grad.astype(brain_type))
        totals[4 * layer + 3] = tn_low(branch, hidden)
        grad_pre = (nn(branch, fc_out_w) * slope.astype(float_type)).astype(brain_type)
        totals[4 * layer + 2] = tn_low(normed_two, grad_pre)
        grad_normed = summed(lambda left: nt(left, fc_in_w), grad_pre)
        below, vector_grads[2 * layers + layer], vector_grads[3 * layers + layer] = normed_back(
            mid, gain_two, grad_normed
        )
        grad = grad + below
        branch = whole_tokens(grad.astype(brain_type))
        totals[4 * layer + 1] = tn_low(branch, attended)
        grad_attended = nn(branch, output_w).astype(brain_type)
        grad_qkv = attend_back(qkv, grad_attended, ids, score_scale)
        totals[4 * layer] = tn_low(normed_one, grad_qkv)
        grad_normed = summed(lambda left: nt(left, qkv_w), grad_qkv)
        below, vector_grads[layer], vector_grads[layers + layer] = normed_back(
            rows, gain_one, grad_normed
        )
        grad = grad + below
    vector_grads = jnp.stack(vector_grads).reshape(4 * layers, 2, 4, -1)
    second = vector_grads[:, 1]
    second = jnp.stack([second[:, i] for i in (0, 2, 1, 3)], axis=1)
    vector_grads = jnp.stack([vector_grads[:, 0], second])
    order = [4 * layer + kind for layer in reversed(range(layers)) for kind in (3, 2, 1, 0)]
    block_output, vector_grads, outs = collect_all(
        (block_output.astype(brain_type), grad.astype(brain_type)),
        vector_grads.transpose(0, 2, 1, 3),
        [totals[i] for i in order],
    )
    outs = [(pick(core, out[0], out[1]), pick(core, out[1], out[0])) for out in outs]
    outs = [outs[order.index(i)] for i in range(4 * layers)]
    block_output, input_grad = (tokens.astype(float_type) for tokens in block_output)

    def joined(kind, columns=None):
        per_layer = []
        for layer in range(layers):
            low, high = outs[4 * layer + kind]
            if columns is not None:
                low, high = low[:, columns], high[:, columns]
            per_layer.append(jnp.concatenate([low, high], axis=1))
        return jnp.stack(per_layer)

    width = w_query.shape[2] // 2
    grad_query, grad_key, grad_value = (joined(0, slice(i * width, (i + 1) * width)) for i in range(3))
    grad_output = joined(1).transpose(0, 2, 1)
    grad_fc_in = joined(2)
    grad_fc_out = joined(3).transpose(0, 2, 1)

    gain_one, shift_one, gain_two, shift_two = (
        vector_grads[i * layers : (i + 1) * layers] for i in range(4)
    )
    return (
        block_output[:, None],
        input_grad[:, None],
        gain_one,
        shift_one,
        grad_query.astype(float_type),
        grad_key.astype(float_type),
        grad_value.astype(float_type),
        grad_output.astype(float_type),
        gain_two,
        shift_two,
        grad_fc_in.astype(float_type),
        grad_fc_out.astype(float_type),
    )


def layer_norm(token_rows, gain_vec, shift_vec):
    center = token_rows - jnp.mean(token_rows, axis=-1, keepdims=True)
    spread = jnp.mean(center * center, axis=-1, keepdims=True)
    return center * lax.rsqrt(spread + 1e-05) * gain_vec + shift_vec


def normed_local(token_rows, gain_vec, shift_vec):
    return layer_norm(token_rows, gain_vec.astype(float_type), shift_vec.astype(float_type)).astype(
        brain_type
    )


def normed_send(token_rows, gain_vec, shift_vec):
    return lax.all_gather(
        normed_local(token_rows, gain_vec, shift_vec), "tensor", axis=0, tiled=True
    )


def normed_resend(token_rows, gain_vec, shift_vec):
    return lax.all_gather(
        normed_local(token_rows, gain_vec, shift_vec), "tensor", axis=0, tiled=True
    )


def branch_total(partial_sum):
    return lax.psum_scatter(
        partial_sum.astype(jnp.bfloat16), "tensor", scatter_dimension=0, tiled=True
    ).astype(jnp.float32)


def branch_cotangent(grad_rows):
    return lax.all_gather(grad_rows.astype(brain_type), "tensor", axis=0, tiled=True)


def input_total(partial_sum):
    return lax.psum_scatter(
        partial_sum.astype(jnp.bfloat16), "tensor", scatter_dimension=0, tiled=True
    ).astype(jnp.float32)


def norm_backward(token_rows, gain_vec, shift_vec, grad_normed):
    _, norm_pull = jax.vjp(
        layer_norm, token_rows, gain_vec.astype(float_type), shift_vec.astype(float_type)
    )
    return norm_pull(grad_normed)


def masked_scores(query_part, segment_part, key_heads, segment, score_scale):
    raw_scores = jnp.einsum(
        "qhd,khd->hqk", query_part, key_heads, preferred_element_type=float_type
    )
    same_scene = segment_part[:, None] == segment[None, :]
    return jnp.where(same_scene[None], raw_scores * score_scale, -1e30)


def attend_forward(queries, key_heads, values, segment, block_rows):
    seq_len, head_count, head_width = queries.shape
    score_scale = 1.0 / math.sqrt(head_width)
    block_count = seq_len // block_rows

    def one_block(block_pair):
        query_part, segment_part = block_pair
        scores = masked_scores(query_part, segment_part, key_heads, segment, score_scale)
        row_max = jnp.max(scores, axis=-1, keepdims=True)
        exp_scores = jnp.exp(scores - row_max)
        row_total = jnp.sum(exp_scores, axis=-1, keepdims=True)
        probabilities = (exp_scores / row_total).astype(brain_type)
        block_out = jnp.einsum(
            "hqk,khd->qhd", probabilities, values, preferred_element_type=float_type
        )
        log_total = (row_max + jnp.log(row_total))[..., 0]
        return (block_out.astype(brain_type), log_total)

    query_blocks = queries.reshape(block_count, block_rows, head_count, head_width)
    segment_blocks = segment.reshape(block_count, block_rows)
    outputs, log_totals = lax.map(one_block, (query_blocks, segment_blocks))
    return (outputs.reshape(seq_len, head_count * head_width), log_totals)


def attend_backward(queries, key_heads, values, segment, log_totals, grad_out, block_rows):
    seq_len, head_count, head_width = queries.shape
    score_scale = 1.0 / math.sqrt(head_width)
    block_count = seq_len // block_rows

    def one_block(carry_pair, block_items):
        grad_keys, grad_values = carry_pair
        query_part, segment_part, log_part, grad_part = block_items
        scores = masked_scores(query_part, segment_part, key_heads, segment, score_scale)
        probabilities = jnp.exp(scores - log_part[..., None])
        grad_probs = jnp.einsum(
            "qhd,khd->hqk", grad_part, values, preferred_element_type=float_type
        )
        row_inner = jnp.sum(probabilities * grad_probs, axis=-1, keepdims=True)
        grad_raw = (probabilities * (grad_probs - row_inner) * score_scale).astype(brain_type)
        grad_query = jnp.einsum(
            "hqk,khd->qhd", grad_raw, key_heads, preferred_element_type=float_type
        )
        grad_keys = grad_keys + jnp.einsum(
            "hqk,qhd->khd", grad_raw, query_part, preferred_element_type=float_type
        )
        grad_values = grad_values + jnp.einsum(
            "hqk,qhd->khd",
            probabilities.astype(brain_type),
            grad_part,
            preferred_element_type=float_type,
        )
        return ((grad_keys, grad_values), grad_query.astype(brain_type))

    zero_heads = jnp.zeros((seq_len, head_count, head_width), float_type)
    block_items = (
        queries.reshape(block_count, block_rows, head_count, head_width),
        segment.reshape(block_count, block_rows),
        log_totals,
        grad_out.reshape(block_count, block_rows, head_count, head_width),
    )
    (grad_keys, grad_values), grad_queries = lax.scan(
        one_block, (zero_heads, zero_heads), block_items
    )
    flat_shape = (seq_len, head_count * head_width)
    return (
        grad_queries.reshape(flat_shape),
        grad_keys.astype(brain_type).reshape(flat_shape),
        grad_values.astype(brain_type).reshape(flat_shape),
    )


def fresh_totals(layers, attn_width, hidden_width):
    vector_zero = jnp.zeros((layers, D), float_type)
    column_zero = jnp.zeros((layers, D, attn_width), float_type)
    return [
        vector_zero,
        vector_zero,
        column_zero,
        column_zero,
        column_zero,
        jnp.zeros((layers, attn_width, D), float_type),
        vector_zero,
        vector_zero,
        jnp.zeros((layers, D, hidden_width), float_type),
        jnp.zeros((layers, hidden_width, D), float_type),
    ]


def add_into(grad_totals, position, layer_index, term):
    grad_totals[position] = grad_totals[position].at[layer_index].add(term)


def per_device(
    inputs,
    segment_ids,
    norm1_gain,
    norm1_shift,
    w_query,
    w_key,
    w_value,
    w_output,
    norm2_gain,
    norm2_shift,
    w_fc_in,
    w_fc_out,
    cotangent,
):
    micro_count = inputs.shape[0]
    layers = norm1_gain.shape[0]
    seq_len = segment_ids.shape[2]
    block_rows = min(512, seq_len)
    head_width = D // HEADS
    attn_width = w_query.shape[2]
    hidden_width = w_fc_in.shape[2]
    grad_totals = fresh_totals(layers, attn_width, hidden_width)
    reduced = None
    output_list = []
    input_grad_list = []
    for micro_index in range(micro_count):
        token_rows = inputs[micro_index, 0].astype(float_type)
        segment = segment_ids[micro_index, 0]
        saved_state = []
        for layer_index in range(layers):
            weights = (
                lax.all_gather(norm1_gain[layer_index], "dp", axis=0, tiled=True),
                lax.all_gather(norm1_shift[layer_index], "dp", axis=0, tiled=True),
                lax.all_gather(w_query[layer_index], "dp", axis=0, tiled=True),
                lax.all_gather(w_key[layer_index], "dp", axis=0, tiled=True),
                lax.all_gather(w_value[layer_index], "dp", axis=0, tiled=True),
                lax.all_gather(w_output[layer_index], "dp", axis=1, tiled=True),
                lax.all_gather(norm2_gain[layer_index], "dp", axis=0, tiled=True),
                lax.all_gather(norm2_shift[layer_index], "dp", axis=0, tiled=True),
                lax.all_gather(w_fc_in[layer_index], "dp", axis=0, tiled=True),
                lax.all_gather(w_fc_out[layer_index], "dp", axis=1, tiled=True),
            )
            (
                gain_one,
                shift_one,
                query_w,
                key_w,
                value_w,
                output_w,
                gain_two,
                shift_two,
                fc_in_w,
                fc_out_w,
            ) = weights
            whole_weights = None
            normed = normed_send(token_rows, gain_one, shift_one)
            queries = jnp.dot(normed, query_w, preferred_element_type=float_type).astype(brain_type)
            key_heads = jnp.dot(normed, key_w, preferred_element_type=float_type).astype(brain_type)
            values = jnp.dot(normed, value_w, preferred_element_type=float_type).astype(brain_type)
            attended, log_totals = attend_forward(
                queries.reshape(seq_len, -1, head_width),
                key_heads.reshape(seq_len, -1, head_width),
                values.reshape(seq_len, -1, head_width),
                segment,
                block_rows,
            )
            mid_rows = token_rows + branch_total(
                jnp.dot(attended, output_w, preferred_element_type=float_type)
            )
            normed_two = normed_send(mid_rows, gain_two, shift_two)
            pre_act = jnp.dot(normed_two, fc_in_w, preferred_element_type=float_type)
            hidden = jax.nn.gelu(pre_act, approximate=False).astype(brain_type)
            next_rows = mid_rows + branch_total(
                jnp.dot(hidden, fc_out_w, preferred_element_type=float_type)
            )
            saved_state.append(
                (
                    token_rows,
                    mid_rows,
                    weights,
                    normed,
                    normed_two,
                    queries,
                    key_heads,
                    values,
                    attended,
                    log_totals,
                    pre_act,
                    hidden,
                    whole_weights,
                )
            )
            token_rows = next_rows
        output_list.append(token_rows)
        grad_rows = cotangent[micro_index, 0].astype(float_type)
        for layer_index in reversed(range(layers)):
            (
                layer_rows,
                mid_rows,
                weights,
                normed,
                normed_two,
                queries,
                key_heads,
                values,
                attended,
                log_totals,
                pre_act,
                hidden,
                whole_weights,
            ) = saved_state[layer_index]
            weights = (
                lax.all_gather(norm1_gain[layer_index], "dp", axis=0, tiled=True),
                lax.all_gather(norm1_shift[layer_index], "dp", axis=0, tiled=True),
                lax.all_gather(w_query[layer_index], "dp", axis=0, tiled=True),
                lax.all_gather(w_key[layer_index], "dp", axis=0, tiled=True),
                lax.all_gather(w_value[layer_index], "dp", axis=0, tiled=True),
                lax.all_gather(w_output[layer_index], "dp", axis=1, tiled=True),
                lax.all_gather(norm2_gain[layer_index], "dp", axis=0, tiled=True),
                lax.all_gather(norm2_shift[layer_index], "dp", axis=0, tiled=True),
                lax.all_gather(w_fc_in[layer_index], "dp", axis=0, tiled=True),
                lax.all_gather(w_fc_out[layer_index], "dp", axis=1, tiled=True),
            )
            (
                gain_one,
                shift_one,
                query_w,
                key_w,
                value_w,
                output_w,
                gain_two,
                shift_two,
                fc_in_w,
                fc_out_w,
            ) = weights
            normed = normed_resend(layer_rows, gain_one, shift_one)
            normed_two = normed_resend(mid_rows, gain_two, shift_two)
            grad_branch = branch_cotangent(grad_rows)
            add_into(
                grad_totals,
                9,
                layer_index,
                jnp.einsum("sf,sd->fd", hidden, grad_branch, preferred_element_type=float_type),
            )
            grad_hidden = jnp.einsum(
                "sd,fd->sf", grad_branch, fc_out_w, preferred_element_type=float_type
            )
            _, gelu_pull = jax.vjp(partial(jax.nn.gelu, approximate=False), pre_act)
            grad_pre = gelu_pull(grad_hidden)[0].astype(brain_type)
            add_into(
                grad_totals,
                8,
                layer_index,
                jnp.einsum("sd,sf->df", normed_two, grad_pre, preferred_element_type=float_type),
            )
            grad_normed = input_total(
                jnp.einsum("sf,df->sd", grad_pre, fc_in_w, preferred_element_type=float_type)
            )
            grad_mid_part, grad_gain, grad_shift = norm_backward(
                mid_rows, gain_two, shift_two, grad_normed
            )
            add_into(grad_totals, 6, layer_index, grad_gain)
            add_into(grad_totals, 7, layer_index, grad_shift)
            grad_mid = grad_rows + grad_mid_part
            grad_branch = branch_cotangent(grad_mid)
            add_into(
                grad_totals,
                5,
                layer_index,
                jnp.einsum("sa,sd->ad", attended, grad_branch, preferred_element_type=float_type),
            )
            grad_attended = jnp.einsum(
                "sd,ad->sa", grad_branch, output_w, preferred_element_type=float_type
            ).astype(brain_type)
            grad_queries, grad_keys, grad_values = attend_backward(
                queries.reshape(seq_len, -1, head_width),
                key_heads.reshape(seq_len, -1, head_width),
                values.reshape(seq_len, -1, head_width),
                segment,
                log_totals,
                grad_attended.reshape(seq_len, -1, head_width),
                block_rows,
            )
            add_into(
                grad_totals,
                2,
                layer_index,
                jnp.einsum("sd,sa->da", normed, grad_queries, preferred_element_type=float_type),
            )
            add_into(
                grad_totals,
                3,
                layer_index,
                jnp.einsum("sd,sa->da", normed, grad_keys, preferred_element_type=float_type),
            )
            add_into(
                grad_totals,
                4,
                layer_index,
                jnp.einsum("sd,sa->da", normed, grad_values, preferred_element_type=float_type),
            )
            grad_input_part = jnp.einsum(
                "sa,da->sd", grad_queries, query_w, preferred_element_type=float_type
            )
            grad_input_part = grad_input_part + jnp.einsum(
                "sa,da->sd", grad_keys, key_w, preferred_element_type=float_type
            )
            grad_input_part = grad_input_part + jnp.einsum(
                "sa,da->sd", grad_values, value_w, preferred_element_type=float_type
            )
            grad_normed = input_total(grad_input_part)
            grad_below, grad_gain, grad_shift = norm_backward(
                layer_rows, gain_one, shift_one, grad_normed
            )
            add_into(grad_totals, 0, layer_index, grad_gain)
            add_into(grad_totals, 1, layer_index, grad_shift)
            grad_rows = grad_mid + grad_below
        input_grad_list.append(grad_rows)
    reduced = (
        lax.psum_scatter(
            grad_totals[0].astype(jnp.bfloat16), "dp", scatter_dimension=1, tiled=True
        ).astype(jnp.float32),
        lax.psum_scatter(
            grad_totals[1].astype(jnp.bfloat16), "dp", scatter_dimension=1, tiled=True
        ).astype(jnp.float32),
        lax.psum_scatter(
            grad_totals[2].astype(jnp.bfloat16), "dp", scatter_dimension=1, tiled=True
        ).astype(jnp.float32),
        lax.psum_scatter(
            grad_totals[3].astype(jnp.bfloat16), "dp", scatter_dimension=1, tiled=True
        ).astype(jnp.float32),
        lax.psum_scatter(
            grad_totals[4].astype(jnp.bfloat16), "dp", scatter_dimension=1, tiled=True
        ).astype(jnp.float32),
        lax.psum_scatter(
            grad_totals[5].astype(jnp.bfloat16), "dp", scatter_dimension=2, tiled=True
        ).astype(jnp.float32),
        lax.psum_scatter(
            grad_totals[6].astype(jnp.bfloat16), "dp", scatter_dimension=1, tiled=True
        ).astype(jnp.float32),
        lax.psum_scatter(
            grad_totals[7].astype(jnp.bfloat16), "dp", scatter_dimension=1, tiled=True
        ).astype(jnp.float32),
        lax.psum_scatter(
            grad_totals[8].astype(jnp.bfloat16), "dp", scatter_dimension=1, tiled=True
        ).astype(jnp.float32),
        lax.psum_scatter(
            grad_totals[9].astype(jnp.bfloat16), "dp", scatter_dimension=2, tiled=True
        ).astype(jnp.float32),
    )
    norm_sums = lax.psum((reduced[0], reduced[1], reduced[6], reduced[7]), "tensor")
    block_output = jnp.stack(output_list)[:, None]
    input_grad = jnp.stack(input_grad_list)[:, None]
    return (
        block_output,
        input_grad,
        norm_sums[0],
        norm_sums[1],
        reduced[2],
        reduced[3],
        reduced[4],
        reduced[5],
        norm_sums[2],
        norm_sums[3],
        reduced[8],
        reduced[9],
    )


def solution(mesh):
    placed = (
        P(None, "dp", "tensor", None),
        P(None, "dp", None),
        P(None, "dp"),
        P(None, "dp"),
        P(None, "dp", "tensor"),
        P(None, "dp", "tensor"),
        P(None, "dp", "tensor"),
        P(None, "tensor", "dp"),
        P(None, "dp"),
        P(None, "dp"),
        P(None, "dp", "tensor"),
        P(None, "tensor", "dp"),
        P(None, "dp", "tensor", None),
    )
    line, plane = mesh.shape["tensor"], mesh.shape["dp"]
    fits = line == 4 and plane == 8 and 2 * line == plane
    return jax.shard_map(
        per_chip if fits else per_device,
        mesh=mesh,
        in_specs=placed,
        out_specs=(
            P(None, "dp", "tensor", None),
            P(None, "dp", "tensor", None),
            P(None, "dp"),
            P(None, "dp"),
            P(None, "dp", "tensor"),
            P(None, "dp", "tensor"),
            P(None, "dp", "tensor"),
            P(None, "tensor", "dp"),
            P(None, "dp"),
            P(None, "dp"),
            P(None, "dp", "tensor"),
            P(None, "tensor", "dp"),
        ),
        check_vma=False,
    )
```

```python
from functools import partial
import math

import jax
import jax.numpy as jnp
from jax import lax
from jax.experimental import pallas as pl
from jax.experimental.pallas import tpu as pltpu
from jax.sharding import PartitionSpec as P

D = 1024
HEADS = 16
float_type = jnp.float32
brain_type = jnp.bfloat16


def pick(flag, when_zero, when_one):
    return jnp.where(flag == 0, when_zero, when_one)


def nt(left, right):
    return lax.dot_general(left, right, (((1,), (1,)), ((), ())), preferred_element_type=float_type)


def nn(left, right):
    return lax.dot_general(left, right, (((1,), (0,)), ((), ())), preferred_element_type=float_type)


def tn(left, right):
    return lax.dot_general(left, right, (((0,), (0,)), ((), ())), preferred_element_type=float_type)


def center_of(rows):
    center = rows - jnp.mean(rows, axis=-1, keepdims=True)
    scale = lax.rsqrt(jnp.mean(center * center, axis=-1, keepdims=True) + 1e-05)
    return center * scale, scale


class Mover:
    def __init__(self, send_sems, recv_sems, local_sems):
        self.send_sems, self.recv_sems, self.local_sems = send_sems, recv_sems, local_sems
        self.remote, self.local = 0, 0
        self.place = lax.axis_index("dp")
        self.height = lax.axis_index("tensor")
        self.core = lax.rem(self.place, 2)
        self.x_bit = lax.rem(self.place // 2, 2)
        self.y_bit = lax.rem(self.place // 4, 2)
        self.z_low = lax.rem(self.height, 2)
        self.z_high = self.height // 2
        self.sibling = {"dp": self.place + 1 - 2 * self.core}
        self.x_side = {"dp": self.place + 2 - 4 * self.x_bit}
        self.y_side = {"dp": self.place + 4 - 8 * self.y_bit}
        self.z_near = {"tensor": self.height + 1 - 2 * self.z_low}
        self.z_far = {"tensor": self.height + 2 - 4 * self.z_high}

    def make(self, source, target, device, send_index, recv_index):
        return pltpu.make_async_remote_copy(
            src_ref=source,
            dst_ref=target,
            send_sem=self.send_sems.at[send_index],
            recv_sem=self.recv_sems.at[recv_index],
            device_id=device,
            device_id_type=pl.DeviceIdType.MESH,
        )

    def send(self, source, target, device):
        copy = self.make(source, target, device, self.remote, self.remote)
        self.remote += 1
        copy.start()
        return copy

    def keep(self, source, target):
        copy = pltpu.make_async_copy(source, target, self.local_sems.at[self.local])
        self.local += 1
        copy.start()
        return copy

    def greet(self):
        barrier = pltpu.get_barrier_semaphore()
        plane = self.place - self.core
        devices = [self.x_side, self.y_side]
        for step in range(1, 8):
            other = lax.rem(self.core * 4 + self.height + step, 8)
            devices.append({"dp": plane + other // 4, "tensor": lax.rem(other, 4)})
        for device in devices:
            pl.semaphore_signal(
                barrier, inc=1, device_id=device, device_id_type=pl.DeviceIdType.MESH
            )
        pl.semaphore_wait(barrier, len(devices))

    def column(self, y, x, half):
        y_off = lax.rem(y + self.y_bit, 2)
        x_off = lax.rem(x + self.x_bit, 2)
        spot = 2 * y_off + x_off if half == 0 else y_off + 2 * x_off
        return pl.multiple_of((half * 4 + spot) * 128, 128)


BLOCKS = [(y, x, half) for y in range(2) for x in range(2) for half in range(2)]


def move_tokens(move, ways, origins):
    base, local = move.remote, move.local
    move.remote += 2
    move.local += 2
    closing = []
    for i, (to_core, to_z, copies, whole, slot) in enumerate(ways):
        stays = jnp.logical_and(to_core == move.core, to_z == move.height)
        device = {"dp": move.place - move.core + to_core, "tensor": to_z}

        @pl.when(stays)
        def _():
            for source, target in copies:
                pltpu.make_async_copy(source, target, move.local_sems.at[local + i]).start()

        @pl.when(jnp.logical_not(stays))
        def _():
            for source, target in copies:
                move.make(source, target, device, base + i, base + slot).start()

        closing.append((stays, device, whole, i))

    def finish():
        for stays, device, (source, target), i in closing:
            @pl.when(stays)
            def _():
                pltpu.make_async_copy(source, target, move.local_sems.at[local + i]).wait()

            @pl.when(jnp.logical_not(stays))
            def _():
                move.make(source, target, device, base + i, base + i).wait_send()

        for slot, (from_core, from_z, (source, target)) in enumerate(origins):
            comes = jnp.logical_not(
                jnp.logical_and(from_core == move.core, from_z == move.height)
            )

            @pl.when(comes)
            def _():
                move.make(source, target, move.sibling, base + slot, base + slot).wait_recv()

    return finish


def fetch_tokens(move, source, target):
    rows = source.shape[1]
    here = pl.ds(pl.multiple_of(move.z_low * rows, rows), rows)
    ways, origins = [], []
    for micro in range(2):
        copies = [
            (
                source.at[micro, :, pl.ds(i * 128, 128)],
                target.at[here, pl.ds(move.column(*block), 128)],
            )
            for i, block in enumerate(BLOCKS)
        ]
        whole = (source.at[micro], target.at[here])
        ways.append((move.z_high, 2 * micro + move.core, copies, whole, move.z_low))
    for slot in range(2):
        whole = (source.at[slot], target.at[pl.ds(slot * rows, rows)])
        origins.append((move.z_low, 2 * move.core + slot, whole))
    return move_tokens(move, ways, origins)


def return_tokens(move, source, target):
    rows = target.shape[1]
    ways, origins = [], []
    for slot in range(2):
        copies = [
            (
                source.at[pl.ds(slot * rows, rows), pl.ds(move.column(*block), 128)],
                target.at[move.z_high, :, pl.ds(i * 128, 128)],
            )
            for i, block in enumerate(BLOCKS)
        ]
        whole = (source.at[pl.ds(slot * rows, rows)], target.at[move.z_high])
        ways.append((move.z_low, 2 * move.core + slot, copies, whole, move.z_high))
    for micro in range(2):
        whole = (source.at[pl.ds(micro * rows, rows)], target.at[micro])
        origins.append((move.z_high, 2 * micro + move.core, whole))
    return move_tokens(move, ways, origins)


class Clock:
    def __init__(self):
        self.now = 0.0
        self.free = {}

    def post(self, size, links):
        start, end = self.now, self.now
        for link, share in links:
            begin = max(self.free.get(link, 0.0), self.now)
            self.free[link] = begin + share * size * PER_BYTE
            end = max(end, self.free[link])
        return end + LATENCY


PER_BYTE = 2.0 / 88e3
LATENCY = 1.5
OVER_X, OVER_Y = (("x", 1.0),), (("y", 1.0),)
OVER_NEAR, OVER_FAR = (("z_out", 1.0),), (("z_out", 1.0), ("z_mid", 2.0))
OVER_CORE = (("core", 0.1),)


class Plan:
    def __init__(self, clock):
        self.clock, self.tasks = clock, []

    def add(self, task):
        due = next(task, None)
        if due is not None:
            self.tasks.append((due, task))

    def step(self):
        index = min(range(len(self.tasks)), key=lambda i: self.tasks[i][0])
        due, task = self.tasks.pop(index)
        self.clock.now = max(self.clock.now, due)
        self.add(task)

    def due(self):
        return min((due for due, _ in self.tasks), default=float("inf"))

    def finish(self, task):
        while any(task is other for _, other in self.tasks):
            self.step()

    def run(self, compute, ready):
        over = False
        while self.tasks or not over:
            if self.due() <= self.clock.now:
                self.step()
            elif not over and ready():
                cost = next(compute, None)
                if cost is None:
                    over = True
                else:
                    self.clock.now += cost
            elif self.tasks:
                self.step()


def size_of(ref):
    return math.prod(ref.shape) * jnp.dtype(ref.dtype).itemsize


def spread_group(move, plan, mine, other, whole, onward, complete):
    clock = plan.clock
    rows, units = mine.shape
    half = whole.shape[0] // 2
    own = pl.ds(pl.multiple_of(move.core * half, half), rows)
    done, planes = [], []

    def part(first, spot, lane, lanes):
        return whole.at[pl.ds(first * half + spot * rows, rows), pl.ds(lane * units, lanes * units)]

    def go(first, spot, lane, lanes, to_spot, to_lane, device, links):
        source = part(first, spot, lane, lanes)
        copy = move.send(source, part(first, to_spot, to_lane, lanes), device)
        done.append(copy)
        return copy, clock.post(size_of(source), links)

    x_way, y_way = (move.x_side, OVER_X), (move.y_side, OVER_Y)

    def plane(lane, lanes):
        one = go(0, 0, lane, lanes, 1, lane, *x_way)
        two = go(1, 0, lane, lanes, 1, lane, *y_way)
        last = [go(0, 0, lane, lanes, 2, lane, *y_way), go(1, 0, lane, lanes, 2, lane, *x_way)]

        def relay():
            yield one[1]
            one[0].wait_recv()
            last.append(go(0, 1, lane, lanes, 3, lane, *y_way))
            yield two[1]
            two[0].wait_recv()
            last.append(go(1, 1, lane, lanes, 3, lane, *x_way))
            yield max(due for _, due in last)
            for copy, _ in last:
                copy.wait_recv()
            planes.append(lane)
            if len(planes) == 3:
                for copy in done:
                    copy.wait_send()
                complete()

        plan.add(relay())

    def stages():
        yield clock.now
        swapped.wait()
        kept.wait()
        near = [go(i, 0, 0, 1, 0, 1, move.z_near, OVER_NEAR) for i in range(2)]
        far = [go(i, 0, 0, 1, 0, 2, move.z_far, OVER_FAR) for i in range(2)]
        plane(0, 1)
        yield near[1][1]
        for copy, _ in near:
            copy.wait_recv()
        far += [go(i, 0, 1, 1, 0, 3, move.z_far, OVER_FAR) for i in range(2)]
        plane(1, 1)
        onward()
        yield far[3][1]
        for copy, _ in far:
            copy.wait_recv()
        plane(2, 2)

    swapped = move.send(other, whole.at[own, pl.ds(0, units)], move.sibling)
    kept = move.keep(mine, whole.at[own, pl.ds(0, units)])
    return stages()


def vector_stages(move, clock, vectors, out):
    own = move.core * 4
    keep = move.keep(vectors, out.at[own])
    copy = move.send(vectors, out.at[own], move.sibling)
    yield clock.now + 2.0
    keep.wait()
    copy.wait()
    over_x = [move.send(out.at[i], out.at[j], move.x_side) for i, j in ((0, 1), (4, 6))]
    yield clock.now + 4.0
    for copy in over_x:
        copy.wait()
    over_y = [
        move.send(out.at[i], out.at[j], move.y_side) for i, j in ((0, 2), (1, 3), (4, 5), (6, 7))
    ]
    yield clock.now + 4.0
    for copy in over_y:
        copy.wait()


def hbm(count):
    return [pl.BlockSpec(memory_space=pl.ANY)] * count


def loop(count, body):
    def step(i, carry):
        body(i)
        return carry

    lax.fori_loop(0, count, step, 0)


def at(i, size):
    return pl.ds(pl.multiple_of(i * size, size), size)


def vector_row(vectors, index):
    return jnp.concatenate([vectors[spot, index : index + 1, :] for spot in range(8)], axis=1)


def segment_rows(move, own_ids, other_ids, seg_row, seg_col):
    own, other = own_ids[move.z_high], other_ids[move.z_high]
    ids = jnp.where(move.z_low == move.core, own, other).astype(float_type)
    half = ids.shape[1] // 2
    turned = jnp.concatenate([ids[:, half:], ids[:, :half]], axis=1)
    ids = jnp.where(move.core == 0, ids, turned)
    seg_row[...] = ids
    seg_col[...] = jnp.transpose(jnp.broadcast_to(ids, (128, 2 * half)))


def forward_steps(move, score_scale, layers, box):
    half = box["x"].shape[0]
    tile = 256
    vectors = box["vectors"]
    send, got = box["send"], box["got"]
    saves = {}

    def save(name, layer):
        source = box[name]
        copy = move.keep(source, box["saved"][layer][name])
        saves[name] = copy

    def before(*names):
        for name in names:
            if name in saves:
                saves.pop(name).wait()

    def norm(source, target, gain, shift):
        gain_row, shift_row = vector_row(vectors, gain), vector_row(vectors, shift)

        def body(i):
            rows = at(i, 64)
            target[rows, :] = (center_of(source[rows, :])[0] * gain_row + shift_row).astype(
                brain_type
            )

        loop(half // 64, body)
        return move.send(target.at[pl.ds(0, half)], target.at[pl.ds(half, half)], move.sibling)

    def partial_sums(left, weight, first):
        def body(i):
            columns = at(i, tile)
            send[:, columns] = nt(left[pl.ds(half, half), :], weight[columns, :]).astype(brain_type)

        loop(weight.shape[0] // tile, body)
        return move.send(send, got, move.sibling)

    def whole_sums(left, weight, base, target, copy):
        copy.wait()

        def body(i):
            columns = at(i, tile)
            target[:, columns] = (
                base[:, columns]
                + nt(left[pl.ds(0, half), :], weight[columns, :])
                + got[:, columns].astype(float_type)
            )

        loop(weight.shape[0] // tile, body)

    for layer in range(layers):
        x, mid, n1, n2 = box["x"], box["mid"], box["n1"], box["n2"]
        qkv, att, hid, slope = box["qkv"], box["att"], box["hid"], box["slope"]
        base = 4 * layer
        save("x", layer)
        before("n1", "qkv")
        sent = norm(x, n1, layer, layers + layer)
        box["need"](base)
        yield 2.0
        box["load"](base)

        def project(first):
            def body(i):
                columns = at(i, tile)
                rows = pl.ds(first * half, half)
                qkv[rows, columns] = nn(n1[rows, :], box["w0"][:, columns]).astype(brain_type)

            loop(qkv.shape[1] // tile, body)

        project(0)
        yield 3.0
        sent.wait()
        project(1)
        save("n1", layer)
        save("qkv", layer)
        before("att")
        yield 3.0
        for pair in range(qkv.shape[1] // 384):

            def body(part, pair=pair):
                rows = at(part, tile)
                low_lane = lax.broadcasted_iota(jnp.int32, (tile, 128), 1) < 64
                query = qkv[rows, pl.ds(pair * 384, 128)] * jnp.asarray(score_scale, brain_type)
                keys = qkv[:, pl.ds(pair * 384 + 128, 128)]
                values = qkv[:, pl.ds(pair * 384 + 256, 128)]
                same = box["seg_col"][rows, :1] == box["seg_row"][...]
                outs = []
                for head in range(2):
                    mine = low_lane if head == 0 else jnp.logical_not(low_lane)
                    scores = nt(jnp.where(mine, query, jnp.zeros_like(query)), keys)
                    scores = jnp.where(same, scores, -1e30)
                    weight = jnp.exp(scores - jnp.max(scores, axis=1, keepdims=True))
                    inverse = 1.0 / jnp.sum(weight, axis=1, keepdims=True)
                    outs.append(nn((weight * inverse).astype(brain_type), values))
                att[rows, pl.ds(pair * 128, 128)] = jnp.where(low_lane, outs[0], outs[1]).astype(
                    brain_type
                )

            loop(2 * half // tile, body)
            if pair == qkv.shape[1] // 384 - 1:
                box["need"](base + 1)
            yield 5.5
        box["load"](base + 1)
        sent = partial_sums(att, box["w1"], half)
        save("att", layer)
        yield 1.5
        before("mid", "n2")
        whole_sums(att, box["w1"], x, mid, sent)
        sent = norm(mid, n2, 2 * layers + layer, 3 * layers + layer)
        save("mid", layer)
        before("hid", "slope")
        box["need"](base + 2)
        yield 4.0
        box["load"](base + 2)
        for first in range(2):
            if first == 1:
                sent.wait()
                save("n2", layer)
            rows = pl.ds(first * half, half)
            count = hid.shape[1] // tile
            for part in range(2):

                def body(i, rows=rows, part=part):
                    columns = at(part * (count // 2) + i, tile)
                    pre = nn(n2[rows, :], box["w2"][:, columns])
                    cdf = 0.5 * (1.0 + lax.erf(pre * math.sqrt(0.5)))
                    density = jnp.exp(-0.5 * pre * pre) * (1.0 / math.sqrt(2.0 * math.pi))
                    hid[rows, columns] = (pre * cdf).astype(brain_type)
                    slope[rows, columns] = (cdf + pre * density).astype(brain_type)

                loop(count // 2, body)
                if first == 1 and part == 1:
                    box["need"](base + 3)
                yield 3.0
        save("slope", layer)
        box["load"](base + 3)
        before("n1", "qkv", "att", "n2")
        sent = partial_sums(hid, box["w3"], half)
        save("hid", layer)
        yield 3.5
        before("x")
        whole_sums(hid, box["w3"], mid, x, sent)
        yield 4.0
    low = box["low"]

    def body(i):
        rows = at(i, 64)
        low[rows, :] = x[rows, :].astype(brain_type)

    loop(half // 64, body)
    copy = move.keep(low, box["block"])
    before(*list(saves))
    copy.wait()


def forward_kernel(groups, layers, score_scale, *refs):
    refs = list(refs)

    def take(count):
        taken, refs[:count] = refs[:count], []
        return taken

    inputs, cotangent, vectors, ids = take(4)
    pieces = take(2 * groups)
    rows_out, grad_out, vectors_out, ids_out, block_out = take(5)
    wholes = take(groups)
    names = ("n1", "qkv", "att", "mid", "n2", "hid", "slope", "x")
    saved = [dict(zip(names, take(8))) for _ in range(layers)]
    box = dict(zip(names, take(8)))
    box["saved"], box["block"] = saved, block_out
    weights = take(4)
    for i in range(4):
        box[f"w{i}"] = weights[i]
    box["send"], box["got"], box["low"], box["vectors"] = take(4)
    own_ids, other_ids, box["seg_row"], box["seg_col"] = take(4)
    move = Mover(*refs)
    clock = Clock()
    plan = Plan(clock)
    move.greet()
    finish_rows = fetch_tokens(move, inputs, rows_out)
    clock.post(size_of(inputs), OVER_FAR)
    clock.now = 2.0
    loads, complete = {}, set()
    state = {"need": None, "begun": False, "loaded": -1, "used": 0}

    def prefetch():
        group = state["loaded"] + 1
        while group < groups and group in complete and (group < 4 or state["used"] > group - 4):
            loads[group] = move.keep(wholes[group], weights[group % 4])
            state["loaded"] = group
            group += 1

    def spread_next(group):
        if group < groups:
            plan.add(tasks[group])

    def completed(group):
        complete.add(group)
        prefetch()

    tasks = [
        spread_group(
            move,
            plan,
            pieces[2 * i],
            pieces[2 * i + 1],
            wholes[i],
            partial(spread_next, i + 1),
            partial(completed, i),
        )
        for i in range(groups)
    ]
    ids_copy = move.send(ids, other_ids, move.sibling)
    ids_here = move.keep(ids, own_ids)
    plan.add(vector_stages(move, clock, vectors, vectors_out))
    plan.add(tasks[0])

    def need(group):
        state["need"], state["used"] = group, group
        prefetch()

    def load(group):
        loads.pop(group).wait()
        state["need"] = None

    box["need"], box["load"] = need, load
    ends = []

    def prepare():
        yield 35.0
        ids_copy.wait()
        ids_here.wait()
        ends.append(move.keep(other_ids, ids_out).wait)
        segment_rows(move, own_ids, other_ids, box["seg_row"], box["seg_col"])
        finish_rows()
        copies = [move.keep(rows_out, box["low"]), move.keep(vectors_out, box["vectors"])]
        for copy in copies:
            copy.wait()

        def body(i):
            rows = at(i, 64)
            box["x"][rows, :] = box["low"][rows, :].astype(float_type)

        loop(box["x"].shape[0] // 64, body)
        state["begun"] = True
        yield 80.0
        ends.append(fetch_tokens(move, cotangent, grad_out))

    plan.add(prepare())

    def ready():
        return state["begun"] and (state["need"] is None or state["need"] in loads)

    plan.run(forward_steps(move, score_scale, layers, box), ready)
    for finish in ends:
        finish()


def forward_all(inputs, cotangent, vectors, ids, pieces, layers, score_scale):
    groups = len(pieces)
    tokens, width = 2 * inputs.shape[1], inputs.shape[2]
    units = [p.shape[1] for p, _ in pieces[:4]]
    flat = [block for piece in pieces for block in piece]
    remote = 27 * groups + 16 + 4 * layers
    kept = [
        ((2 * tokens, width), brain_type),
        ((2 * tokens, 4 * units[0]), brain_type),
        ((2 * tokens, 4 * units[1]), brain_type),
        ((tokens, width), float_type),
        ((2 * tokens, width), brain_type),
        ((2 * tokens, 4 * units[2]), brain_type),
        ((2 * tokens, 4 * units[2]), brain_type),
        ((tokens, width), float_type),
    ]
    outs = pl.pallas_call(
        partial(forward_kernel, groups, layers, score_scale),
        out_shape=[
            jax.ShapeDtypeStruct((tokens, width), inputs.dtype),
            jax.ShapeDtypeStruct((tokens, width), inputs.dtype),
            jax.ShapeDtypeStruct((8, *vectors.shape), vectors.dtype),
            jax.ShapeDtypeStruct(ids.shape, ids.dtype),
            jax.ShapeDtypeStruct((tokens, width), brain_type),
        ]
        + [jax.ShapeDtypeStruct((8 * p.shape[0], 4 * p.shape[1]), p.dtype) for p, _ in pieces]
        + [jax.ShapeDtypeStruct(*shape) for _ in range(layers) for shape in kept],
        in_specs=hbm(4 + 2 * groups),
        out_specs=hbm(5 + groups + 8 * layers),
        scratch_shapes=[pltpu.VMEM(*shape) for shape in kept]
        + [pltpu.VMEM((8 * p.shape[0], 4 * p.shape[1]), p.dtype) for p, _ in pieces[:4]]
        + [
            pltpu.VMEM((tokens, width), brain_type),
            pltpu.VMEM((tokens, width), brain_type),
            pltpu.VMEM((tokens, width), brain_type),
            pltpu.VMEM((8, *vectors.shape), vectors.dtype),
            pltpu.VMEM(ids.shape, ids.dtype),
            pltpu.VMEM(ids.shape, ids.dtype),
            pltpu.VMEM((1, 2 * tokens), float_type),
            pltpu.VMEM((2 * tokens, 128), float_type),
            pltpu.SemaphoreType.DMA((remote,)),
            pltpu.SemaphoreType.DMA((remote,)),
            pltpu.SemaphoreType.DMA((2 * groups + 10 + 8 * layers,)),
        ],
        compiler_params=pltpu.CompilerParams(
            collective_id=0, has_side_effects=True, vmem_limit_bytes=60 * 1024 * 1024
        ),
        name="forward",
    )(inputs, cotangent, vectors, ids, *flat)
    saved = [outs[5 + groups + 8 * i : 13 + groups + 8 * i] for i in range(layers)]
    return outs[1], outs[2], outs[3], outs[4], outs[5 : 5 + groups], saved


def collect_stages(move, clock, first, loaded, got, out, free, release):
    first_got, second_got, far_got, near_got = got
    rows, units = loaded.shape[1] // 2, loaded.shape[2] // 4
    sides = ((move.x_side, OVER_X), (move.y_side, OVER_Y))
    done = [copy for copy, _ in first]

    def go(source, target, device, links):
        copy = move.send(source, target, device)
        done.append(copy)
        return copy, clock.post(size_of(source), links)

    def total(target, source, height, width):
        def body(i):
            span = (at(i, 32), pl.ds(0, width))
            target[span] = (
                target[span].astype(float_type) + source[span].astype(float_type)
            ).astype(brain_type)

        loop(height // 32, body)

    second = []
    for i in range(2):
        yield first[i][1]
        first[i][0].wait_recv()
        total(loaded.at[i], first_got.at[i], 2 * rows, 4 * units)
        second.append(go(loaded.at[i, pl.ds(rows, rows)], second_got.at[i], *sides[i]))
    far = []
    free("far")
    for i in range(2):
        yield second[i][1]
        second[i][0].wait_recv()
        total(loaded.at[i], second_got.at[i], rows, 4 * units)
        far.append(
            go(
                loaded.at[i, pl.ds(0, rows), pl.ds(2 * units, 2 * units)],
                far_got.at[i],
                move.z_far,
                OVER_FAR,
            )
        )
    near = []
    free("near")
    for i in range(2):
        yield far[i][1]
        far[i][0].wait_recv()
        total(loaded.at[i], far_got.at[i], rows, 2 * units)
        near.append(
            go(
                loaded.at[i, pl.ds(0, rows), pl.ds(units, units)],
                near_got.at[i],
                move.z_near,
                OVER_NEAR,
            )
        )
    yield max(near[0][1], near[1][1])
    for i in range(2):
        near[i][0].wait_recv()
        total(loaded.at[i], near_got.at[i], rows, units)
    release()
    ready = pl.ds(0, rows), pl.ds(0, units)
    last, due = go(loaded.at[(1 - move.core, *ready)], out.at[1], move.sibling, OVER_CORE)
    stay = move.keep(loaded.at[(move.core, *ready)], out.at[0])
    yield due + 1.0
    last.wait_recv()
    stay.wait()
    for copy in done:
        copy.wait_send()


def vector_sum_stages(move, clock, vectors, sums, by_core, by_y, by_x, by_near, by_far, out):
    def go(source, target, device):
        return move.send(source, target, device), clock.now + 3.0

    copy, due = go(vectors.at[1 - move.core], by_core, move.sibling)
    yield due
    copy.wait()
    sums[...] = vectors[move.core] + by_core[...]
    copy, due = go(sums.at[pl.ds(2, 2)], by_y, move.y_side)
    yield due
    copy.wait()
    sums[:2] += by_y[...]
    copy, due = go(sums.at[1], by_x, move.x_side)
    yield due
    copy.wait()
    sums[0] += by_x[...]
    copy, due = go(sums.at[0], by_near, move.z_near)
    yield due
    copy.wait()
    sums[1] = sums[0] + by_near[...]
    copy, due = go(sums.at[1], by_far, move.z_far)
    yield due
    copy.wait()
    out[...] = sums[1] + by_far[...]


def backward_steps(move, plan, score_scale, layers, box, start_group):
    clock = plan.clock
    grad, below, source = box["grad"], box["below"], box["source"]
    branch, normed = box["branch"], box["normed"]
    upper, fc_in, hid, slope = box["upper"], box["fc_in"], box["hid"], box["slope"]
    send, got, sums = box["send"], box["got"], box["sums"]
    half = grad.shape[0]
    whole = 2 * half
    tile = 256
    qkv_width = box["layers"][0]["qkv"].shape[1]
    att_width = box["layers"][0]["att"].shape[1]
    wide = hid.shape[1]
    qkv_part, att_part = pl.ds(0, qkv_width), pl.ds(qkv_width, att_width)
    loads = {}

    def load(layer, name, target):
        loads[name] = move.keep(box["layers"][layer][name], target)

    def need(*names):
        for name in names:
            if name in loads:
                loads.pop(name).wait()

    def load_mlp(layer):
        load(layer, "hid", hid)
        load(layer, "w3", upper)
        load(layer, "slope", slope)

    def share_branch():
        def body(i):
            rows = at(i, 64)
            branch[rows, :] = grad[rows, :].astype(brain_type)

        loop(half // 64, body)
        return move.send(
            branch.at[pl.ds(0, half)], branch.at[pl.ds(half, half)], move.sibling
        )

    def weight_grads(kind, layer, left, right, first, width):
        group = start_group(kind, layer)
        step = width if width <= 1024 else width // 2
        for target, side, quarter, link in (
            ("sent", 0, 1, OVER_Y),
            ("sent", 1, 3, OVER_X),
            ("loaded", 0, 0, None),
            ("loaded", 1, 2, None),
        ):
            rows = left[:, pl.ds(quarter * 256, 256)]

            def body(i, target=target, side=side, rows=rows):
                part = right[:, pl.ds(pl.multiple_of(first + i * step, 128), step)]
                group[target][side, :, at(i, step)] = tn(rows, part).astype(brain_type)

            loop(width // step, body)
            if target == "sent":
                group["go"](side, link)
            yield 1.0 + width * 0.85e-3
        group["begin"]()

    def partial_sums(left, first, width, weight, at_column):
        def body(i):
            columns = at(i, tile)
            send[:, columns] = nt(
                left[pl.ds(half, half), pl.ds(first, width)],
                weight[columns, pl.ds(at_column, width)],
            ).astype(brain_type)

        loop(weight.shape[0] // tile, body)
        return move.send(send, got, move.sibling)

    def whole_sums(left, first, width, weight, at_column, copy):
        def product(i):
            columns = at(i, tile)
            below[:, columns] = nt(
                left[pl.ds(0, half), pl.ds(first, width)],
                weight[columns, pl.ds(at_column, width)],
            )

        loop(weight.shape[0] // tile, product)
        copy.wait()

    def norm_back(gain, grad_gain, grad_shift):
        gain_row = vector_row(box["vectors"], gain)
        sums[...] = jnp.zeros_like(sums)

        def body(i):
            rows = at(i, 64)
            unit, scale = center_of(source[rows, :])
            down = below[rows, :] + got[rows, :].astype(float_type)
            turn = down * gain_row
            grad[rows, :] += scale * (
                turn
                - jnp.mean(turn, axis=-1, keepdims=True)
                - unit * jnp.mean(turn * unit, axis=-1, keepdims=True)
            )
            sums[0:1, :] += jnp.sum(down * unit, axis=0, keepdims=True)
            sums[1:2, :] += jnp.sum(down, axis=0, keepdims=True)

        loop(half // 64, body)
        for row, index in ((0, grad_gain), (1, grad_shift)):
            for core in range(2):
                for spot in range(4):
                    to = spot if core == 0 else (0, 2, 1, 3)[spot]
                    box["vector_grads"][core, to, index : index + 1, :] = sums[
                        row : row + 1, pl.ds((core * 4 + spot) * 128, 128)
                    ]

    def slope_times(first):
        def body(i):
            rows, columns = pl.ds(first * half, half), at(i, tile)
            product = nn(branch[rows, :], upper[:, columns])
            slope[rows, columns] = (product * slope[rows, columns].astype(float_type)).astype(
                brain_type
            )

        loop(wide // tile, body)

    def attention(pair):
        keys_at, values_at = pl.ds(pair * 384 + 128, 128), pl.ds(pair * 384 + 256, 128)
        grad_keys, grad_values = box["grad_keys"], box["grad_values"]
        grad_keys[...] = jnp.zeros_like(grad_keys)
        grad_values[...] = jnp.zeros_like(grad_values)

        def body(part):
            rows = at(part, tile)
            low_lane = lax.broadcasted_iota(jnp.int32, (tile, 128), 1) < 64
            keys, values = hid[:, keys_at], hid[:, values_at]
            query = hid[rows, pl.ds(pair * 384, 128)]
            out_grad = slope[rows, pl.ds(qkv_width + pair * 128, 128)]
            same = box["seg_col"][:, :1] == box["seg_row"][:, rows]
            grad_queries = []
            for head in range(2):
                mine = low_lane if head == 0 else jnp.logical_not(low_lane)
                masked = jnp.where(mine, query, jnp.zeros_like(query))
                masked = masked * jnp.asarray(score_scale, brain_type)
                grad_masked = jnp.where(mine, out_grad, jnp.zeros_like(out_grad))
                scores = jnp.where(same, nt(keys, masked), -1e30)
                weight = jnp.exp(scores - jnp.max(scores, axis=0, keepdims=True))
                probs = weight * (1.0 / jnp.sum(weight, axis=0, keepdims=True))
                grad_probs = nt(values, grad_masked)
                inner = jnp.sum(probs * grad_probs, axis=0, keepdims=True)
                grad_raw = (probs * (grad_probs - inner)).astype(brain_type)
                grad_values[...] += nn(probs.astype(brain_type), grad_masked)
                grad_keys[...] += nn(grad_raw, masked)
                grad_queries.append(tn(grad_raw, keys))
            slope[rows, pl.ds(pair * 384, 128)] = (
                jnp.where(low_lane, grad_queries[0], grad_queries[1]) * score_scale
            ).astype(brain_type)

        loop(whole // tile, body)
        slope[:, keys_at] = grad_keys[...].astype(brain_type)
        slope[:, values_at] = grad_values[...].astype(brain_type)

    load_mlp(layers - 1)
    load(layers - 1, "n2", normed)
    load(layers - 1, "w2", fc_in)
    load(layers - 1, "mid", source)
    for layer in reversed(range(layers)):
        sent = share_branch()
        need("w3", "slope")
        yield 1.0
        slope_times(0)
        yield 4.0
        sent.wait()
        need("hid")
        yield from weight_grads(3, layer, branch, hid, 0, wide)
        load(layer, "qkv", hid.at[:, qkv_part])
        load(layer, "att", hid.at[:, att_part])
        slope_times(1)
        load(layer, "w0", upper.at[:, qkv_part])
        load(layer, "w1", upper.at[:, att_part])
        yield 4.0
        need("n2")
        yield from weight_grads(2, layer, normed, slope, 0, wide)
        load(layer, "n1", normed)
        need("w2")
        sent = partial_sums(slope, 0, wide, fc_in, 0)
        yield 3.5
        need("mid")
        whole_sums(slope, 0, wide, fc_in, 0, sent)
        if layer > 0:
            load(layer - 1, "w2", fc_in)
        yield 3.5
        norm_back(2 * layers + layer, 2 * layers + layer, 3 * layers + layer)
        load(layer, "x", source)
        sent = share_branch()
        need("w1")
        yield 5.0

        def grad_attended(first):
            rows = pl.ds(first * half, half)
            slope[rows, att_part] = nn(branch[rows, :], upper[:, att_part]).astype(brain_type)

        grad_attended(0)
        sent.wait()
        grad_attended(1)
        yield 2.0
        need("att")
        yield from weight_grads(1, layer, branch, hid, qkv_width, att_width)
        need("qkv")
        for pair in range(qkv_width // 384):
            attention(pair)
            yield 9.0
        need("n1")
        yield from weight_grads(0, layer, normed, slope, 0, qkv_width)
        if layer > 0:
            load(layer - 1, "n2", normed)
            load(layer - 1, "hid", hid)
        need("w0")
        sent = partial_sums(slope, 0, qkv_width, upper, 0)
        yield 3.0
        whole_sums(slope, 0, qkv_width, upper, 0, sent)
        if layer > 0:
            load(layer - 1, "w3", upper)
            load(layer - 1, "slope", slope)
        need("x")
        yield 3.0
        norm_back(layer, layer, layers + layer)
        if layer > 0:
            load(layer - 1, "mid", source)
        yield 4.0

    def body(i):
        rows = at(i, 64)
        send[rows, :] = grad[rows, :].astype(brain_type)

    loop(half // 64, body)


BACK_NAMES = ("n1", "qkv", "att", "mid", "n2", "hid", "slope", "x")


def backward_kernel(layers, score_scale, *refs):
    refs = list(refs)

    def take(count):
        taken, refs[:count] = refs[:count], []
        return taken

    kinds = 4
    groups = kinds * layers
    block, cotangent, vectors, ids, other_ids_in = take(5)
    weights = take(groups)
    saved = [dict(zip(BACK_NAMES, take(8))) for _ in range(layers)]
    for layer in range(layers):
        for kind in range(kinds):
            saved[layer][f"w{kind}"] = weights[kinds * layer + kind]
    block_out, below_out, vectors_out = take(3)
    outs = take(groups)
    box = {"layers": saved}
    names = ("upper", "fc_in", "hid", "slope", "normed", "branch", "source", "grad", "below")
    box.update(zip(names, take(9)))
    names = ("send", "got", "grad_keys", "grad_values", "seg_row", "seg_col", "vectors", "sums")
    box.update(zip(names, take(8)))
    own_ids, other_ids, box["vector_grads"] = take(3)
    small = take(6)
    buffers = [take(6) for _ in range(kinds)]
    (credits,) = take(1)
    move = Mover(*refs)
    clock = Clock()
    plan = Plan(clock)
    copies = [
        move.keep(cotangent, box["send"]),
        move.keep(vectors, box["vectors"]),
        move.keep(ids, own_ids),
        move.keep(other_ids_in, other_ids),
    ]
    move.greet()
    finish_above = return_tokens(move, block, block_out)
    for copy in copies:
        copy.wait()
    segment_rows(move, own_ids, other_ids, box["seg_row"], box["seg_col"])

    def body(i):
        rows = at(i, 64)
        box["grad"][rows, :] = box["send"][rows, :].astype(float_type)

    loop(box["grad"].shape[0] // 64, body)
    devices = {"x": move.x_side, "y": move.y_side, "far": move.z_far, "near": move.z_near}
    order = list(devices)
    running = {}

    def start_group(kind, layer):
        if kind in running:
            plan.finish(running.pop(kind))
        sent, loaded, *got = buffers[kind]
        first = [None, None]

        def free(name):
            if layer < layers - 1:
                pl.semaphore_wait(credits.at[kind * 4 + order.index(name)], 1)

        def release():
            if layer > 0:
                for i, name in enumerate(order):
                    pl.semaphore_signal(
                        credits.at[kind * 4 + i],
                        inc=1,
                        device_id=devices[name],
                        device_id_type=pl.DeviceIdType.MESH,
                    )

        def go(side, link):
            name = "y" if side == 0 else "x"
            free(name)
            copy = move.send(sent.at[side], got[0].at[side], devices[name])
            first[side] = (copy, clock.post(size_of(sent.at[side]), link))

        def begin():
            task = collect_stages(
                move, clock, first, loaded, got, outs[kinds * layer + kind], free, release
            )
            plan.add(task)
            running[kind] = task

        return {"sent": sent, "loaded": loaded, "go": go, "begin": begin}

    def compute():
        yield from backward_steps(move, plan, score_scale, layers, box, start_group)
        ends.append(return_tokens(move, box["send"], below_out))
        plan.add(vector_sum_stages(move, clock, box["vector_grads"], *small, vectors_out))

    ends = [finish_above]
    plan.run(compute(), lambda: True)
    for finish in ends:
        finish()


def backward_all(block, cotangent, vectors, ids, other_ids, weights, saved, layers, score_scale):
    tokens, width = cotangent.shape
    units = [w.shape[1] for w in weights[:4]]
    count = len(weights)
    low, high = brain_type, float_type
    small_vectors = (2, 4, vectors.shape[1], vectors.shape[2])
    scratch = [((2 * tokens, units[2]), low)] * 4
    scratch += [((2 * tokens, width), low)] * 2
    scratch += [((tokens, width), high)] * 3
    scratch += [((tokens, width), low)] * 2
    scratch += [((2 * tokens, 128), high)] * 2
    scratch += [((1, 2 * tokens), high), ((2 * tokens, 128), high)]
    scratch += [(vectors.shape, high), ((8, width), high)]
    scratch += [(ids.shape, ids.dtype)] * 2
    scratch += [(small_vectors, high), (small_vectors[1:], high), (small_vectors[1:], high)]
    scratch += [((2, *small_vectors[2:]), high)] + [(small_vectors[2:], high)] * 3
    for wide in units:
        for rows, columns in ((256, 1), (256, 1), (256, 1), (128, 1), (128, 2), (128, 4)):
            scratch.append(((2, rows, wide // columns), low))
    remote = 12 * count + 9 + 4 * layers + 8
    outs = pl.pallas_call(
        partial(backward_kernel, layers, score_scale),
        out_shape=[jax.ShapeDtypeStruct((2, tokens // 2, width), low)] * 2
        + [jax.ShapeDtypeStruct(vectors.shape[1:], high)]
        + [jax.ShapeDtypeStruct((2, 128, w.shape[1] // 4), low) for w in weights],
        in_specs=hbm(5 + count + 8 * layers),
        out_specs=hbm(2) + [pl.BlockSpec(memory_space=pltpu.VMEM)] + hbm(count),
        scratch_shapes=[pltpu.VMEM(*shape) for shape in scratch]
        + [
            pltpu.SemaphoreType.REGULAR((16,)),
            pltpu.SemaphoreType.DMA((remote,)),
            pltpu.SemaphoreType.DMA((remote,)),
            pltpu.SemaphoreType.DMA((8 + 14 * layers + count,)),
        ],
        compiler_params=pltpu.CompilerParams(
            collective_id=1, has_side_effects=True, vmem_limit_bytes=62 * 1024 * 1024
        ),
        name="backward",
    )(block, cotangent, vectors, ids, other_ids, *weights, *[a for kept in saved for a in kept])
    return outs[:2], outs[2], outs[3:]


def per_chip(
    inputs,
    segment_ids,
    norm1_gain,
    norm1_shift,
    w_query,
    w_key,
    w_value,
    w_output,
    norm2_gain,
    norm2_shift,
    w_fc_in,
    w_fc_out,
    cotangent,
):
    layers = norm1_gain.shape[0]
    head_width = inputs.shape[3] // HEADS
    score_scale = 1.0 / math.sqrt(head_width)
    core = lax.axis_index("dp") & 1

    def halves(columns):
        wide = columns.shape[1] // 2
        low, high = columns[:, :wide], columns[:, wide:]
        return pick(core, low, high), pick(core, high, low)

    pieces = []
    for layer in range(layers):
        both = [halves(w[layer]) for w in (w_query, w_key, w_value)]
        pieces += [
            tuple(jnp.concatenate([b[side] for b in both], axis=1) for side in range(2)),
            halves(w_output[layer].T),
            halves(w_fc_in[layer]),
            halves(w_fc_out[layer].T),
        ]
    vectors = jnp.concatenate([norm1_gain, norm1_shift, norm2_gain, norm2_shift], axis=0)
    grad, vectors, other_ids, block, weights, saved = forward_all(
        inputs[:, 0],
        cotangent[:, 0],
        vectors.astype(float_type),
        segment_ids,
        pieces,
        layers,
        score_scale,
    )
    tokens, vector_grads, outs = backward_all(
        block, grad, vectors, segment_ids, other_ids, weights, saved, layers, score_scale
    )
    block_output, input_grad = (part.astype(float_type) for part in tokens)
    outs = [(pick(core, out[0], out[1]), pick(core, out[1], out[0])) for out in outs]

    def joined(kind, columns=None):
        per_layer = []
        for layer in range(layers):
            low, high = outs[4 * layer + kind]
            if columns is not None:
                low, high = low[:, columns], high[:, columns]
            per_layer.append(jnp.concatenate([low, high], axis=1))
        return jnp.stack(per_layer)

    width = w_query.shape[2] // 2
    grad_query, grad_key, grad_value = (joined(0, slice(i * width, (i + 1) * width)) for i in range(3))
    grad_output = joined(1).transpose(0, 2, 1)
    grad_fc_in = joined(2)
    grad_fc_out = joined(3).transpose(0, 2, 1)

    gain_one, shift_one, gain_two, shift_two = (
        vector_grads[i * layers : (i + 1) * layers] for i in range(4)
    )
    return (
        block_output[:, None],
        input_grad[:, None],
        gain_one,
        shift_one,
        grad_query.astype(float_type),
        grad_key.astype(float_type),
        grad_value.astype(float_type),
        grad_output.astype(float_type),
        gain_two,
        shift_two,
        grad_fc_in.astype(float_type),
        grad_fc_out.astype(float_type),
    )


def layer_norm(token_rows, gain_vec, shift_vec):
    center = token_rows - jnp.mean(token_rows, axis=-1, keepdims=True)
    spread = jnp.mean(center * center, axis=-1, keepdims=True)
    return center * lax.rsqrt(spread + 1e-05) * gain_vec + shift_vec


def normed_local(token_rows, gain_vec, shift_vec):
    return layer_norm(token_rows, gain_vec.astype(float_type), shift_vec.astype(float_type)).astype(
        brain_type
    )


def normed_send(token_rows, gain_vec, shift_vec):
    return lax.all_gather(
        normed_local(token_rows, gain_vec, shift_vec), "tensor", axis=0, tiled=True
    )


def normed_resend(token_rows, gain_vec, shift_vec):
    return lax.all_gather(
        normed_local(token_rows, gain_vec, shift_vec), "tensor", axis=0, tiled=True
    )


def branch_total(partial_sum):
    return lax.psum_scatter(
        partial_sum.astype(jnp.bfloat16), "tensor", scatter_dimension=0, tiled=True
    ).astype(jnp.float32)


def branch_cotangent(grad_rows):
    return lax.all_gather(grad_rows.astype(brain_type), "tensor", axis=0, tiled=True)


def input_total(partial_sum):
    return lax.psum_scatter(
        partial_sum.astype(jnp.bfloat16), "tensor", scatter_dimension=0, tiled=True
    ).astype(jnp.float32)


def norm_backward(token_rows, gain_vec, shift_vec, grad_normed):
    _, norm_pull = jax.vjp(
        layer_norm, token_rows, gain_vec.astype(float_type), shift_vec.astype(float_type)
    )
    return norm_pull(grad_normed)


def masked_scores(query_part, segment_part, key_heads, segment, score_scale):
    raw_scores = jnp.einsum(
        "qhd,khd->hqk", query_part, key_heads, preferred_element_type=float_type
    )
    same_scene = segment_part[:, None] == segment[None, :]
    return jnp.where(same_scene[None], raw_scores * score_scale, -1e30)


def attend_forward(queries, key_heads, values, segment, block_rows):
    seq_len, head_count, head_width = queries.shape
    score_scale = 1.0 / math.sqrt(head_width)
    block_count = seq_len // block_rows

    def one_block(block_pair):
        query_part, segment_part = block_pair
        scores = masked_scores(query_part, segment_part, key_heads, segment, score_scale)
        row_max = jnp.max(scores, axis=-1, keepdims=True)
        exp_scores = jnp.exp(scores - row_max)
        row_total = jnp.sum(exp_scores, axis=-1, keepdims=True)
        probabilities = (exp_scores / row_total).astype(brain_type)
        block_out = jnp.einsum(
            "hqk,khd->qhd", probabilities, values, preferred_element_type=float_type
        )
        log_total = (row_max + jnp.log(row_total))[..., 0]
        return (block_out.astype(brain_type), log_total)

    query_blocks = queries.reshape(block_count, block_rows, head_count, head_width)
    segment_blocks = segment.reshape(block_count, block_rows)
    outputs, log_totals = lax.map(one_block, (query_blocks, segment_blocks))
    return (outputs.reshape(seq_len, head_count * head_width), log_totals)


def attend_backward(queries, key_heads, values, segment, log_totals, grad_out, block_rows):
    seq_len, head_count, head_width = queries.shape
    score_scale = 1.0 / math.sqrt(head_width)
    block_count = seq_len // block_rows

    def one_block(carry_pair, block_items):
        grad_keys, grad_values = carry_pair
        query_part, segment_part, log_part, grad_part = block_items
        scores = masked_scores(query_part, segment_part, key_heads, segment, score_scale)
        probabilities = jnp.exp(scores - log_part[..., None])
        grad_probs = jnp.einsum(
            "qhd,khd->hqk", grad_part, values, preferred_element_type=float_type
        )
        row_inner = jnp.sum(probabilities * grad_probs, axis=-1, keepdims=True)
        grad_raw = (probabilities * (grad_probs - row_inner) * score_scale).astype(brain_type)
        grad_query = jnp.einsum(
            "hqk,khd->qhd", grad_raw, key_heads, preferred_element_type=float_type
        )
        grad_keys = grad_keys + jnp.einsum(
            "hqk,qhd->khd", grad_raw, query_part, preferred_element_type=float_type
        )
        grad_values = grad_values + jnp.einsum(
            "hqk,qhd->khd",
            probabilities.astype(brain_type),
            grad_part,
            preferred_element_type=float_type,
        )
        return ((grad_keys, grad_values), grad_query.astype(brain_type))

    zero_heads = jnp.zeros((seq_len, head_count, head_width), float_type)
    block_items = (
        queries.reshape(block_count, block_rows, head_count, head_width),
        segment.reshape(block_count, block_rows),
        log_totals,
        grad_out.reshape(block_count, block_rows, head_count, head_width),
    )
    (grad_keys, grad_values), grad_queries = lax.scan(
        one_block, (zero_heads, zero_heads), block_items
    )
    flat_shape = (seq_len, head_count * head_width)
    return (
        grad_queries.reshape(flat_shape),
        grad_keys.astype(brain_type).reshape(flat_shape),
        grad_values.astype(brain_type).reshape(flat_shape),
    )


def fresh_totals(layers, attn_width, hidden_width):
    vector_zero = jnp.zeros((layers, D), float_type)
    column_zero = jnp.zeros((layers, D, attn_width), float_type)
    return [
        vector_zero,
        vector_zero,
        column_zero,
        column_zero,
        column_zero,
        jnp.zeros((layers, attn_width, D), float_type),
        vector_zero,
        vector_zero,
        jnp.zeros((layers, D, hidden_width), float_type),
        jnp.zeros((layers, hidden_width, D), float_type),
    ]


def add_into(grad_totals, position, layer_index, term):
    grad_totals[position] = grad_totals[position].at[layer_index].add(term)


def per_device(
    inputs,
    segment_ids,
    norm1_gain,
    norm1_shift,
    w_query,
    w_key,
    w_value,
    w_output,
    norm2_gain,
    norm2_shift,
    w_fc_in,
    w_fc_out,
    cotangent,
):
    micro_count = inputs.shape[0]
    layers = norm1_gain.shape[0]
    seq_len = segment_ids.shape[2]
    block_rows = min(512, seq_len)
    head_width = D // HEADS
    attn_width = w_query.shape[2]
    hidden_width = w_fc_in.shape[2]
    grad_totals = fresh_totals(layers, attn_width, hidden_width)
    reduced = None
    output_list = []
    input_grad_list = []
    for micro_index in range(micro_count):
        token_rows = inputs[micro_index, 0].astype(float_type)
        segment = segment_ids[micro_index, 0]
        saved_state = []
        for layer_index in range(layers):
            weights = (
                lax.all_gather(norm1_gain[layer_index], "dp", axis=0, tiled=True),
                lax.all_gather(norm1_shift[layer_index], "dp", axis=0, tiled=True),
                lax.all_gather(w_query[layer_index], "dp", axis=0, tiled=True),
                lax.all_gather(w_key[layer_index], "dp", axis=0, tiled=True),
                lax.all_gather(w_value[layer_index], "dp", axis=0, tiled=True),
                lax.all_gather(w_output[layer_index], "dp", axis=1, tiled=True),
                lax.all_gather(norm2_gain[layer_index], "dp", axis=0, tiled=True),
                lax.all_gather(norm2_shift[layer_index], "dp", axis=0, tiled=True),
                lax.all_gather(w_fc_in[layer_index], "dp", axis=0, tiled=True),
                lax.all_gather(w_fc_out[layer_index], "dp", axis=1, tiled=True),
            )
            (
                gain_one,
                shift_one,
                query_w,
                key_w,
                value_w,
                output_w,
                gain_two,
                shift_two,
                fc_in_w,
                fc_out_w,
            ) = weights
            whole_weights = None
            normed = normed_send(token_rows, gain_one, shift_one)
            queries = jnp.dot(normed, query_w, preferred_element_type=float_type).astype(brain_type)
            key_heads = jnp.dot(normed, key_w, preferred_element_type=float_type).astype(brain_type)
            values = jnp.dot(normed, value_w, preferred_element_type=float_type).astype(brain_type)
            attended, log_totals = attend_forward(
                queries.reshape(seq_len, -1, head_width),
                key_heads.reshape(seq_len, -1, head_width),
                values.reshape(seq_len, -1, head_width),
                segment,
                block_rows,
            )
            mid_rows = token_rows + branch_total(
                jnp.dot(attended, output_w, preferred_element_type=float_type)
            )
            normed_two = normed_send(mid_rows, gain_two, shift_two)
            pre_act = jnp.dot(normed_two, fc_in_w, preferred_element_type=float_type)
            hidden = jax.nn.gelu(pre_act, approximate=False).astype(brain_type)
            next_rows = mid_rows + branch_total(
                jnp.dot(hidden, fc_out_w, preferred_element_type=float_type)
            )
            saved_state.append(
                (
                    token_rows,
                    mid_rows,
                    weights,
                    normed,
                    normed_two,
                    queries,
                    key_heads,
                    values,
                    attended,
                    log_totals,
                    pre_act,
                    hidden,
                    whole_weights,
                )
            )
            token_rows = next_rows
        output_list.append(token_rows)
        grad_rows = cotangent[micro_index, 0].astype(float_type)
        for layer_index in reversed(range(layers)):
            (
                layer_rows,
                mid_rows,
                weights,
                normed,
                normed_two,
                queries,
                key_heads,
                values,
                attended,
                log_totals,
                pre_act,
                hidden,
                whole_weights,
            ) = saved_state[layer_index]
            weights = (
                lax.all_gather(norm1_gain[layer_index], "dp", axis=0, tiled=True),
                lax.all_gather(norm1_shift[layer_index], "dp", axis=0, tiled=True),
                lax.all_gather(w_query[layer_index], "dp", axis=0, tiled=True),
                lax.all_gather(w_key[layer_index], "dp", axis=0, tiled=True),
                lax.all_gather(w_value[layer_index], "dp", axis=0, tiled=True),
                lax.all_gather(w_output[layer_index], "dp", axis=1, tiled=True),
                lax.all_gather(norm2_gain[layer_index], "dp", axis=0, tiled=True),
                lax.all_gather(norm2_shift[layer_index], "dp", axis=0, tiled=True),
                lax.all_gather(w_fc_in[layer_index], "dp", axis=0, tiled=True),
                lax.all_gather(w_fc_out[layer_index], "dp", axis=1, tiled=True),
            )
            (
                gain_one,
                shift_one,
                query_w,
                key_w,
                value_w,
                output_w,
                gain_two,
                shift_two,
                fc_in_w,
                fc_out_w,
            ) = weights
            normed = normed_resend(layer_rows, gain_one, shift_one)
            normed_two = normed_resend(mid_rows, gain_two, shift_two)
            grad_branch = branch_cotangent(grad_rows)
            add_into(
                grad_totals,
                9,
                layer_index,
                jnp.einsum("sf,sd->fd", hidden, grad_branch, preferred_element_type=float_type),
            )
            grad_hidden = jnp.einsum(
                "sd,fd->sf", grad_branch, fc_out_w, preferred_element_type=float_type
            )
            _, gelu_pull = jax.vjp(partial(jax.nn.gelu, approximate=False), pre_act)
            grad_pre = gelu_pull(grad_hidden)[0].astype(brain_type)
            add_into(
                grad_totals,
                8,
                layer_index,
                jnp.einsum("sd,sf->df", normed_two, grad_pre, preferred_element_type=float_type),
            )
            grad_normed = input_total(
                jnp.einsum("sf,df->sd", grad_pre, fc_in_w, preferred_element_type=float_type)
            )
            grad_mid_part, grad_gain, grad_shift = norm_backward(
                mid_rows, gain_two, shift_two, grad_normed
            )
            add_into(grad_totals, 6, layer_index, grad_gain)
            add_into(grad_totals, 7, layer_index, grad_shift)
            grad_mid = grad_rows + grad_mid_part
            grad_branch = branch_cotangent(grad_mid)
            add_into(
                grad_totals,
                5,
                layer_index,
                jnp.einsum("sa,sd->ad", attended, grad_branch, preferred_element_type=float_type),
            )
            grad_attended = jnp.einsum(
                "sd,ad->sa", grad_branch, output_w, preferred_element_type=float_type
            ).astype(brain_type)
            grad_queries, grad_keys, grad_values = attend_backward(
                queries.reshape(seq_len, -1, head_width),
                key_heads.reshape(seq_len, -1, head_width),
                values.reshape(seq_len, -1, head_width),
                segment,
                log_totals,
                grad_attended.reshape(seq_len, -1, head_width),
                block_rows,
            )
            add_into(
                grad_totals,
                2,
                layer_index,
                jnp.einsum("sd,sa->da", normed, grad_queries, preferred_element_type=float_type),
            )
            add_into(
                grad_totals,
                3,
                layer_index,
                jnp.einsum("sd,sa->da", normed, grad_keys, preferred_element_type=float_type),
            )
            add_into(
                grad_totals,
                4,
                layer_index,
                jnp.einsum("sd,sa->da", normed, grad_values, preferred_element_type=float_type),
            )
            grad_input_part = jnp.einsum(
                "sa,da->sd", grad_queries, query_w, preferred_element_type=float_type
            )
            grad_input_part = grad_input_part + jnp.einsum(
                "sa,da->sd", grad_keys, key_w, preferred_element_type=float_type
            )
            grad_input_part = grad_input_part + jnp.einsum(
                "sa,da->sd", grad_values, value_w, preferred_element_type=float_type
            )
            grad_normed = input_total(grad_input_part)
            grad_below, grad_gain, grad_shift = norm_backward(
                layer_rows, gain_one, shift_one, grad_normed
            )
            add_into(grad_totals, 0, layer_index, grad_gain)
            add_into(grad_totals, 1, layer_index, grad_shift)
            grad_rows = grad_mid + grad_below
        input_grad_list.append(grad_rows)
    reduced = (
        lax.psum_scatter(
            grad_totals[0].astype(jnp.bfloat16), "dp", scatter_dimension=1, tiled=True
        ).astype(jnp.float32),
        lax.psum_scatter(
            grad_totals[1].astype(jnp.bfloat16), "dp", scatter_dimension=1, tiled=True
        ).astype(jnp.float32),
        lax.psum_scatter(
            grad_totals[2].astype(jnp.bfloat16), "dp", scatter_dimension=1, tiled=True
        ).astype(jnp.float32),
        lax.psum_scatter(
            grad_totals[3].astype(jnp.bfloat16), "dp", scatter_dimension=1, tiled=True
        ).astype(jnp.float32),
        lax.psum_scatter(
            grad_totals[4].astype(jnp.bfloat16), "dp", scatter_dimension=1, tiled=True
        ).astype(jnp.float32),
        lax.psum_scatter(
            grad_totals[5].astype(jnp.bfloat16), "dp", scatter_dimension=2, tiled=True
        ).astype(jnp.float32),
        lax.psum_scatter(
            grad_totals[6].astype(jnp.bfloat16), "dp", scatter_dimension=1, tiled=True
        ).astype(jnp.float32),
        lax.psum_scatter(
            grad_totals[7].astype(jnp.bfloat16), "dp", scatter_dimension=1, tiled=True
        ).astype(jnp.float32),
        lax.psum_scatter(
            grad_totals[8].astype(jnp.bfloat16), "dp", scatter_dimension=1, tiled=True
        ).astype(jnp.float32),
        lax.psum_scatter(
            grad_totals[9].astype(jnp.bfloat16), "dp", scatter_dimension=2, tiled=True
        ).astype(jnp.float32),
    )
    norm_sums = lax.psum((reduced[0], reduced[1], reduced[6], reduced[7]), "tensor")
    block_output = jnp.stack(output_list)[:, None]
    input_grad = jnp.stack(input_grad_list)[:, None]
    return (
        block_output,
        input_grad,
        norm_sums[0],
        norm_sums[1],
        reduced[2],
        reduced[3],
        reduced[4],
        reduced[5],
        norm_sums[2],
        norm_sums[3],
        reduced[8],
        reduced[9],
    )


def solution(mesh):
    placed = (
        P(None, "dp", "tensor", None),
        P(None, "dp", None),
        P(None, "dp"),
        P(None, "dp"),
        P(None, "dp", "tensor"),
        P(None, "dp", "tensor"),
        P(None, "dp", "tensor"),
        P(None, "tensor", "dp"),
        P(None, "dp"),
        P(None, "dp"),
        P(None, "dp", "tensor"),
        P(None, "tensor", "dp"),
        P(None, "dp", "tensor", None),
    )
    line, plane = mesh.shape["tensor"], mesh.shape["dp"]
    fits = line == 4 and plane == 8 and 2 * line == plane
    return jax.shard_map(
        per_chip if fits else per_device,
        mesh=mesh,
        in_specs=placed,
        out_specs=(
            P(None, "dp", "tensor", None),
            P(None, "dp", "tensor", None),
            P(None, "dp"),
            P(None, "dp"),
            P(None, "dp", "tensor"),
            P(None, "dp", "tensor"),
            P(None, "dp", "tensor"),
            P(None, "tensor", "dp"),
            P(None, "dp"),
            P(None, "dp"),
            P(None, "dp", "tensor"),
            P(None, "tensor", "dp"),
        ),
        check_vma=False,
    )
```

```python
from functools import partial
import math

import jax
import jax.numpy as jnp
from jax import lax
from jax.experimental import pallas as pl
from jax.experimental.pallas import tpu as pltpu
from jax.sharding import PartitionSpec as P

D = 1024
HEADS = 16
float_type = jnp.float32
brain_type = jnp.bfloat16


def nt(left, right):
    return lax.dot_general(left, right, (((1,), (1,)), ((), ())), preferred_element_type=float_type)


def nn(left, right):
    return lax.dot_general(left, right, (((1,), (0,)), ((), ())), preferred_element_type=float_type)


def tn(left, right):
    return lax.dot_general(left, right, (((0,), (0,)), ((), ())), preferred_element_type=float_type)


def center_of(rows):
    center = rows - jnp.mean(rows, axis=-1, keepdims=True)
    scale = lax.rsqrt(jnp.mean(center * center, axis=-1, keepdims=True) + 1e-05)
    return center * scale, scale


class Mover:
    def __init__(self, send_sems, recv_sems, local_sems):
        self.send_sems, self.recv_sems, self.local_sems = send_sems, recv_sems, local_sems
        self.remote, self.local = 0, 0
        self.place = lax.axis_index("dp")
        self.height = lax.axis_index("tensor")
        self.core = lax.rem(self.place, 2)
        self.x_bit = lax.rem(self.place // 2, 2)
        self.y_bit = lax.rem(self.place // 4, 2)
        self.z_low = lax.rem(self.height, 2)
        self.z_high = self.height // 2
        self.sibling = {"dp": self.place + 1 - 2 * self.core}
        self.x_side = {"dp": self.place + 2 - 4 * self.x_bit}
        self.y_side = {"dp": self.place + 4 - 8 * self.y_bit}
        self.z_near = {"tensor": self.height + 1 - 2 * self.z_low}
        self.z_across = {"tensor": 3 - self.height}
        self.inner = self.z_low != self.z_high
        self.outer = jnp.logical_not(self.inner)

    def make(self, source, target, device, send_index, recv_index):
        return pltpu.make_async_remote_copy(
            src_ref=source,
            dst_ref=target,
            send_sem=self.send_sems.at[send_index],
            recv_sem=self.recv_sems.at[recv_index],
            device_id=device,
            device_id_type=pl.DeviceIdType.MESH,
        )

    def send(self, source, target, device):
        copy = self.make(source, target, device, self.remote, self.remote)
        self.remote += 1
        copy.start()
        return copy

    def keep(self, source, target):
        copy = pltpu.make_async_copy(source, target, self.local_sems.at[self.local])
        self.local += 1
        copy.start()
        return copy

    def greet(self):
        barrier = pltpu.get_barrier_semaphore()
        plane = self.place - self.core
        devices = [self.x_side, self.y_side]
        for step in range(1, 8):
            other = lax.rem(self.core * 4 + self.height + step, 8)
            devices.append({"dp": plane + other // 4, "tensor": lax.rem(other, 4)})
        for device in devices:
            pl.semaphore_signal(
                barrier, inc=1, device_id=device, device_id_type=pl.DeviceIdType.MESH
            )
        pl.semaphore_wait(barrier, len(devices))

    def column(self, y, x, half):
        y_off = lax.rem(y + self.y_bit, 2)
        x_off = lax.rem(x + self.x_bit, 2)
        spot = 2 * y_off + x_off if half == 0 else y_off + 2 * x_off
        return pl.multiple_of((half * 4 + spot) * 128, 128)


BLOCKS = [(y, x, half) for y in range(2) for x in range(2) for half in range(2)]


def move_tokens(move, ways, origins):
    base, local = move.remote, move.local
    move.remote += 2
    move.local += 2
    closing = []
    for i, (to_core, to_z, copies, whole, slot) in enumerate(ways):
        stays = jnp.logical_and(to_core == move.core, to_z == move.height)
        device = {"dp": move.place - move.core + to_core, "tensor": to_z}

        @pl.when(stays)
        def _():
            for source, target in copies:
                pltpu.make_async_copy(source, target, move.local_sems.at[local + i]).start()

        @pl.when(jnp.logical_not(stays))
        def _():
            for source, target in copies:
                move.make(source, target, device, base + i, base + slot).start()

        closing.append((stays, device, whole, i))

    def finish():
        for stays, device, (source, target), i in closing:
            @pl.when(stays)
            def _():
                pltpu.make_async_copy(source, target, move.local_sems.at[local + i]).wait()

            @pl.when(jnp.logical_not(stays))
            def _():
                move.make(source, target, device, base + i, base + i).wait_send()

        for slot, (from_core, from_z, (source, target)) in enumerate(origins):
            comes = jnp.logical_not(
                jnp.logical_and(from_core == move.core, from_z == move.height)
            )

            @pl.when(comes)
            def _():
                move.make(source, target, move.sibling, base + slot, base + slot).wait_recv()

    return finish


def fetch_tokens(move, source, target):
    rows = source.shape[1]
    here = pl.ds(pl.multiple_of(move.z_low * rows, rows), rows)
    ways, origins = [], []
    for micro in range(2):
        copies = [
            (
                source.at[micro, :, pl.ds(i * 128, 128)],
                target.at[here, pl.ds(move.column(*block), 128)],
            )
            for i, block in enumerate(BLOCKS)
        ]
        whole = (source.at[micro], target.at[here])
        ways.append((move.z_high, 2 * micro + move.core, copies, whole, move.z_low))
    for slot in range(2):
        whole = (source.at[slot], target.at[pl.ds(slot * rows, rows)])
        origins.append((move.z_low, 2 * move.core + slot, whole))
    return move_tokens(move, ways, origins)


def return_tokens(move, source, target):
    rows = target.shape[1]
    ways, origins = [], []
    for slot in range(2):
        copies = [
            (
                source.at[pl.ds(slot * rows, rows), pl.ds(move.column(*block), 128)],
                target.at[move.z_high, :, pl.ds(i * 128, 128)],
            )
            for i, block in enumerate(BLOCKS)
        ]
        whole = (source.at[pl.ds(slot * rows, rows)], target.at[move.z_high])
        ways.append((move.z_low, 2 * move.core + slot, copies, whole, move.z_high))
    for micro in range(2):
        whole = (source.at[pl.ds(micro * rows, rows)], target.at[micro])
        origins.append((move.z_high, 2 * micro + move.core, whole))
    return move_tokens(move, ways, origins)


class Clock:
    def __init__(self, latency):
        self.now = 0.0
        self.latency = latency
        self.free = {}

    def post(self, size, links):
        start, end = self.now, self.now
        for link, share in links:
            begin = max(self.free.get(link, 0.0), self.now)
            self.free[link] = begin + share * size * PER_BYTE
            end = max(end, self.free[link])
        return end + self.latency


PER_BYTE = 2.0 / 84e3
LATENCY, SLACK = 2.0, 6.0
BACKLOG = 4.0
Z_BACKLOG = 8.0
TOKENS_AT = 8.0
OVER_X, OVER_Y = (("x", 1.0),), (("y", 1.0),)
OVER_NEAR, OVER_MID = (("z_out", 1.0),), (("z_mid", 1.0),)
OVER_CORE = (("core", 0.1),)


class Plan:
    def __init__(self, clock):
        self.clock, self.tasks = clock, []

    def add(self, task):
        due = next(task, None)
        if due is not None:
            self.tasks.append((due, task))

    def step(self):
        index = min(range(len(self.tasks)), key=lambda i: self.tasks[i][0])
        due, task = self.tasks.pop(index)
        self.clock.now = max(self.clock.now, due)
        self.add(task)

    def due(self):
        return min((due for due, _ in self.tasks), default=float("inf"))

    def finish(self, task):
        while any(task is other for _, other in self.tasks):
            self.step()

    def run(self, compute, ready):
        over = False
        while self.tasks or not over:
            if self.due() <= self.clock.now:
                self.step()
            elif not over and ready():
                cost = next(compute, None)
                if cost is None:
                    over = True
                else:
                    self.clock.now += cost
            elif self.tasks:
                self.step()


def size_of(ref):
    return math.prod(ref.shape) * jnp.dtype(ref.dtype).itemsize


def spread_group(move, plan, pieces, whole, rank, plane_first, onward, complete):
    clock = plan.clock
    rows = whole.shape[0] // 8
    units = whole.shape[1] // 4
    half = whole.shape[0] // 2
    own = pl.ds(pl.multiple_of(move.core * half, half), rows)
    done, planes, swapped, kept = [], [], [], []

    def part(first, spot, lane, lanes):
        return whole.at[pl.ds(first * half + spot * rows, rows), pl.ds(lane * units, lanes * units)]

    def go(first, spot, lane, lanes, to_spot, to_lane, device, links):
        source = part(first, spot, lane, lanes)
        copy = move.send(source, part(first, to_spot, to_lane, lanes), device)
        done.append(copy)
        return copy, clock.post(size_of(source), links)

    x_way, y_way = (move.x_side, OVER_X), (move.y_side, OVER_Y)

    def backlog(*links):
        return max(clock.free.get(link, 0.0) for link in links) - clock.now

    def plane(lane, lanes, arrived):
        def relay():
            while backlog("x", "y") > BACKLOG:
                yield clock.now + backlog("x", "y") - BACKLOG + 0.01 * rank
            one = go(0, 0, lane, lanes, 1, lane, *x_way)
            two = go(1, 0, lane, lanes, 1, lane, *y_way)
            last = [go(0, 0, lane, lanes, 2, lane, *y_way), go(1, 0, lane, lanes, 2, lane, *x_way)]
            yield one[1]
            one[0].wait_recv()
            last.append(go(0, 1, lane, lanes, 3, lane, *y_way))
            yield two[1]
            two[0].wait_recv()
            last.append(go(1, 1, lane, lanes, 3, lane, *x_way))
            yield max(due for _, due in last)
            for copy, _ in last:
                copy.wait_recv()
            planes.append(lane)
            arrived()

        plan.add(relay())

    def line(block, parts, after_near):
        size = parts * size_of(block(0, 0))
        base = move.remote
        move.remote += 4 * parts

        def cross(i, lane, to_lane):
            index = base + 4 * i + (0 if lane == 0 else 1)
            return move.make(block(i, lane), block(i, to_lane), move.z_across, index, index)

        def hand_on(i, lane, to_lane):
            index = base + 4 * i
            to_index = index + (0 if to_lane == 3 else 1)
            return move.make(block(i, lane), block(i, to_lane), move.z_near, index + lane, to_index)

        def sent_across(lane, to_lane):
            @pl.when(move.inner)
            def _():
                for i in range(parts):
                    cross(i, lane, to_lane).start()

            return clock.post(size, OVER_MID)

        def handed(lane, to_lane):
            @pl.when(move.inner)
            def _():
                for i in range(parts):
                    cross(i, 0 if lane == 3 else 1, lane).wait_recv()
                    hand_on(i, lane, to_lane).start()

            return clock.post(size, OVER_NEAR)

        near = []
        for i in range(parts):
            near.append(move.send(block(i, 0), block(i, 1), move.z_near))
        done.extend(near)
        near_due = clock.post(size, OVER_NEAR)
        first_due = sent_across(0, 3)
        if not plane_first:
            plane(0, 1, arrived)
            onward()
        yield near_due
        for copy in near:
            copy.wait_recv()
        second_due = sent_across(1, 2)
        after_near()
        yield first_due
        handed(3, 2)
        yield second_due
        last_due = handed(2, 3)
        yield last_due

        @pl.when(move.outer)
        def _():
            for i in range(parts):
                hand_on(i, 3, 2).wait_recv()
                hand_on(i, 2, 3).wait_recv()

        @pl.when(move.inner)
        def _():
            for i in range(parts):
                cross(i, 0, 3).wait_send()
                cross(i, 1, 2).wait_send()
                hand_on(i, 3, 2).wait_send()
                hand_on(i, 2, 3).wait_send()

    def finish():
        for copy in done:
            copy.wait_send()
        complete()

    def arrived():
        if len(planes) == 3:
            finish()

    def start():
        yield clock.now
        while backlog("z_mid", "z_out") > Z_BACKLOG:
            yield clock.now + backlog("z_mid", "z_out") - Z_BACKLOG
        for copy in swapped + kept:
            copy.wait()

    def over_line_first():
        yield from start()

        def after_near():
            plane(1, 1, arrived)

        yield from line(lambda i, lane: part(i, 0, lane, 1), 2, after_near)
        plane(2, 2, arrived)

    def over_plane_first():
        yield from start()

        def along():
            yield clock.now
            yield from line(
                lambda i, lane: whole.at[pl.ds(0, 2 * half), pl.ds(lane * units, units)],
                1,
                lambda: None,
            )
            finish()

        plane(0, 1, lambda: plan.add(along()))
        onward()

    at_column = 0
    for mine, other in pieces:
        width = mine.shape[1]
        target = whole.at[own, pl.ds(at_column, width)]
        swapped.append(move.send(other, target, move.sibling))
        kept.append(move.keep(mine, target))
        at_column += width
    return over_plane_first() if plane_first else over_line_first()


def vector_stages(move, clock, vectors, out):
    own = move.core * 4
    keep = move.keep(vectors, out.at[own])
    copy = move.send(vectors, out.at[own], move.sibling)
    yield clock.now + 2.0
    keep.wait()
    copy.wait()
    over_x = [move.send(out.at[i], out.at[j], move.x_side) for i, j in ((0, 1), (4, 6))]
    yield clock.now + 4.0
    for copy in over_x:
        copy.wait()
    over_y = [
        move.send(out.at[i], out.at[j], move.y_side) for i, j in ((0, 2), (1, 3), (4, 5), (6, 7))
    ]
    yield clock.now + 4.0
    for copy in over_y:
        copy.wait()


def hbm(count):
    return [pl.BlockSpec(memory_space=pl.ANY)] * count


def loop(count, body):
    def step(i, carry):
        body(i)
        return carry

    lax.fori_loop(0, count, step, 0)


def at(i, size):
    return pl.ds(pl.multiple_of(i * size, size), size)


def vector_row(vectors, index):
    return jnp.concatenate([vectors[spot, index : index + 1, :] for spot in range(8)], axis=1)


def segment_rows(move, own_ids, other_ids, seg_row, seg_col):
    own, other = own_ids[move.z_high], other_ids[move.z_high]
    ids = jnp.where(move.z_low == move.core, own, other).astype(float_type)
    half = ids.shape[1] // 2
    turned = jnp.concatenate([ids[:, half:], ids[:, :half]], axis=1)
    ids = jnp.where(move.core == 0, ids, turned)
    seg_row[...] = ids
    seg_col[...] = jnp.transpose(jnp.broadcast_to(ids, (128, 2 * half)))


def forward_steps(move, score_scale, layers, box):
    half = box["x"].shape[0]
    tile = 256
    vectors = box["vectors"]
    send, got = box["send"], box["got"]
    saves = {}

    def save(name, layer):
        source = box[name]
        copy = move.keep(source, box["saved"][layer][name])
        saves[name] = copy

    def before(*names):
        for name in names:
            if name in saves:
                saves.pop(name).wait()

    def norm(source, target, gain, shift):
        gain_row, shift_row = vector_row(vectors, gain), vector_row(vectors, shift)

        def body(i):
            rows = at(i, 64)
            target[rows, :] = (center_of(source[rows, :])[0] * gain_row + shift_row).astype(
                brain_type
            )

        loop(half // 64, body)
        return move.send(target.at[pl.ds(0, half)], target.at[pl.ds(half, half)], move.sibling)

    def partial_sums(left, weight, first):
        def body(i):
            columns = at(i, tile)
            send[:, columns] = nt(left[pl.ds(half, half), :], weight[columns, :]).astype(brain_type)

        loop(weight.shape[0] // tile, body)
        return move.send(send, got, move.sibling)

    def whole_sums(left, weight, base, target, copy):
        copy.wait()

        def body(i):
            columns = at(i, tile)
            target[:, columns] = (
                base[:, columns]
                + nt(left[pl.ds(0, half), :], weight[columns, :])
                + got[:, columns].astype(float_type)
            )

        loop(weight.shape[0] // tile, body)

    for layer in range(layers):
        x, mid, n1, n2 = box["x"], box["mid"], box["n1"], box["n2"]
        qkv, att, hid, slope = box["qkv"], box["att"], box["hid"], box["slope"]
        base = 4 * layer
        save("x", layer)
        before("n1", "qkv")
        sent = norm(x, n1, layer, layers + layer)
        box["need"](base)
        yield 2.0
        box["load"](base)

        def project(first):
            def body(i):
                columns = at(i, tile)
                rows = pl.ds(first * half, half)
                qkv[rows, columns] = nn(n1[rows, :], box["w0"][:, columns]).astype(brain_type)

            loop(qkv.shape[1] // tile, body)

        project(0)
        yield 3.0
        sent.wait()
        project(1)
        save("n1", layer)
        save("qkv", layer)
        before("att")
        yield 3.0
        for pair in range(qkv.shape[1] // 384):

            def body(part, pair=pair):
                rows = at(part, tile)
                low_lane = lax.broadcasted_iota(jnp.int32, (tile, 128), 1) < 64
                query = qkv[rows, pl.ds(pair * 384, 128)] * jnp.asarray(score_scale, brain_type)
                keys = qkv[:, pl.ds(pair * 384 + 128, 128)]
                values = qkv[:, pl.ds(pair * 384 + 256, 128)]
                same = box["seg_col"][rows, :1] == box["seg_row"][...]
                outs = []
                for head in range(2):
                    mine = low_lane if head == 0 else jnp.logical_not(low_lane)
                    scores = nt(jnp.where(mine, query, jnp.zeros_like(query)), keys)
                    scores = jnp.where(same, scores, -1e30)
                    weight = jnp.exp(scores - jnp.max(scores, axis=1, keepdims=True))
                    inverse = 1.0 / jnp.sum(weight, axis=1, keepdims=True)
                    outs.append(nn((weight * inverse).astype(brain_type), values))
                att[rows, pl.ds(pair * 128, 128)] = jnp.where(low_lane, outs[0], outs[1]).astype(
                    brain_type
                )

            loop(2 * half // tile, body)
            if pair == qkv.shape[1] // 384 - 1:
                box["need"](base + 1)
            yield 5.5
        box["load"](base + 1)
        sent = partial_sums(att, box["w1"], half)
        save("att", layer)
        yield 1.5
        before("mid", "n2")
        whole_sums(att, box["w1"], x, mid, sent)
        sent = norm(mid, n2, 2 * layers + layer, 3 * layers + layer)
        save("mid", layer)
        before("hid", "slope")
        box["need"](base + 2)
        yield 4.0
        box["load"](base + 2)
        for first in range(2):
            if first == 1:
                sent.wait()
                save("n2", layer)
            rows = pl.ds(first * half, half)
            count = hid.shape[1] // tile
            for part in range(2):

                def body(i, rows=rows, part=part):
                    columns = at(part * (count // 2) + i, tile)
                    pre = nn(n2[rows, :], box["w2"][:, columns])
                    cdf = 0.5 * (1.0 + lax.erf(pre * math.sqrt(0.5)))
                    density = jnp.exp(-0.5 * pre * pre) * (1.0 / math.sqrt(2.0 * math.pi))
                    hid[rows, columns] = (pre * cdf).astype(brain_type)
                    slope[rows, columns] = (cdf + pre * density).astype(brain_type)

                loop(count // 2, body)
                if first == 1 and part == 1:
                    box["need"](base + 3)
                yield 3.0
        save("slope", layer)
        box["load"](base + 3)
        before("n1", "qkv", "att", "n2")
        sent = partial_sums(hid, box["w3"], half)
        save("hid", layer)
        yield 3.5
        before("x")
        whole_sums(hid, box["w3"], mid, x, sent)
        yield 4.0
    low = box["low"]

    def body(i):
        rows = at(i, 64)
        low[rows, :] = x[rows, :].astype(brain_type)

    loop(half // 64, body)
    copy = move.keep(low, box["block"])
    before(*list(saves))
    copy.wait()


def forward_kernel(groups, layers, score_scale, *refs):
    refs = list(refs)

    def take(count):
        taken, refs[:count] = refs[:count], []
        return taken

    inputs, cotangent, vectors, ids = take(4)
    raw = take(6)
    rows_out, grad_out, vectors_out, ids_out, block_out = take(5)
    wholes = take(groups)
    names = ("n1", "qkv", "att", "mid", "n2", "hid", "slope", "x")
    saved = [dict(zip(names, take(8))) for _ in range(layers)]
    box = dict(zip(names, take(8)))
    box["saved"], box["block"] = saved, block_out
    weights = take(4)
    for i in range(4):
        box[f"w{i}"] = weights[i]
    box["send"], box["got"], box["low"], box["vectors"] = take(4)
    own_ids, other_ids, box["seg_row"], box["seg_col"] = take(4)
    move = Mover(*refs)
    clock = Clock(LATENCY)
    plan = Plan(clock)
    move.greet()
    clock.now = 2.0
    loads, complete = {}, set()
    state = {"need": None, "begun": False, "loaded": -1, "used": 0}

    def prefetch():
        group = state["loaded"] + 1
        while group < groups and group in complete and (group < 4 or state["used"] > group - 4):
            loads[group] = move.keep(wholes[group], weights[group % 4])
            state["loaded"] = group
            group += 1

    def spread_next(group):
        if group < groups:
            plan.add(tasks[group])

    def completed(group):
        complete.add(group)
        prefetch()

    def halves(ref, layer):
        wide = ref.shape[2] // 2
        return tuple(
            ref.at[layer, :, pl.ds(pl.multiple_of(side * wide, 128), wide)]
            for side in (move.core, 1 - move.core)
        )

    kinds = (raw[:3], raw[3:4], raw[4:5], raw[5:6])
    tasks = [
        spread_group(
            move,
            plan,
            [halves(ref, i // 4) for ref in kinds[i % 4]],
            wholes[i],
            i,
            i % 4 == 1,
            partial(spread_next, i + 1),
            partial(completed, i),
        )
        for i in range(groups)
    ]
    ids_copy = move.send(ids, other_ids, move.sibling)
    ids_here = move.keep(ids, own_ids)
    plan.add(vector_stages(move, clock, vectors, vectors_out))
    plan.add(tasks[0])

    def need(group):
        state["need"], state["used"] = group, group
        prefetch()

    def load(group):
        loads.pop(group).wait()
        state["need"] = None

    box["need"], box["load"] = need, load
    ends = []

    def prepare():
        yield TOKENS_AT
        finish_rows = fetch_tokens(move, inputs, rows_out)
        clock.post(size_of(inputs), OVER_MID)
        yield TOKENS_AT + 33.0
        ids_copy.wait()
        ids_here.wait()
        ends.append(move.keep(other_ids, ids_out).wait)
        segment_rows(move, own_ids, other_ids, box["seg_row"], box["seg_col"])
        finish_rows()
        copies = [move.keep(rows_out, box["low"]), move.keep(vectors_out, box["vectors"])]
        for copy in copies:
            copy.wait()

        def body(i):
            rows = at(i, 64)
            box["x"][rows, :] = box["low"][rows, :].astype(float_type)

        loop(box["x"].shape[0] // 64, body)
        state["begun"] = True
        yield 100.0
        clock.post(size_of(inputs), OVER_MID)
        ends.append(fetch_tokens(move, cotangent, grad_out))

    plan.add(prepare())

    def ready():
        return state["begun"] and (state["need"] is None or state["need"] in loads)

    plan.run(forward_steps(move, score_scale, layers, box), ready)
    for finish in ends:
        finish()


def forward_all(inputs, cotangent, vectors, ids, raw, layers, score_scale):
    groups = 4 * layers
    tokens, width = 2 * inputs.shape[1], inputs.shape[2]
    units = [w.shape[2] // 2 for w in raw]
    units = [sum(units[:3])] + units[3:]
    remote = 33 * groups + 16 + 4 * layers
    kept = [
        ((2 * tokens, width), brain_type),
        ((2 * tokens, 4 * units[0]), brain_type),
        ((2 * tokens, 4 * units[1]), brain_type),
        ((tokens, width), float_type),
        ((2 * tokens, width), brain_type),
        ((2 * tokens, 4 * units[2]), brain_type),
        ((2 * tokens, 4 * units[2]), brain_type),
        ((tokens, width), float_type),
    ]
    outs = pl.pallas_call(
        partial(forward_kernel, groups, layers, score_scale),
        out_shape=[
            jax.ShapeDtypeStruct((tokens, width), inputs.dtype),
            jax.ShapeDtypeStruct((tokens, width), inputs.dtype),
            jax.ShapeDtypeStruct((8, *vectors.shape), vectors.dtype),
            jax.ShapeDtypeStruct(ids.shape, ids.dtype),
            jax.ShapeDtypeStruct((tokens, width), brain_type),
        ]
        + [jax.ShapeDtypeStruct((width, 4 * u), brain_type) for _ in range(layers) for u in units]
        + [jax.ShapeDtypeStruct(*shape) for _ in range(layers) for shape in kept],
        in_specs=hbm(10),
        out_specs=hbm(5 + groups + 8 * layers),
        scratch_shapes=[pltpu.VMEM(*shape) for shape in kept]
        + [pltpu.VMEM((width, 4 * u), brain_type) for u in units]
        + [
            pltpu.VMEM((tokens, width), brain_type),
            pltpu.VMEM((tokens, width), brain_type),
            pltpu.VMEM((tokens, width), brain_type),
            pltpu.VMEM((8, *vectors.shape), vectors.dtype),
            pltpu.VMEM(ids.shape, ids.dtype),
            pltpu.VMEM(ids.shape, ids.dtype),
            pltpu.VMEM((1, 2 * tokens), float_type),
            pltpu.VMEM((2 * tokens, 128), float_type),
            pltpu.SemaphoreType.DMA((remote,)),
            pltpu.SemaphoreType.DMA((remote,)),
            pltpu.SemaphoreType.DMA((2 * groups + 10 + 12 * layers,)),
        ],
        compiler_params=pltpu.CompilerParams(
            collective_id=0, has_side_effects=True, vmem_limit_bytes=60 * 1024 * 1024
        ),
        name="forward",
    )(inputs, cotangent, vectors, ids, *raw)
    saved = [outs[5 + groups + 8 * i : 13 + groups + 8 * i] for i in range(layers)]
    return outs[1], outs[2], outs[3], outs[4], outs[5 : 5 + groups], saved


def hand_out(move, clock, loaded, out, units):
    n = units // len(out)
    rows = pl.ds(0, loaded.shape[1] // 2)
    lanes = pl.ds(pl.multiple_of(move.core * n, 128), n)
    copies = []
    for i, target in enumerate(out):
        columns = pl.ds(i * n, n)
        there = loaded.at[1 - move.core, rows, columns]
        copies.append(move.send(there, target.at[:, lanes], move.sibling))
        copies.append(move.keep(loaded.at[move.core, rows, columns], target.at[:, lanes]))
    yield clock.post(units * 512, OVER_CORE) + 1.0
    for copy in copies:
        copy.wait()


def collect_stages(move, clock, first, loaded, got, out, free, release):
    first_got, second_got, far_got, cross_got, near_got = got
    rows, units = loaded.shape[1] // 2, loaded.shape[2] // 4
    sides = ((move.x_side, OVER_X), (move.y_side, OVER_Y))
    done = [copy for copy, _ in first]

    def go(source, target, device, links):
        copy = move.send(source, target, device)
        done.append(copy)
        return copy, clock.post(size_of(source), links)

    def total(target, source, height, width):
        def body(i):
            span = (at(i, 32), pl.ds(0, width))
            target[span] = (
                target[span].astype(float_type) + source[span].astype(float_type)
            ).astype(brain_type)

        loop(height // 32, body)

    second = []
    for i in range(2):
        yield first[i][1]
        first[i][0].wait_recv()
        total(loaded.at[i], first_got.at[i], 2 * rows, 4 * units)
        second.append(go(loaded.at[i, pl.ds(rows, rows)], second_got.at[i], *sides[i]))
    free("near")
    free("across")
    base = move.remote
    move.remote += 6
    outer_lanes = pl.ds(2 * units, 2 * units)

    def far(i):
        source = loaded.at[i, pl.ds(0, rows), outer_lanes]
        return move.make(source, far_got.at[i], move.z_near, base + i, base + i)

    def cross(i):
        source = loaded.at[i, pl.ds(0, rows), outer_lanes]
        return move.make(source, cross_got.at[i], move.z_across, base + 2 + i, base + 2 + i)

    def near(i):
        source = loaded.at[i, pl.ds(0, rows), pl.ds(units, units)]
        return move.make(source, near_got.at[i], move.z_near, base + 4 + i, base + 4 + i)

    def lanes_total(i, source, pairs):
        def body(step):
            rows_here = at(step, 32)
            for lane, to_lane in pairs:
                span = (rows_here, pl.ds(to_lane * units, units))
                loaded[(i, *span)] = (
                    loaded[(i, *span)].astype(float_type)
                    + source[i, rows_here, pl.ds(lane * units, units)].astype(float_type)
                ).astype(brain_type)

        loop(rows // 32, body)

    far_due = []
    for i in range(2):
        yield second[i][1]
        second[i][0].wait_recv()
        total(loaded.at[i], second_got.at[i], rows, 4 * units)

        @pl.when(move.outer)
        def _():
            far(i).start()
            near(i).start()

        far_due.append(clock.post(size_of(far_got.at[i]), OVER_NEAR))
    cross_due = []
    for i in range(2):
        yield far_due[i]

        @pl.when(move.inner)
        def _():
            far(i).wait_recv()
            lanes_total(i, far_got, ((0, 3), (1, 2)))
            cross(i).start()

        cross_due.append(clock.post(size_of(far_got.at[i]), OVER_MID))
    near_due = []
    for i in range(2):
        yield cross_due[i]

        @pl.when(move.inner)
        def _():
            cross(i).wait_recv()
            lanes_total(i, cross_got, ((0, 1), (1, 0)))
            near(i).start()

        near_due.append(clock.post(size_of(near_got.at[i]), OVER_NEAR))
    yield max(near_due)
    for i in range(2):
        near(i).wait()
        lanes_total(i, near_got, ((0, 0),))

    @pl.when(move.outer)
    def _():
        for i in range(2):
            far(i).wait_send()

    @pl.when(move.inner)
    def _():
        for i in range(2):
            cross(i).wait_send()

    release()
    yield from hand_out(move, clock, loaded, out, units)
    for copy in done:
        copy.wait_send()


def vector_sum_stages(move, clock, vectors, sums, by_core, by_y, by_x, by_near, by_far, out):
    def go(source, target, device):
        return move.send(source, target, device), clock.now + 3.0

    copy, due = go(vectors.at[1 - move.core], by_core, move.sibling)
    yield due
    copy.wait()
    sums[...] = vectors[move.core] + by_core[...]
    copy, due = go(sums.at[pl.ds(2, 2)], by_y, move.y_side)
    yield due
    copy.wait()
    sums[:2] += by_y[...]
    copy, due = go(sums.at[1], by_x, move.x_side)
    yield due
    copy.wait()
    sums[0] += by_x[...]
    copy, due = go(sums.at[0], by_near, move.z_near)
    yield due
    copy.wait()
    sums[1] = sums[0] + by_near[...]
    copy, due = go(sums.at[1], by_far, move.z_across)
    yield due
    copy.wait()
    out[...] = sums[1] + by_far[...]


def backward_steps(move, plan, score_scale, layers, box, start_group):
    clock = plan.clock
    grad, below, source = box["grad"], box["below"], box["source"]
    branch, normed = box["branch"], box["normed"]
    upper, fc_in, hid, slope = box["upper"], box["fc_in"], box["hid"], box["slope"]
    send, got, sums = box["send"], box["got"], box["sums"]
    half = grad.shape[0]
    whole = 2 * half
    tile = 256
    qkv_width = box["layers"][0]["qkv"].shape[1]
    att_width = box["layers"][0]["att"].shape[1]
    wide = hid.shape[1]
    qkv_part, att_part = pl.ds(0, qkv_width), pl.ds(qkv_width, att_width)
    loads = {}

    def load(layer, name, target):
        loads[name] = move.keep(box["layers"][layer][name], target)

    def need(*names):
        for name in names:
            if name in loads:
                loads.pop(name).wait()

    def load_mlp(layer):
        load(layer, "hid", hid)
        load(layer, "w3", upper)
        load(layer, "slope", slope)

    def share_branch():
        def body(i):
            rows = at(i, 64)
            branch[rows, :] = grad[rows, :].astype(brain_type)

        loop(half // 64, body)
        return move.send(
            branch.at[pl.ds(0, half)], branch.at[pl.ds(half, half)], move.sibling
        )

    def weight_grads(kind, layer, left, right, first, width):
        group = start_group(kind, layer)
        step = width if width <= 1024 else width // 2
        for target, side, quarter, link in (
            ("sent", 0, 1, OVER_Y),
            ("sent", 1, 3, OVER_X),
            ("loaded", 0, 0, None),
            ("loaded", 1, 2, None),
        ):
            rows = left[:, pl.ds(quarter * 256, 256)]

            def body(i, target=target, side=side, rows=rows):
                part = right[:, pl.ds(pl.multiple_of(first + i * step, 128), step)]
                group[target][side, :, at(i, step)] = tn(rows, part).astype(brain_type)

            loop(width // step, body)
            if target == "sent":
                group["go"](side, link)
            yield 1.0 + width * 0.85e-3
        group["begin"]()

    def partial_sums(left, first, width, weight, at_column):
        def body(i):
            columns = at(i, tile)
            send[:, columns] = nt(
                left[pl.ds(half, half), pl.ds(first, width)],
                weight[columns, pl.ds(at_column, width)],
            ).astype(brain_type)

        loop(weight.shape[0] // tile, body)
        return move.send(send, got, move.sibling)

    def whole_sums(left, first, width, weight, at_column, copy):
        def product(i):
            columns = at(i, tile)
            below[:, columns] = nt(
                left[pl.ds(0, half), pl.ds(first, width)],
                weight[columns, pl.ds(at_column, width)],
            )

        loop(weight.shape[0] // tile, product)
        copy.wait()

    def norm_back(gain, grad_gain, grad_shift):
        gain_row = vector_row(box["vectors"], gain)
        sums[...] = jnp.zeros_like(sums)

        def body(i):
            rows = at(i, 64)
            unit, scale = center_of(source[rows, :])
            down = below[rows, :] + got[rows, :].astype(float_type)
            turn = down * gain_row
            grad[rows, :] += scale * (
                turn
                - jnp.mean(turn, axis=-1, keepdims=True)
                - unit * jnp.mean(turn * unit, axis=-1, keepdims=True)
            )
            sums[0:1, :] += jnp.sum(down * unit, axis=0, keepdims=True)
            sums[1:2, :] += jnp.sum(down, axis=0, keepdims=True)

        loop(half // 64, body)
        for row, index in ((0, grad_gain), (1, grad_shift)):
            for core in range(2):
                for spot in range(4):
                    to = spot if core == 0 else (0, 2, 1, 3)[spot]
                    box["vector_grads"][core, to, index : index + 1, :] = sums[
                        row : row + 1, pl.ds((core * 4 + spot) * 128, 128)
                    ]

    def slope_times(first):
        def body(i):
            rows, columns = pl.ds(first * half, half), at(i, tile)
            product = nn(branch[rows, :], upper[:, columns])
            slope[rows, columns] = (product * slope[rows, columns].astype(float_type)).astype(
                brain_type
            )

        loop(wide // tile, body)

    def attention(pair):
        keys_at, values_at = pl.ds(pair * 384 + 128, 128), pl.ds(pair * 384 + 256, 128)
        grad_keys, grad_values = box["grad_keys"], box["grad_values"]
        grad_keys[...] = jnp.zeros_like(grad_keys)
        grad_values[...] = jnp.zeros_like(grad_values)

        def body(part):
            rows = at(part, tile)
            low_lane = lax.broadcasted_iota(jnp.int32, (tile, 128), 1) < 64
            keys, values = hid[:, keys_at], hid[:, values_at]
            query = hid[rows, pl.ds(pair * 384, 128)]
            out_grad = slope[rows, pl.ds(qkv_width + pair * 128, 128)]
            same = box["seg_col"][:, :1] == box["seg_row"][:, rows]
            grad_queries = []
            for head in range(2):
                mine = low_lane if head == 0 else jnp.logical_not(low_lane)
                masked = jnp.where(mine, query, jnp.zeros_like(query))
                masked = masked * jnp.asarray(score_scale, brain_type)
                grad_masked = jnp.where(mine, out_grad, jnp.zeros_like(out_grad))
                scores = jnp.where(same, nt(keys, masked), -1e30)
                weight = jnp.exp(scores - jnp.max(scores, axis=0, keepdims=True))
                probs = weight * (1.0 / jnp.sum(weight, axis=0, keepdims=True))
                grad_probs = nt(values, grad_masked)
                inner = jnp.sum(probs * grad_probs, axis=0, keepdims=True)
                grad_raw = (probs * (grad_probs - inner)).astype(brain_type)
                grad_values[...] += nn(probs.astype(brain_type), grad_masked)
                grad_keys[...] += nn(grad_raw, masked)
                grad_queries.append(tn(grad_raw, keys))
            slope[rows, pl.ds(pair * 384, 128)] = (
                jnp.where(low_lane, grad_queries[0], grad_queries[1]) * score_scale
            ).astype(brain_type)

        loop(whole // tile, body)
        slope[:, keys_at] = grad_keys[...].astype(brain_type)
        slope[:, values_at] = grad_values[...].astype(brain_type)

    load_mlp(layers - 1)
    load(layers - 1, "n2", normed)
    load(layers - 1, "w2", fc_in)
    load(layers - 1, "mid", source)
    for layer in reversed(range(layers)):
        sent = share_branch()
        need("w3", "slope")
        yield 1.0
        slope_times(0)
        yield 4.0
        sent.wait()
        need("hid")
        yield from weight_grads(3, layer, branch, hid, 0, wide)
        load(layer, "qkv", hid.at[:, qkv_part])
        load(layer, "att", hid.at[:, att_part])
        slope_times(1)
        load(layer, "w0", upper.at[:, qkv_part])
        load(layer, "w1", upper.at[:, att_part])
        yield 4.0
        need("n2")
        yield from weight_grads(2, layer, normed, slope, 0, wide)
        load(layer, "n1", normed)
        need("w2")
        sent = partial_sums(slope, 0, wide, fc_in, 0)
        yield 3.5
        need("mid")
        whole_sums(slope, 0, wide, fc_in, 0, sent)
        if layer > 0:
            load(layer - 1, "w2", fc_in)
        yield 3.5
        norm_back(2 * layers + layer, 2 * layers + layer, 3 * layers + layer)
        load(layer, "x", source)
        sent = share_branch()
        need("w1")
        yield 5.0

        def grad_attended(first):
            rows = pl.ds(first * half, half)
            slope[rows, att_part] = nn(branch[rows, :], upper[:, att_part]).astype(brain_type)

        grad_attended(0)
        sent.wait()
        grad_attended(1)
        yield 2.0
        need("att")
        yield from weight_grads(1, layer, branch, hid, qkv_width, att_width)
        need("qkv")
        for pair in range(qkv_width // 384):
            attention(pair)
            yield 9.0
        need("n1")
        yield from weight_grads(0, layer, normed, slope, 0, qkv_width)
        if layer > 0:
            load(layer - 1, "n2", normed)
            load(layer - 1, "hid", hid)
        need("w0")
        sent = partial_sums(slope, 0, qkv_width, upper, 0)
        yield 3.0
        whole_sums(slope, 0, qkv_width, upper, 0, sent)
        if layer > 0:
            load(layer - 1, "w3", upper)
            load(layer - 1, "slope", slope)
        need("x")
        yield 3.0
        norm_back(layer, layer, layers + layer)
        if layer > 0:
            load(layer - 1, "mid", source)
        yield 4.0

    def body(i):
        rows = at(i, 64)
        send[rows, :] = grad[rows, :].astype(brain_type)

    loop(half // 64, body)


BACK_NAMES = ("n1", "qkv", "att", "mid", "n2", "hid", "slope", "x")


def backward_kernel(layers, score_scale, *refs):
    refs = list(refs)

    def take(count):
        taken, refs[:count] = refs[:count], []
        return taken

    kinds = 4
    groups = kinds * layers
    block, cotangent, vectors, ids, other_ids_in = take(5)
    weights = take(groups)
    saved = [dict(zip(BACK_NAMES, take(8))) for _ in range(layers)]
    for layer in range(layers):
        for kind in range(kinds):
            saved[layer][f"w{kind}"] = weights[kinds * layer + kind]
    block_out, below_out, vectors_out = take(3)
    outs = take(6)
    box = {"layers": saved}
    names = ("upper", "fc_in", "hid", "slope", "normed", "branch", "source", "grad", "below")
    box.update(zip(names, take(9)))
    names = ("send", "got", "grad_keys", "grad_values", "seg_row", "seg_col", "vectors", "sums")
    box.update(zip(names, take(8)))
    own_ids, other_ids, box["vector_grads"] = take(3)
    small = take(6)
    buffers = [take(7) for _ in range(kinds)]
    (credits,) = take(1)
    move = Mover(*refs)
    clock = Clock(SLACK)
    plan = Plan(clock)
    copies = [
        move.keep(cotangent, box["send"]),
        move.keep(vectors, box["vectors"]),
        move.keep(ids, own_ids),
        move.keep(other_ids_in, other_ids),
    ]
    move.greet()
    finish_above = return_tokens(move, block, block_out)
    for copy in copies:
        copy.wait()
    segment_rows(move, own_ids, other_ids, box["seg_row"], box["seg_col"])

    def body(i):
        rows = at(i, 64)
        box["grad"][rows, :] = box["send"][rows, :].astype(float_type)

    loop(box["grad"].shape[0] // 64, body)
    devices = {
        "x": move.x_side,
        "y": move.y_side,
        "across": move.z_across,
        "near": move.z_near,
    }
    order = list(devices)
    running = {}

    def start_group(kind, layer):
        if kind in running:
            plan.finish(running.pop(kind))
        sent, loaded, *got = buffers[kind]
        first = [None, None]

        def free(name):
            if layer < layers - 1:
                pl.semaphore_wait(credits.at[kind * 4 + order.index(name)], 1)

        def release():
            if layer > 0:
                for i, name in enumerate(order):
                    pl.semaphore_signal(
                        credits.at[kind * 4 + i],
                        inc=1,
                        device_id=devices[name],
                        device_id_type=pl.DeviceIdType.MESH,
                    )

        out = [
            ref.at[layer] for ref in (outs[:3], outs[3:4], outs[4:5], outs[5:6])[kind]
        ]

        def go(side, link):
            name = "y" if side == 0 else "x"
            free(name)
            copy = move.send(sent.at[side], got[0].at[side], devices[name])
            first[side] = (copy, clock.post(size_of(sent.at[side]), link))

        def begin():
            task = collect_stages(move, clock, first, loaded, got, out, free, release)
            plan.add(task)
            running[kind] = task

        return {"sent": sent, "loaded": loaded, "go": go, "begin": begin}

    def compute():
        yield from backward_steps(move, plan, score_scale, layers, box, start_group)
        ends.append(return_tokens(move, box["send"], below_out))
        plan.add(vector_sum_stages(move, clock, box["vector_grads"], *small, vectors_out))

    ends = [finish_above]
    plan.run(compute(), lambda: True)
    for finish in ends:
        finish()


def backward_all(block, cotangent, vectors, ids, other_ids, weights, saved, layers, score_scale):
    tokens, width = cotangent.shape
    units = [w.shape[1] for w in weights[:4]]
    count = len(weights)
    low, high = brain_type, float_type
    small_vectors = (2, 4, vectors.shape[1], vectors.shape[2])
    scratch = [((2 * tokens, units[2]), low)] * 4
    scratch += [((2 * tokens, width), low)] * 2
    scratch += [((tokens, width), high)] * 3
    scratch += [((tokens, width), low)] * 2
    scratch += [((2 * tokens, 128), high)] * 2
    scratch += [((1, 2 * tokens), high), ((2 * tokens, 128), high)]
    scratch += [(vectors.shape, high), ((8, width), high)]
    scratch += [(ids.shape, ids.dtype)] * 2
    scratch += [(small_vectors, high), (small_vectors[1:], high), (small_vectors[1:], high)]
    scratch += [((2, *small_vectors[2:]), high)] + [(small_vectors[2:], high)] * 3
    for wide in units:
        for rows, columns in ((256, 1), (256, 1), (256, 1), (128, 1), (128, 2), (128, 2), (128, 4)):
            scratch.append(((2, rows, wide // columns), low))
    remote = 16 * count + 9 + 4 * layers + 8
    outs = pl.pallas_call(
        partial(backward_kernel, layers, score_scale),
        out_shape=[jax.ShapeDtypeStruct((2, tokens // 2, width), low)] * 2
        + [jax.ShapeDtypeStruct(vectors.shape[1:], high)]
        + [jax.ShapeDtypeStruct((layers, 128, units[0] // 6), low)] * 3
        + [jax.ShapeDtypeStruct((layers, 128, w // 2), low) for w in units[1:]],
        in_specs=hbm(5 + count + 8 * layers),
        out_specs=hbm(2) + [pl.BlockSpec(memory_space=pltpu.VMEM)] + hbm(6),
        scratch_shapes=[pltpu.VMEM(*shape) for shape in scratch]
        + [
            pltpu.SemaphoreType.REGULAR((16,)),
            pltpu.SemaphoreType.DMA((remote,)),
            pltpu.SemaphoreType.DMA((remote,)),
            pltpu.SemaphoreType.DMA((8 + 14 * layers + 2 * count,)),
        ],
        compiler_params=pltpu.CompilerParams(
            collective_id=1, has_side_effects=True, vmem_limit_bytes=62 * 1024 * 1024
        ),
        name="backward",
    )(block, cotangent, vectors, ids, other_ids, *weights, *[a for kept in saved for a in kept])
    return outs[:2], outs[2], outs[3:]


def per_chip(
    inputs,
    segment_ids,
    norm1_gain,
    norm1_shift,
    w_query,
    w_key,
    w_value,
    w_output,
    norm2_gain,
    norm2_shift,
    w_fc_in,
    w_fc_out,
    cotangent,
):
    layers = norm1_gain.shape[0]
    head_width = inputs.shape[3] // HEADS
    score_scale = 1.0 / math.sqrt(head_width)
    vectors = jnp.concatenate([norm1_gain, norm1_shift, norm2_gain, norm2_shift], axis=0)
    grad, vectors, other_ids, block, weights, saved = forward_all(
        inputs[:, 0],
        cotangent[:, 0],
        vectors.astype(float_type),
        segment_ids,
        (w_query, w_key, w_value, w_output.mT, w_fc_in, w_fc_out.mT),
        layers,
        score_scale,
    )
    tokens, vector_grads, outs = backward_all(
        block, grad, vectors, segment_ids, other_ids, weights, saved, layers, score_scale
    )
    block_output, input_grad = (part.astype(float_type) for part in tokens)
    grad_query, grad_key, grad_value, grad_output, grad_fc_in, grad_fc_out = outs
    grad_output, grad_fc_out = grad_output.mT, grad_fc_out.mT
    gain_one, shift_one, gain_two, shift_two = (
        vector_grads[i * layers : (i + 1) * layers] for i in range(4)
    )
    return (
        block_output[:, None],
        input_grad[:, None],
        gain_one,
        shift_one,
        grad_query.astype(float_type),
        grad_key.astype(float_type),
        grad_value.astype(float_type),
        grad_output.astype(float_type),
        gain_two,
        shift_two,
        grad_fc_in.astype(float_type),
        grad_fc_out.astype(float_type),
    )


def layer_norm(token_rows, gain_vec, shift_vec):
    center = token_rows - jnp.mean(token_rows, axis=-1, keepdims=True)
    spread = jnp.mean(center * center, axis=-1, keepdims=True)
    return center * lax.rsqrt(spread + 1e-05) * gain_vec + shift_vec


def normed_local(token_rows, gain_vec, shift_vec):
    return layer_norm(token_rows, gain_vec.astype(float_type), shift_vec.astype(float_type)).astype(
        brain_type
    )


def normed_send(token_rows, gain_vec, shift_vec):
    return lax.all_gather(
        normed_local(token_rows, gain_vec, shift_vec), "tensor", axis=0, tiled=True
    )


def normed_resend(token_rows, gain_vec, shift_vec):
    return lax.all_gather(
        normed_local(token_rows, gain_vec, shift_vec), "tensor", axis=0, tiled=True
    )


def branch_total(partial_sum):
    return lax.psum_scatter(
        partial_sum.astype(jnp.bfloat16), "tensor", scatter_dimension=0, tiled=True
    ).astype(jnp.float32)


def branch_cotangent(grad_rows):
    return lax.all_gather(grad_rows.astype(brain_type), "tensor", axis=0, tiled=True)


def input_total(partial_sum):
    return lax.psum_scatter(
        partial_sum.astype(jnp.bfloat16), "tensor", scatter_dimension=0, tiled=True
    ).astype(jnp.float32)


def norm_backward(token_rows, gain_vec, shift_vec, grad_normed):
    _, norm_pull = jax.vjp(
        layer_norm, token_rows, gain_vec.astype(float_type), shift_vec.astype(float_type)
    )
    return norm_pull(grad_normed)


def masked_scores(query_part, segment_part, key_heads, segment, score_scale):
    raw_scores = jnp.einsum(
        "qhd,khd->hqk", query_part, key_heads, preferred_element_type=float_type
    )
    same_scene = segment_part[:, None] == segment[None, :]
    return jnp.where(same_scene[None], raw_scores * score_scale, -1e30)


def attend_forward(queries, key_heads, values, segment, block_rows):
    seq_len, head_count, head_width = queries.shape
    score_scale = 1.0 / math.sqrt(head_width)
    block_count = seq_len // block_rows

    def one_block(block_pair):
        query_part, segment_part = block_pair
        scores = masked_scores(query_part, segment_part, key_heads, segment, score_scale)
        row_max = jnp.max(scores, axis=-1, keepdims=True)
        exp_scores = jnp.exp(scores - row_max)
        row_total = jnp.sum(exp_scores, axis=-1, keepdims=True)
        probabilities = (exp_scores / row_total).astype(brain_type)
        block_out = jnp.einsum(
            "hqk,khd->qhd", probabilities, values, preferred_element_type=float_type
        )
        log_total = (row_max + jnp.log(row_total))[..., 0]
        return (block_out.astype(brain_type), log_total)

    query_blocks = queries.reshape(block_count, block_rows, head_count, head_width)
    segment_blocks = segment.reshape(block_count, block_rows)
    outputs, log_totals = lax.map(one_block, (query_blocks, segment_blocks))
    return (outputs.reshape(seq_len, head_count * head_width), log_totals)


def attend_backward(queries, key_heads, values, segment, log_totals, grad_out, block_rows):
    seq_len, head_count, head_width = queries.shape
    score_scale = 1.0 / math.sqrt(head_width)
    block_count = seq_len // block_rows

    def one_block(carry_pair, block_items):
        grad_keys, grad_values = carry_pair
        query_part, segment_part, log_part, grad_part = block_items
        scores = masked_scores(query_part, segment_part, key_heads, segment, score_scale)
        probabilities = jnp.exp(scores - log_part[..., None])
        grad_probs = jnp.einsum(
            "qhd,khd->hqk", grad_part, values, preferred_element_type=float_type
        )
        row_inner = jnp.sum(probabilities * grad_probs, axis=-1, keepdims=True)
        grad_raw = (probabilities * (grad_probs - row_inner) * score_scale).astype(brain_type)
        grad_query = jnp.einsum(
            "hqk,khd->qhd", grad_raw, key_heads, preferred_element_type=float_type
        )
        grad_keys = grad_keys + jnp.einsum(
            "hqk,qhd->khd", grad_raw, query_part, preferred_element_type=float_type
        )
        grad_values = grad_values + jnp.einsum(
            "hqk,qhd->khd",
            probabilities.astype(brain_type),
            grad_part,
            preferred_element_type=float_type,
        )
        return ((grad_keys, grad_values), grad_query.astype(brain_type))

    zero_heads = jnp.zeros((seq_len, head_count, head_width), float_type)
    block_items = (
        queries.reshape(block_count, block_rows, head_count, head_width),
        segment.reshape(block_count, block_rows),
        log_totals,
        grad_out.reshape(block_count, block_rows, head_count, head_width),
    )
    (grad_keys, grad_values), grad_queries = lax.scan(
        one_block, (zero_heads, zero_heads), block_items
    )
    flat_shape = (seq_len, head_count * head_width)
    return (
        grad_queries.reshape(flat_shape),
        grad_keys.astype(brain_type).reshape(flat_shape),
        grad_values.astype(brain_type).reshape(flat_shape),
    )


def fresh_totals(layers, attn_width, hidden_width):
    vector_zero = jnp.zeros((layers, D), float_type)
    column_zero = jnp.zeros((layers, D, attn_width), float_type)
    return [
        vector_zero,
        vector_zero,
        column_zero,
        column_zero,
        column_zero,
        jnp.zeros((layers, attn_width, D), float_type),
        vector_zero,
        vector_zero,
        jnp.zeros((layers, D, hidden_width), float_type),
        jnp.zeros((layers, hidden_width, D), float_type),
    ]


def add_into(grad_totals, position, layer_index, term):
    grad_totals[position] = grad_totals[position].at[layer_index].add(term)


def per_device(
    inputs,
    segment_ids,
    norm1_gain,
    norm1_shift,
    w_query,
    w_key,
    w_value,
    w_output,
    norm2_gain,
    norm2_shift,
    w_fc_in,
    w_fc_out,
    cotangent,
):
    micro_count = inputs.shape[0]
    layers = norm1_gain.shape[0]
    seq_len = segment_ids.shape[2]
    block_rows = min(512, seq_len)
    head_width = D // HEADS
    attn_width = w_query.shape[2]
    hidden_width = w_fc_in.shape[2]
    grad_totals = fresh_totals(layers, attn_width, hidden_width)
    reduced = None
    output_list = []
    input_grad_list = []
    for micro_index in range(micro_count):
        token_rows = inputs[micro_index, 0].astype(float_type)
        segment = segment_ids[micro_index, 0]
        saved_state = []
        for layer_index in range(layers):
            weights = (
                lax.all_gather(norm1_gain[layer_index], "dp", axis=0, tiled=True),
                lax.all_gather(norm1_shift[layer_index], "dp", axis=0, tiled=True),
                lax.all_gather(w_query[layer_index], "dp", axis=0, tiled=True),
                lax.all_gather(w_key[layer_index], "dp", axis=0, tiled=True),
                lax.all_gather(w_value[layer_index], "dp", axis=0, tiled=True),
                lax.all_gather(w_output[layer_index], "dp", axis=1, tiled=True),
                lax.all_gather(norm2_gain[layer_index], "dp", axis=0, tiled=True),
                lax.all_gather(norm2_shift[layer_index], "dp", axis=0, tiled=True),
                lax.all_gather(w_fc_in[layer_index], "dp", axis=0, tiled=True),
                lax.all_gather(w_fc_out[layer_index], "dp", axis=1, tiled=True),
            )
            (
                gain_one,
                shift_one,
                query_w,
                key_w,
                value_w,
                output_w,
                gain_two,
                shift_two,
                fc_in_w,
                fc_out_w,
            ) = weights
            whole_weights = None
            normed = normed_send(token_rows, gain_one, shift_one)
            queries = jnp.dot(normed, query_w, preferred_element_type=float_type).astype(brain_type)
            key_heads = jnp.dot(normed, key_w, preferred_element_type=float_type).astype(brain_type)
            values = jnp.dot(normed, value_w, preferred_element_type=float_type).astype(brain_type)
            attended, log_totals = attend_forward(
                queries.reshape(seq_len, -1, head_width),
                key_heads.reshape(seq_len, -1, head_width),
                values.reshape(seq_len, -1, head_width),
                segment,
                block_rows,
            )
            mid_rows = token_rows + branch_total(
                jnp.dot(attended, output_w, preferred_element_type=float_type)
            )
            normed_two = normed_send(mid_rows, gain_two, shift_two)
            pre_act = jnp.dot(normed_two, fc_in_w, preferred_element_type=float_type)
            hidden = jax.nn.gelu(pre_act, approximate=False).astype(brain_type)
            next_rows = mid_rows + branch_total(
                jnp.dot(hidden, fc_out_w, preferred_element_type=float_type)
            )
            saved_state.append(
                (
                    token_rows,
                    mid_rows,
                    weights,
                    normed,
                    normed_two,
                    queries,
                    key_heads,
                    values,
                    attended,
                    log_totals,
                    pre_act,
                    hidden,
                    whole_weights,
                )
            )
            token_rows = next_rows
        output_list.append(token_rows)
        grad_rows = cotangent[micro_index, 0].astype(float_type)
        for layer_index in reversed(range(layers)):
            (
                layer_rows,
                mid_rows,
                weights,
                normed,
                normed_two,
                queries,
                key_heads,
                values,
                attended,
                log_totals,
                pre_act,
                hidden,
                whole_weights,
            ) = saved_state[layer_index]
            weights = (
                lax.all_gather(norm1_gain[layer_index], "dp", axis=0, tiled=True),
                lax.all_gather(norm1_shift[layer_index], "dp", axis=0, tiled=True),
                lax.all_gather(w_query[layer_index], "dp", axis=0, tiled=True),
                lax.all_gather(w_key[layer_index], "dp", axis=0, tiled=True),
                lax.all_gather(w_value[layer_index], "dp", axis=0, tiled=True),
                lax.all_gather(w_output[layer_index], "dp", axis=1, tiled=True),
                lax.all_gather(norm2_gain[layer_index], "dp", axis=0, tiled=True),
                lax.all_gather(norm2_shift[layer_index], "dp", axis=0, tiled=True),
                lax.all_gather(w_fc_in[layer_index], "dp", axis=0, tiled=True),
                lax.all_gather(w_fc_out[layer_index], "dp", axis=1, tiled=True),
            )
            (
                gain_one,
                shift_one,
                query_w,
                key_w,
                value_w,
                output_w,
                gain_two,
                shift_two,
                fc_in_w,
                fc_out_w,
            ) = weights
            normed = normed_resend(layer_rows, gain_one, shift_one)
            normed_two = normed_resend(mid_rows, gain_two, shift_two)
            grad_branch = branch_cotangent(grad_rows)
            add_into(
                grad_totals,
                9,
                layer_index,
                jnp.einsum("sf,sd->fd", hidden, grad_branch, preferred_element_type=float_type),
            )
            grad_hidden = jnp.einsum(
                "sd,fd->sf", grad_branch, fc_out_w, preferred_element_type=float_type
            )
            _, gelu_pull = jax.vjp(partial(jax.nn.gelu, approximate=False), pre_act)
            grad_pre = gelu_pull(grad_hidden)[0].astype(brain_type)
            add_into(
                grad_totals,
                8,
                layer_index,
                jnp.einsum("sd,sf->df", normed_two, grad_pre, preferred_element_type=float_type),
            )
            grad_normed = input_total(
                jnp.einsum("sf,df->sd", grad_pre, fc_in_w, preferred_element_type=float_type)
            )
            grad_mid_part, grad_gain, grad_shift = norm_backward(
                mid_rows, gain_two, shift_two, grad_normed
            )
            add_into(grad_totals, 6, layer_index, grad_gain)
            add_into(grad_totals, 7, layer_index, grad_shift)
            grad_mid = grad_rows + grad_mid_part
            grad_branch = branch_cotangent(grad_mid)
            add_into(
                grad_totals,
                5,
                layer_index,
                jnp.einsum("sa,sd->ad", attended, grad_branch, preferred_element_type=float_type),
            )
            grad_attended = jnp.einsum(
                "sd,ad->sa", grad_branch, output_w, preferred_element_type=float_type
            ).astype(brain_type)
            grad_queries, grad_keys, grad_values = attend_backward(
                queries.reshape(seq_len, -1, head_width),
                key_heads.reshape(seq_len, -1, head_width),
                values.reshape(seq_len, -1, head_width),
                segment,
                log_totals,
                grad_attended.reshape(seq_len, -1, head_width),
                block_rows,
            )
            add_into(
                grad_totals,
                2,
                layer_index,
                jnp.einsum("sd,sa->da", normed, grad_queries, preferred_element_type=float_type),
            )
            add_into(
                grad_totals,
                3,
                layer_index,
                jnp.einsum("sd,sa->da", normed, grad_keys, preferred_element_type=float_type),
            )
            add_into(
                grad_totals,
                4,
                layer_index,
                jnp.einsum("sd,sa->da", normed, grad_values, preferred_element_type=float_type),
            )
            grad_input_part = jnp.einsum(
                "sa,da->sd", grad_queries, query_w, preferred_element_type=float_type
            )
            grad_input_part = grad_input_part + jnp.einsum(
                "sa,da->sd", grad_keys, key_w, preferred_element_type=float_type
            )
            grad_input_part = grad_input_part + jnp.einsum(
                "sa,da->sd", grad_values, value_w, preferred_element_type=float_type
            )
            grad_normed = input_total(grad_input_part)
            grad_below, grad_gain, grad_shift = norm_backward(
                layer_rows, gain_one, shift_one, grad_normed
            )
            add_into(grad_totals, 0, layer_index, grad_gain)
            add_into(grad_totals, 1, layer_index, grad_shift)
            grad_rows = grad_mid + grad_below
        input_grad_list.append(grad_rows)
    reduced = (
        lax.psum_scatter(
            grad_totals[0].astype(jnp.bfloat16), "dp", scatter_dimension=1, tiled=True
        ).astype(jnp.float32),
        lax.psum_scatter(
            grad_totals[1].astype(jnp.bfloat16), "dp", scatter_dimension=1, tiled=True
        ).astype(jnp.float32),
        lax.psum_scatter(
            grad_totals[2].astype(jnp.bfloat16), "dp", scatter_dimension=1, tiled=True
        ).astype(jnp.float32),
        lax.psum_scatter(
            grad_totals[3].astype(jnp.bfloat16), "dp", scatter_dimension=1, tiled=True
        ).astype(jnp.float32),
        lax.psum_scatter(
            grad_totals[4].astype(jnp.bfloat16), "dp", scatter_dimension=1, tiled=True
        ).astype(jnp.float32),
        lax.psum_scatter(
            grad_totals[5].astype(jnp.bfloat16), "dp", scatter_dimension=2, tiled=True
        ).astype(jnp.float32),
        lax.psum_scatter(
            grad_totals[6].astype(jnp.bfloat16), "dp", scatter_dimension=1, tiled=True
        ).astype(jnp.float32),
        lax.psum_scatter(
            grad_totals[7].astype(jnp.bfloat16), "dp", scatter_dimension=1, tiled=True
        ).astype(jnp.float32),
        lax.psum_scatter(
            grad_totals[8].astype(jnp.bfloat16), "dp", scatter_dimension=1, tiled=True
        ).astype(jnp.float32),
        lax.psum_scatter(
            grad_totals[9].astype(jnp.bfloat16), "dp", scatter_dimension=2, tiled=True
        ).astype(jnp.float32),
    )
    norm_sums = lax.psum((reduced[0], reduced[1], reduced[6], reduced[7]), "tensor")
    block_output = jnp.stack(output_list)[:, None]
    input_grad = jnp.stack(input_grad_list)[:, None]
    return (
        block_output,
        input_grad,
        norm_sums[0],
        norm_sums[1],
        reduced[2],
        reduced[3],
        reduced[4],
        reduced[5],
        norm_sums[2],
        norm_sums[3],
        reduced[8],
        reduced[9],
    )


def solution(mesh):
    placed = (
        P(None, "dp", "tensor", None),
        P(None, "dp", None),
        P(None, "dp"),
        P(None, "dp"),
        P(None, "dp", "tensor"),
        P(None, "dp", "tensor"),
        P(None, "dp", "tensor"),
        P(None, "tensor", "dp"),
        P(None, "dp"),
        P(None, "dp"),
        P(None, "dp", "tensor"),
        P(None, "tensor", "dp"),
        P(None, "dp", "tensor", None),
    )
    line, plane = mesh.shape["tensor"], mesh.shape["dp"]
    fits = line == 4 and plane == 8 and 2 * line == plane
    return jax.shard_map(
        per_chip if fits else per_device,
        mesh=mesh,
        in_specs=placed,
        out_specs=(
            P(None, "dp", "tensor", None),
            P(None, "dp", "tensor", None),
            P(None, "dp"),
            P(None, "dp"),
            P(None, "dp", "tensor"),
            P(None, "dp", "tensor"),
            P(None, "dp", "tensor"),
            P(None, "tensor", "dp"),
            P(None, "dp"),
            P(None, "dp"),
            P(None, "dp", "tensor"),
            P(None, "tensor", "dp"),
        ),
        check_vma=False,
    )
```

```python
from functools import partial
import math

import jax
import jax.numpy as jnp
from jax import lax
from jax.experimental import pallas as pl
from jax.experimental.pallas import tpu as pltpu
from jax.sharding import PartitionSpec as P

D = 1024
HEADS = 16
float_type = jnp.float32
brain_type = jnp.bfloat16


def nt(left, right):
    return lax.dot_general(left, right, (((1,), (1,)), ((), ())), preferred_element_type=float_type)


def nn(left, right):
    return lax.dot_general(left, right, (((1,), (0,)), ((), ())), preferred_element_type=float_type)


def tn(left, right):
    return lax.dot_general(left, right, (((0,), (0,)), ((), ())), preferred_element_type=float_type)


def center_of(rows):
    center = rows - jnp.mean(rows, axis=-1, keepdims=True)
    scale = lax.rsqrt(jnp.mean(center * center, axis=-1, keepdims=True) + 1e-05)
    return center * scale, scale


class Mover:
    def __init__(self, send_sems, recv_sems, local_sems):
        self.send_sems, self.recv_sems, self.local_sems = send_sems, recv_sems, local_sems
        self.remote, self.local = 0, 0
        self.place = lax.axis_index("dp")
        self.height = lax.axis_index("tensor")
        self.core = lax.rem(self.place, 2)
        self.x_bit = lax.rem(self.place // 2, 2)
        self.y_bit = lax.rem(self.place // 4, 2)
        self.z_low = lax.rem(self.height, 2)
        self.z_high = self.height // 2
        self.sibling = {"dp": self.place + 1 - 2 * self.core}
        self.x_side = {"dp": self.place + 2 - 4 * self.x_bit}
        self.y_side = {"dp": self.place + 4 - 8 * self.y_bit}
        self.z_near = {"tensor": self.height + 1 - 2 * self.z_low}
        self.z_across = {"tensor": 3 - self.height}
        self.inner = self.z_low != self.z_high
        self.outer = jnp.logical_not(self.inner)

    def make(self, source, target, device, send_index, recv_index):
        return pltpu.make_async_remote_copy(
            src_ref=source,
            dst_ref=target,
            send_sem=self.send_sems.at[send_index],
            recv_sem=self.recv_sems.at[recv_index],
            device_id=device,
            device_id_type=pl.DeviceIdType.MESH,
        )

    def send(self, source, target, device):
        copy = self.make(source, target, device, self.remote, self.remote)
        self.remote += 1
        copy.start()
        return copy

    def keep(self, source, target):
        copy = pltpu.make_async_copy(source, target, self.local_sems.at[self.local])
        self.local += 1
        copy.start()
        return copy

    def greet(self):
        barrier = pltpu.get_barrier_semaphore()
        plane = self.place - self.core
        devices = [self.x_side, self.y_side]
        for step in range(1, 8):
            other = lax.rem(self.core * 4 + self.height + step, 8)
            devices.append({"dp": plane + other // 4, "tensor": lax.rem(other, 4)})
        for device in devices:
            pl.semaphore_signal(
                barrier, inc=1, device_id=device, device_id_type=pl.DeviceIdType.MESH
            )
        pl.semaphore_wait(barrier, len(devices))

    def column(self, y, x, half):
        y_off = lax.rem(y + self.y_bit, 2)
        x_off = lax.rem(x + self.x_bit, 2)
        spot = 2 * y_off + x_off if half == 0 else y_off + 2 * x_off
        return pl.multiple_of((half * 4 + spot) * 128, 128)


BLOCKS = [(y, x, half) for y in range(2) for x in range(2) for half in range(2)]


def move_tokens(move, ways, origins):
    base, local = move.remote, move.local
    move.remote += 2
    move.local += 2
    closing = []
    for i, (to_core, to_z, copies, whole, slot) in enumerate(ways):
        stays = jnp.logical_and(to_core == move.core, to_z == move.height)
        device = {"dp": move.place - move.core + to_core, "tensor": to_z}

        @pl.when(stays)
        def _():
            for source, target in copies:
                pltpu.make_async_copy(source, target, move.local_sems.at[local + i]).start()

        @pl.when(jnp.logical_not(stays))
        def _():
            for source, target in copies:
                move.make(source, target, device, base + i, base + slot).start()

        closing.append((stays, device, whole, i))

    def finish():
        for stays, device, (source, target), i in closing:
            @pl.when(stays)
            def _():
                pltpu.make_async_copy(source, target, move.local_sems.at[local + i]).wait()

            @pl.when(jnp.logical_not(stays))
            def _():
                move.make(source, target, device, base + i, base + i).wait_send()

        for slot, (from_core, from_z, (source, target)) in enumerate(origins):
            comes = jnp.logical_not(
                jnp.logical_and(from_core == move.core, from_z == move.height)
            )

            @pl.when(comes)
            def _():
                move.make(source, target, move.sibling, base + slot, base + slot).wait_recv()

    return finish


def fetch_tokens(move, source, target):
    rows = source.shape[1]
    here = pl.ds(pl.multiple_of(move.z_low * rows, rows), rows)
    ways, origins = [], []
    for micro in range(2):
        copies = [
            (
                source.at[micro, :, pl.ds(i * 128, 128)],
                target.at[here, pl.ds(move.column(*block), 128)],
            )
            for i, block in enumerate(BLOCKS)
        ]
        whole = (source.at[micro], target.at[here])
        ways.append((move.z_high, 2 * micro + move.core, copies, whole, move.z_low))
    for slot in range(2):
        whole = (source.at[slot], target.at[pl.ds(slot * rows, rows)])
        origins.append((move.z_low, 2 * move.core + slot, whole))
    return move_tokens(move, ways, origins)


def return_tokens(move, source, target):
    rows = target.shape[1]
    ways, origins = [], []
    for slot in range(2):
        copies = [
            (
                source.at[pl.ds(slot * rows, rows), pl.ds(move.column(*block), 128)],
                target.at[move.z_high, :, pl.ds(i * 128, 128)],
            )
            for i, block in enumerate(BLOCKS)
        ]
        whole = (source.at[pl.ds(slot * rows, rows)], target.at[move.z_high])
        ways.append((move.z_low, 2 * move.core + slot, copies, whole, move.z_high))
    for micro in range(2):
        whole = (source.at[pl.ds(micro * rows, rows)], target.at[micro])
        origins.append((move.z_high, 2 * micro + move.core, whole))
    return move_tokens(move, ways, origins)


class Clock:
    def __init__(self, latency):
        self.now = 0.0
        self.latency = latency
        self.free = {}

    def post(self, size, links):
        start, end = self.now, self.now
        for link, share in links:
            begin = max(self.free.get(link, 0.0), self.now)
            self.free[link] = begin + share * size * PER_BYTE
            end = max(end, self.free[link])
        return end + self.latency


PER_BYTE = 2.0 / 84e3
LATENCY, SLACK = 2.0, 6.0
BACKLOG = 8.0
Z_BACKLOG = 8.0
TOKENS_AT = 12.0
SCALE = 1.3
OVER_X, OVER_Y = (("x", 1.0),), (("y", 1.0),)
OVER_NEAR, OVER_MID = (("z_out", 1.0),), (("z_mid", 1.0),)
OVER_CORE = (("core", 0.1),)


class Plan:
    def __init__(self, clock):
        self.clock, self.tasks = clock, []

    def add(self, task):
        due = next(task, None)
        if due is not None:
            self.tasks.append((due, task))

    def step(self):
        index = min(range(len(self.tasks)), key=lambda i: self.tasks[i][0])
        due, task = self.tasks.pop(index)
        self.clock.now = max(self.clock.now, due)
        self.add(task)

    def due(self):
        return min((due for due, _ in self.tasks), default=float("inf"))

    def finish(self, task):
        while any(task is other for _, other in self.tasks):
            self.step()

    def run(self, compute, ready, scale=1.0):
        over = False
        while self.tasks or not over:
            if self.due() <= self.clock.now:
                self.step()
            elif not over and ready():
                cost = next(compute, None)
                if cost is None:
                    over = True
                else:
                    self.clock.now += scale * cost
            elif self.tasks:
                self.step()


def size_of(ref):
    return math.prod(ref.shape) * jnp.dtype(ref.dtype).itemsize


def spread_group(move, plan, pieces, whole, rank, plane_first, onward, complete):
    clock = plan.clock
    rows = whole.shape[0] // 8
    units = whole.shape[1] // 4
    half = whole.shape[0] // 2
    own = pl.ds(pl.multiple_of(move.core * half, half), rows)
    done, planes, swapped, kept = [], [], [], []

    def part(first, spot, lane, lanes):
        return whole.at[pl.ds(first * half + spot * rows, rows), pl.ds(lane * units, lanes * units)]

    def go(first, spot, lane, lanes, to_spot, to_lane, device, links):
        source = part(first, spot, lane, lanes)
        copy = move.send(source, part(first, to_spot, to_lane, lanes), device)
        done.append(copy)
        return copy, clock.post(size_of(source), links)

    x_way, y_way = (move.x_side, OVER_X), (move.y_side, OVER_Y)

    def backlog(*links):
        return max(clock.free.get(link, 0.0) for link in links) - clock.now

    def plane(lane, lanes, arrived):
        def relay():
            while backlog("x", "y") > BACKLOG:
                yield clock.now + backlog("x", "y") - BACKLOG + 0.01 * rank
            one = go(0, 0, lane, lanes, 1, lane, *x_way)
            two = go(1, 0, lane, lanes, 1, lane, *y_way)
            last = [go(0, 0, lane, lanes, 2, lane, *y_way), go(1, 0, lane, lanes, 2, lane, *x_way)]
            yield one[1]
            one[0].wait_recv()
            last.append(go(0, 1, lane, lanes, 3, lane, *y_way))
            yield two[1]
            two[0].wait_recv()
            last.append(go(1, 1, lane, lanes, 3, lane, *x_way))
            yield max(due for _, due in last)
            for copy, _ in last:
                copy.wait_recv()
            planes.append(lane)
            arrived()

        plan.add(relay())

    def line(block, parts, after_near):
        size = parts * size_of(block(0, 0))
        base = move.remote
        move.remote += 4 * parts

        def cross(i, lane, to_lane):
            index = base + 4 * i + (0 if lane == 0 else 1)
            return move.make(block(i, lane), block(i, to_lane), move.z_across, index, index)

        def hand_on(i, lane, to_lane):
            index = base + 4 * i
            to_index = index + (0 if to_lane == 3 else 1)
            return move.make(block(i, lane), block(i, to_lane), move.z_near, index + lane, to_index)

        def sent_across(lane, to_lane):
            @pl.when(move.inner)
            def _():
                for i in range(parts):
                    cross(i, lane, to_lane).start()

            return clock.post(size, OVER_MID)

        def handed(lane, to_lane):
            @pl.when(move.inner)
            def _():
                for i in range(parts):
                    cross(i, 0 if lane == 3 else 1, lane).wait_recv()
                    hand_on(i, lane, to_lane).start()

            return clock.post(size, OVER_NEAR)

        near = []
        for i in range(parts):
            near.append(move.send(block(i, 0), block(i, 1), move.z_near))
        done.extend(near)
        near_due = clock.post(size, OVER_NEAR)
        first_due = sent_across(0, 3)
        if not plane_first:
            plane(0, 1, arrived)
            onward()
        yield near_due
        for copy in near:
            copy.wait_recv()
        second_due = sent_across(1, 2)
        after_near()
        yield first_due
        handed(3, 2)
        yield second_due
        last_due = handed(2, 3)
        yield last_due

        @pl.when(move.outer)
        def _():
            for i in range(parts):
                hand_on(i, 3, 2).wait_recv()
                hand_on(i, 2, 3).wait_recv()

        @pl.when(move.inner)
        def _():
            for i in range(parts):
                cross(i, 0, 3).wait_send()
                cross(i, 1, 2).wait_send()
                hand_on(i, 3, 2).wait_send()
                hand_on(i, 2, 3).wait_send()

    def finish():
        for copy in done:
            copy.wait_send()
        complete()

    def arrived():
        if len(planes) == 3:
            finish()

    def start():
        yield clock.now
        while backlog("z_mid", "z_out") > Z_BACKLOG:
            yield clock.now + backlog("z_mid", "z_out") - Z_BACKLOG
        for copy in swapped + kept:
            copy.wait()

    def over_line_first():
        yield from start()

        def after_near():
            plane(1, 1, arrived)

        yield from line(lambda i, lane: part(i, 0, lane, 1), 2, after_near)
        plane(2, 2, arrived)

    def over_plane_first():
        yield from start()

        def along():
            yield clock.now
            yield from line(
                lambda i, lane: whole.at[pl.ds(0, 2 * half), pl.ds(lane * units, units)],
                1,
                lambda: None,
            )
            finish()

        plane(0, 1, lambda: plan.add(along()))
        onward()

    at_column = 0
    for mine, other in pieces:
        width = mine.shape[1]
        target = whole.at[own, pl.ds(at_column, width)]
        swapped.append(move.send(other, target, move.sibling))
        kept.append(move.keep(mine, target))
        at_column += width
    return over_plane_first() if plane_first else over_line_first()


def vector_stages(move, clock, vectors, out):
    own = move.core * 4
    keep = move.keep(vectors, out.at[own])
    copy = move.send(vectors, out.at[own], move.sibling)
    yield clock.now + 2.0
    keep.wait()
    copy.wait()
    over_x = [move.send(out.at[i], out.at[j], move.x_side) for i, j in ((0, 1), (4, 6))]
    yield clock.now + 4.0
    for copy in over_x:
        copy.wait()
    over_y = [
        move.send(out.at[i], out.at[j], move.y_side) for i, j in ((0, 2), (1, 3), (4, 5), (6, 7))
    ]
    yield clock.now + 4.0
    for copy in over_y:
        copy.wait()


def hbm(count):
    return [pl.BlockSpec(memory_space=pl.ANY)] * count


def loop(count, body):
    def step(i, carry):
        body(i)
        return carry

    lax.fori_loop(0, count, step, 0)


def at(i, size):
    return pl.ds(pl.multiple_of(i * size, size), size)


def vector_row(vectors, index):
    return jnp.concatenate([vectors[spot, index : index + 1, :] for spot in range(8)], axis=1)


def segment_rows(move, own_ids, other_ids, seg_row, seg_col):
    own, other = own_ids[move.z_high], other_ids[move.z_high]
    ids = jnp.where(move.z_low == move.core, own, other).astype(float_type)
    half = ids.shape[1] // 2
    turned = jnp.concatenate([ids[:, half:], ids[:, :half]], axis=1)
    ids = jnp.where(move.core == 0, ids, turned)
    seg_row[...] = ids
    seg_col[...] = jnp.transpose(jnp.broadcast_to(ids, (128, 2 * half)))


def forward_steps(move, score_scale, layers, box):
    half = box["x"].shape[0]
    tile = 256
    vectors = box["vectors"]
    send, got = box["send"], box["got"]
    saves = {}

    def save(name, layer):
        source = box[name]
        copy = move.keep(source, box["saved"][layer][name])
        saves[name] = copy

    def before(*names):
        for name in names:
            if name in saves:
                saves.pop(name).wait()

    def norm(source, target, gain, shift):
        gain_row, shift_row = vector_row(vectors, gain), vector_row(vectors, shift)

        def body(i):
            rows = at(i, 64)
            target[rows, :] = (center_of(source[rows, :])[0] * gain_row + shift_row).astype(
                brain_type
            )

        loop(half // 64, body)
        return move.send(target.at[pl.ds(0, half)], target.at[pl.ds(half, half)], move.sibling)

    def partial_sums(left, weight, first):
        def body(i):
            columns = at(i, tile)
            send[:, columns] = nt(left[pl.ds(half, half), :], weight[columns, :]).astype(brain_type)

        loop(weight.shape[0] // tile, body)
        return move.send(send, got, move.sibling)

    def whole_sums(left, weight, base, target, copy):
        copy.wait()

        def body(i):
            columns = at(i, tile)
            target[:, columns] = (
                base[:, columns]
                + nt(left[pl.ds(0, half), :], weight[columns, :])
                + got[:, columns].astype(float_type)
            )

        loop(weight.shape[0] // tile, body)

    for layer in range(layers):
        x, mid, n1, n2 = box["x"], box["mid"], box["n1"], box["n2"]
        qkv, att, hid, slope = box["qkv"], box["att"], box["hid"], box["slope"]
        base = 4 * layer
        save("x", layer)
        before("n1", "qkv")
        sent = norm(x, n1, layer, layers + layer)
        box["need"](base)
        yield 2.0
        box["load"](base)

        def project(first):
            def body(i):
                columns = at(i, tile)
                rows = pl.ds(first * half, half)
                qkv[rows, columns] = nn(n1[rows, :], box["w0"][:, columns]).astype(brain_type)

            loop(qkv.shape[1] // tile, body)

        project(0)
        yield 3.0
        sent.wait()
        project(1)
        save("n1", layer)
        save("qkv", layer)
        before("att")
        yield 3.0
        for pair in range(qkv.shape[1] // 384):

            def body(part, pair=pair):
                rows = at(part, tile)
                low_lane = lax.broadcasted_iota(jnp.int32, (tile, 128), 1) < 64
                query = qkv[rows, pl.ds(pair * 384, 128)] * jnp.asarray(score_scale, brain_type)
                keys = qkv[:, pl.ds(pair * 384 + 128, 128)]
                values = qkv[:, pl.ds(pair * 384 + 256, 128)]
                same = box["seg_col"][rows, :1] == box["seg_row"][...]
                outs = []
                for head in range(2):
                    mine = low_lane if head == 0 else jnp.logical_not(low_lane)
                    scores = nt(jnp.where(mine, query, jnp.zeros_like(query)), keys)
                    scores = jnp.where(same, scores, -1e30)
                    weight = jnp.exp(scores - jnp.max(scores, axis=1, keepdims=True))
                    inverse = 1.0 / jnp.sum(weight, axis=1, keepdims=True)
                    outs.append(nn((weight * inverse).astype(brain_type), values))
                att[rows, pl.ds(pair * 128, 128)] = jnp.where(low_lane, outs[0], outs[1]).astype(
                    brain_type
                )

            loop(2 * half // tile, body)
            if pair == qkv.shape[1] // 384 - 1:
                box["need"](base + 1)
            yield 5.5
        box["load"](base + 1)
        sent = partial_sums(att, box["w1"], half)
        save("att", layer)
        yield 1.5
        before("mid", "n2")
        whole_sums(att, box["w1"], x, mid, sent)
        sent = norm(mid, n2, 2 * layers + layer, 3 * layers + layer)
        save("mid", layer)
        before("hid", "slope")
        box["need"](base + 2)
        yield 4.0
        box["load"](base + 2)
        for first in range(2):
            if first == 1:
                sent.wait()
                save("n2", layer)
            rows = pl.ds(first * half, half)
            count = hid.shape[1] // tile
            for part in range(2):

                def body(i, rows=rows, part=part):
                    columns = at(part * (count // 2) + i, tile)
                    pre = nn(n2[rows, :], box["w2"][:, columns])
                    cdf = 0.5 * (1.0 + lax.erf(pre * math.sqrt(0.5)))
                    density = jnp.exp(-0.5 * pre * pre) * (1.0 / math.sqrt(2.0 * math.pi))
                    hid[rows, columns] = (pre * cdf).astype(brain_type)
                    slope[rows, columns] = (cdf + pre * density).astype(brain_type)

                loop(count // 2, body)
                if first == 1 and part == 1:
                    box["need"](base + 3)
                yield 3.0
        save("slope", layer)
        box["load"](base + 3)
        before("n1", "qkv", "att", "n2")
        sent = partial_sums(hid, box["w3"], half)
        save("hid", layer)
        yield 3.5
        before("x")
        whole_sums(hid, box["w3"], mid, x, sent)
        yield 4.0
    low = box["low"]

    def body(i):
        rows = at(i, 64)
        low[rows, :] = x[rows, :].astype(brain_type)

    loop(half // 64, body)
    copy = move.keep(low, box["block"])
    before(*list(saves))
    copy.wait()


def forward_kernel(groups, layers, score_scale, *refs):
    refs = list(refs)

    def take(count):
        taken, refs[:count] = refs[:count], []
        return taken

    inputs, cotangent, vectors, ids = take(4)
    raw = take(6)
    rows_out, grad_out, vectors_out, ids_out, block_out = take(5)
    wholes = take(groups)
    names = ("n1", "qkv", "att", "mid", "n2", "hid", "slope", "x")
    saved = [dict(zip(names, take(8))) for _ in range(layers)]
    box = dict(zip(names, take(8)))
    box["saved"], box["block"] = saved, block_out
    weights = take(4)
    for i in range(4):
        box[f"w{i}"] = weights[i]
    box["send"], box["got"], box["low"], box["vectors"] = take(4)
    own_ids, other_ids, box["seg_row"], box["seg_col"] = take(4)
    move = Mover(*refs)
    clock = Clock(LATENCY)
    plan = Plan(clock)
    move.greet()
    clock.now = 2.0
    loads, complete = {}, set()
    state = {"need": None, "begun": False, "loaded": -1, "used": 0}

    def prefetch():
        group = state["loaded"] + 1
        while group < groups and group in complete and (group < 4 or state["used"] > group - 4):
            loads[group] = move.keep(wholes[group], weights[group % 4])
            state["loaded"] = group
            group += 1

    def spread_next(group):
        if group < groups:
            plan.add(tasks[group])

    def completed(group):
        complete.add(group)
        prefetch()

    def halves(ref, layer):
        wide = ref.shape[2] // 2
        return tuple(
            ref.at[layer, :, pl.ds(pl.multiple_of(side * wide, 128), wide)]
            for side in (move.core, 1 - move.core)
        )

    kinds = (raw[:3], raw[3:4], raw[4:5], raw[5:6])
    tasks = [
        spread_group(
            move,
            plan,
            [halves(ref, i // 4) for ref in kinds[i % 4]],
            wholes[i],
            i,
            i % 4 == 1,
            partial(spread_next, i + 1),
            partial(completed, i),
        )
        for i in range(groups)
    ]
    ids_copy = move.send(ids, other_ids, move.sibling)
    ids_here = move.keep(ids, own_ids)
    plan.add(vector_stages(move, clock, vectors, vectors_out))
    plan.add(tasks[0])

    def need(group):
        state["need"], state["used"] = group, group
        prefetch()

    def load(group):
        loads.pop(group).wait()
        state["need"] = None

    box["need"], box["load"] = need, load
    ends = []

    def prepare():
        yield TOKENS_AT
        finish_rows = fetch_tokens(move, inputs, rows_out)
        clock.post(size_of(inputs), OVER_MID)
        yield TOKENS_AT + 33.0
        ids_copy.wait()
        ids_here.wait()
        ends.append(move.keep(other_ids, ids_out).wait)
        segment_rows(move, own_ids, other_ids, box["seg_row"], box["seg_col"])
        finish_rows()
        copies = [move.keep(rows_out, box["low"]), move.keep(vectors_out, box["vectors"])]
        for copy in copies:
            copy.wait()

        def body(i):
            rows = at(i, 64)
            box["x"][rows, :] = box["low"][rows, :].astype(float_type)

        loop(box["x"].shape[0] // 64, body)
        state["begun"] = True
        yield 100.0
        clock.post(size_of(inputs), OVER_MID)
        ends.append(fetch_tokens(move, cotangent, grad_out))

    plan.add(prepare())

    def ready():
        return state["begun"] and (state["need"] is None or state["need"] in loads)

    plan.run(forward_steps(move, score_scale, layers, box), ready, SCALE)
    for finish in ends:
        finish()


def forward_all(inputs, cotangent, vectors, ids, raw, layers, score_scale):
    groups = 4 * layers
    tokens, width = 2 * inputs.shape[1], inputs.shape[2]
    units = [w.shape[2] // 2 for w in raw]
    units = [sum(units[:3])] + units[3:]
    remote = 33 * groups + 16 + 4 * layers
    kept = [
        ((2 * tokens, width), brain_type),
        ((2 * tokens, 4 * units[0]), brain_type),
        ((2 * tokens, 4 * units[1]), brain_type),
        ((tokens, width), float_type),
        ((2 * tokens, width), brain_type),
        ((2 * tokens, 4 * units[2]), brain_type),
        ((2 * tokens, 4 * units[2]), brain_type),
        ((tokens, width), float_type),
    ]
    outs = pl.pallas_call(
        partial(forward_kernel, groups, layers, score_scale),
        out_shape=[
            jax.ShapeDtypeStruct((tokens, width), inputs.dtype),
            jax.ShapeDtypeStruct((tokens, width), inputs.dtype),
            jax.ShapeDtypeStruct((8, *vectors.shape), vectors.dtype),
            jax.ShapeDtypeStruct(ids.shape, ids.dtype),
            jax.ShapeDtypeStruct((tokens, width), brain_type),
        ]
        + [jax.ShapeDtypeStruct((width, 4 * u), brain_type) for _ in range(layers) for u in units]
        + [jax.ShapeDtypeStruct(*shape) for _ in range(layers) for shape in kept],
        in_specs=hbm(10),
        out_specs=hbm(5 + groups + 8 * layers),
        scratch_shapes=[pltpu.VMEM(*shape) for shape in kept]
        + [pltpu.VMEM((width, 4 * u), brain_type) for u in units]
        + [
            pltpu.VMEM((tokens, width), brain_type),
            pltpu.VMEM((tokens, width), brain_type),
            pltpu.VMEM((tokens, width), brain_type),
            pltpu.VMEM((8, *vectors.shape), vectors.dtype),
            pltpu.VMEM(ids.shape, ids.dtype),
            pltpu.VMEM(ids.shape, ids.dtype),
            pltpu.VMEM((1, 2 * tokens), float_type),
            pltpu.VMEM((2 * tokens, 128), float_type),
            pltpu.SemaphoreType.DMA((remote,)),
            pltpu.SemaphoreType.DMA((remote,)),
            pltpu.SemaphoreType.DMA((2 * groups + 10 + 12 * layers,)),
        ],
        compiler_params=pltpu.CompilerParams(
            collective_id=0, has_side_effects=True, vmem_limit_bytes=60 * 1024 * 1024
        ),
        name="forward",
    )(inputs, cotangent, vectors, ids, *raw)
    saved = [outs[5 + groups + 8 * i : 13 + groups + 8 * i] for i in range(layers)]
    return outs[1], outs[2], outs[3], outs[4], outs[5 : 5 + groups], saved


def hand_out(move, clock, loaded, out, units):
    n = units // len(out)
    rows = pl.ds(0, loaded.shape[1] // 2)
    lanes = pl.ds(pl.multiple_of(move.core * n, 128), n)
    copies = []
    for i, target in enumerate(out):
        columns = pl.ds(i * n, n)
        there = loaded.at[1 - move.core, rows, columns]
        copies.append(move.send(there, target.at[:, lanes], move.sibling))
        copies.append(move.keep(loaded.at[move.core, rows, columns], target.at[:, lanes]))
    yield clock.post(units * 512, OVER_CORE) + 1.0
    for copy in copies:
        copy.wait()


def collect_stages(move, clock, first, loaded, got, out, free, release):
    first_got, second_got, far_got, cross_got, near_got = got
    rows, units = loaded.shape[1] // 2, loaded.shape[2] // 4
    sides = ((move.x_side, OVER_X), (move.y_side, OVER_Y))
    done = [copy for copy, _ in first]

    def go(source, target, device, links):
        copy = move.send(source, target, device)
        done.append(copy)
        return copy, clock.post(size_of(source), links)

    def total(target, source, height, width):
        def body(i):
            span = (at(i, 32), pl.ds(0, width))
            target[span] = (
                target[span].astype(float_type) + source[span].astype(float_type)
            ).astype(brain_type)

        loop(height // 32, body)

    second = []
    for i in range(2):
        yield first[i][1]
        first[i][0].wait_recv()
        total(loaded.at[i], first_got.at[i], 2 * rows, 4 * units)
        second.append(go(loaded.at[i, pl.ds(rows, rows)], second_got.at[i], *sides[i]))
    free("near")
    free("across")
    base = move.remote
    move.remote += 6
    outer_lanes = pl.ds(2 * units, 2 * units)

    def far(i):
        source = loaded.at[i, pl.ds(0, rows), outer_lanes]
        return move.make(source, far_got.at[i], move.z_near, base + i, base + i)

    def cross(i):
        source = loaded.at[i, pl.ds(0, rows), outer_lanes]
        return move.make(source, cross_got.at[i], move.z_across, base + 2 + i, base + 2 + i)

    def near(i):
        source = loaded.at[i, pl.ds(0, rows), pl.ds(units, units)]
        return move.make(source, near_got.at[i], move.z_near, base + 4 + i, base + 4 + i)

    def lanes_total(i, source, pairs):
        def body(step):
            rows_here = at(step, 32)
            for lane, to_lane in pairs:
                span = (rows_here, pl.ds(to_lane * units, units))
                loaded[(i, *span)] = (
                    loaded[(i, *span)].astype(float_type)
                    + source[i, rows_here, pl.ds(lane * units, units)].astype(float_type)
                ).astype(brain_type)

        loop(rows // 32, body)

    far_due = []
    for i in range(2):
        yield second[i][1]
        second[i][0].wait_recv()
        total(loaded.at[i], second_got.at[i], rows, 4 * units)

        @pl.when(move.outer)
        def _():
            far(i).start()
            near(i).start()

        far_due.append(clock.post(size_of(far_got.at[i]), OVER_NEAR))
    cross_due = []
    for i in range(2):
        yield far_due[i]

        @pl.when(move.inner)
        def _():
            far(i).wait_recv()
            lanes_total(i, far_got, ((0, 3), (1, 2)))
            cross(i).start()

        cross_due.append(clock.post(size_of(far_got.at[i]), OVER_MID))
    near_due = []
    for i in range(2):
        yield cross_due[i]

        @pl.when(move.inner)
        def _():
            cross(i).wait_recv()
            lanes_total(i, cross_got, ((0, 1), (1, 0)))
            near(i).start()

        near_due.append(clock.post(size_of(near_got.at[i]), OVER_NEAR))
    yield max(near_due)
    for i in range(2):
        near(i).wait()
        lanes_total(i, near_got, ((0, 0),))

    @pl.when(move.outer)
    def _():
        for i in range(2):
            far(i).wait_send()

    @pl.when(move.inner)
    def _():
        for i in range(2):
            cross(i).wait_send()

    release()
    yield from hand_out(move, clock, loaded, out, units)
    for copy in done:
        copy.wait_send()


def vector_sum_stages(move, clock, vectors, sums, by_core, by_y, by_x, by_near, by_far, out):
    def go(source, target, device):
        return move.send(source, target, device), clock.now + 3.0

    copy, due = go(vectors.at[1 - move.core], by_core, move.sibling)
    yield due
    copy.wait()
    sums[...] = vectors[move.core] + by_core[...]
    copy, due = go(sums.at[pl.ds(2, 2)], by_y, move.y_side)
    yield due
    copy.wait()
    sums[:2] += by_y[...]
    copy, due = go(sums.at[1], by_x, move.x_side)
    yield due
    copy.wait()
    sums[0] += by_x[...]
    copy, due = go(sums.at[0], by_near, move.z_near)
    yield due
    copy.wait()
    sums[1] = sums[0] + by_near[...]
    copy, due = go(sums.at[1], by_far, move.z_across)
    yield due
    copy.wait()
    out[...] = sums[1] + by_far[...]


def backward_steps(move, plan, score_scale, layers, box, start_group):
    clock = plan.clock
    grad, below, source = box["grad"], box["below"], box["source"]
    branch, normed = box["branch"], box["normed"]
    upper, fc_in, hid, slope = box["upper"], box["fc_in"], box["hid"], box["slope"]
    send, got, sums = box["send"], box["got"], box["sums"]
    half = grad.shape[0]
    whole = 2 * half
    tile = 256
    qkv_width = box["layers"][0]["qkv"].shape[1]
    att_width = box["layers"][0]["att"].shape[1]
    wide = hid.shape[1]
    qkv_part, att_part = pl.ds(0, qkv_width), pl.ds(qkv_width, att_width)
    loads = {}

    def load(layer, name, target):
        loads[name] = move.keep(box["layers"][layer][name], target)

    def need(*names):
        for name in names:
            if name in loads:
                loads.pop(name).wait()

    def load_mlp(layer):
        load(layer, "hid", hid)
        load(layer, "w3", upper)
        load(layer, "slope", slope)

    def share_branch():
        def body(i):
            rows = at(i, 64)
            branch[rows, :] = grad[rows, :].astype(brain_type)

        loop(half // 64, body)
        return move.send(
            branch.at[pl.ds(0, half)], branch.at[pl.ds(half, half)], move.sibling
        )

    def weight_grads(kind, layer, left, right, first, width):
        group = start_group(kind, layer)
        step = width if width <= 1024 else width // 2
        for target, side, quarter, link in (
            ("sent", 0, 1, OVER_Y),
            ("sent", 1, 3, OVER_X),
            ("loaded", 0, 0, None),
            ("loaded", 1, 2, None),
        ):
            rows = left[:, pl.ds(quarter * 256, 256)]

            def body(i, target=target, side=side, rows=rows):
                part = right[:, pl.ds(pl.multiple_of(first + i * step, 128), step)]
                group[target][side, :, at(i, step)] = tn(rows, part).astype(brain_type)

            loop(width // step, body)
            if target == "sent":
                group["go"](side, link)
            yield 1.0 + width * 0.85e-3
        group["begin"]()

    def partial_sums(left, first, width, weight, at_column):
        def body(i):
            columns = at(i, tile)
            send[:, columns] = nt(
                left[pl.ds(half, half), pl.ds(first, width)],
                weight[columns, pl.ds(at_column, width)],
            ).astype(brain_type)

        loop(weight.shape[0] // tile, body)
        return move.send(send, got, move.sibling)

    def whole_sums(left, first, width, weight, at_column, copy):
        def product(i):
            columns = at(i, tile)
            below[:, columns] = nt(
                left[pl.ds(0, half), pl.ds(first, width)],
                weight[columns, pl.ds(at_column, width)],
            )

        loop(weight.shape[0] // tile, product)
        copy.wait()

    def norm_back(gain, grad_gain, grad_shift):
        gain_row = vector_row(box["vectors"], gain)
        sums[...] = jnp.zeros_like(sums)

        def body(i):
            rows = at(i, 64)
            unit, scale = center_of(source[rows, :])
            down = below[rows, :] + got[rows, :].astype(float_type)
            turn = down * gain_row
            grad[rows, :] += scale * (
                turn
                - jnp.mean(turn, axis=-1, keepdims=True)
                - unit * jnp.mean(turn * unit, axis=-1, keepdims=True)
            )
            sums[0:1, :] += jnp.sum(down * unit, axis=0, keepdims=True)
            sums[1:2, :] += jnp.sum(down, axis=0, keepdims=True)

        loop(half // 64, body)
        for row, index in ((0, grad_gain), (1, grad_shift)):
            for core in range(2):
                for spot in range(4):
                    to = spot if core == 0 else (0, 2, 1, 3)[spot]
                    box["vector_grads"][core, to, index : index + 1, :] = sums[
                        row : row + 1, pl.ds((core * 4 + spot) * 128, 128)
                    ]

    def slope_times(first):
        def body(i):
            rows, columns = pl.ds(first * half, half), at(i, tile)
            product = nn(branch[rows, :], upper[:, columns])
            slope[rows, columns] = (product * slope[rows, columns].astype(float_type)).astype(
                brain_type
            )

        loop(wide // tile, body)

    def attention(pair):
        keys_at, values_at = pl.ds(pair * 384 + 128, 128), pl.ds(pair * 384 + 256, 128)
        grad_keys, grad_values = box["grad_keys"], box["grad_values"]
        grad_keys[...] = jnp.zeros_like(grad_keys)
        grad_values[...] = jnp.zeros_like(grad_values)

        def body(part):
            rows = at(part, tile)
            low_lane = lax.broadcasted_iota(jnp.int32, (tile, 128), 1) < 64
            keys, values = hid[:, keys_at], hid[:, values_at]
            query = hid[rows, pl.ds(pair * 384, 128)]
            out_grad = slope[rows, pl.ds(qkv_width + pair * 128, 128)]
            same = box["seg_col"][:, :1] == box["seg_row"][:, rows]
            grad_queries = []
            for head in range(2):
                mine = low_lane if head == 0 else jnp.logical_not(low_lane)
                masked = jnp.where(mine, query, jnp.zeros_like(query))
                masked = masked * jnp.asarray(score_scale, brain_type)
                grad_masked = jnp.where(mine, out_grad, jnp.zeros_like(out_grad))
                scores = jnp.where(same, nt(keys, masked), -1e30)
                weight = jnp.exp(scores - jnp.max(scores, axis=0, keepdims=True))
                probs = weight * (1.0 / jnp.sum(weight, axis=0, keepdims=True))
                grad_probs = nt(values, grad_masked)
                inner = jnp.sum(probs * grad_probs, axis=0, keepdims=True)
                grad_raw = (probs * (grad_probs - inner)).astype(brain_type)
                grad_values[...] += nn(probs.astype(brain_type), grad_masked)
                grad_keys[...] += nn(grad_raw, masked)
                grad_queries.append(tn(grad_raw, keys))
            slope[rows, pl.ds(pair * 384, 128)] = (
                jnp.where(low_lane, grad_queries[0], grad_queries[1]) * score_scale
            ).astype(brain_type)

        loop(whole // tile, body)
        slope[:, keys_at] = grad_keys[...].astype(brain_type)
        slope[:, values_at] = grad_values[...].astype(brain_type)

    load_mlp(layers - 1)
    load(layers - 1, "n2", normed)
    load(layers - 1, "w2", fc_in)
    load(layers - 1, "mid", source)
    for layer in reversed(range(layers)):
        sent = share_branch()
        need("w3", "slope")
        yield 1.0
        slope_times(0)
        yield 4.0
        sent.wait()
        need("hid")
        yield from weight_grads(3, layer, branch, hid, 0, wide)
        load(layer, "qkv", hid.at[:, qkv_part])
        load(layer, "att", hid.at[:, att_part])
        slope_times(1)
        load(layer, "w0", upper.at[:, qkv_part])
        load(layer, "w1", upper.at[:, att_part])
        yield 4.0
        need("n2")
        yield from weight_grads(2, layer, normed, slope, 0, wide)
        load(layer, "n1", normed)
        need("w2")
        sent = partial_sums(slope, 0, wide, fc_in, 0)
        yield 3.5
        need("mid")
        whole_sums(slope, 0, wide, fc_in, 0, sent)
        if layer > 0:
            load(layer - 1, "w2", fc_in)
        yield 3.5
        norm_back(2 * layers + layer, 2 * layers + layer, 3 * layers + layer)
        load(layer, "x", source)
        sent = share_branch()
        need("w1")
        yield 5.0

        def grad_attended(first):
            rows = pl.ds(first * half, half)
            slope[rows, att_part] = nn(branch[rows, :], upper[:, att_part]).astype(brain_type)

        grad_attended(0)
        sent.wait()
        grad_attended(1)
        yield 2.0
        need("att")
        yield from weight_grads(1, layer, branch, hid, qkv_width, att_width)
        need("qkv")
        for pair in range(qkv_width // 384):
            attention(pair)
            yield 9.0
        need("n1")
        yield from weight_grads(0, layer, normed, slope, 0, qkv_width)
        if layer > 0:
            load(layer - 1, "n2", normed)
            load(layer - 1, "hid", hid)
        need("w0")
        sent = partial_sums(slope, 0, qkv_width, upper, 0)
        yield 3.0
        whole_sums(slope, 0, qkv_width, upper, 0, sent)
        if layer > 0:
            load(layer - 1, "w3", upper)
            load(layer - 1, "slope", slope)
        need("x")
        yield 3.0
        norm_back(layer, layer, layers + layer)
        if layer > 0:
            load(layer - 1, "mid", source)
        yield 4.0

    def body(i):
        rows = at(i, 64)
        send[rows, :] = grad[rows, :].astype(brain_type)

    loop(half // 64, body)


BACK_NAMES = ("n1", "qkv", "att", "mid", "n2", "hid", "slope", "x")


def backward_kernel(layers, score_scale, *refs):
    refs = list(refs)

    def take(count):
        taken, refs[:count] = refs[:count], []
        return taken

    kinds = 4
    groups = kinds * layers
    block, cotangent, vectors, ids, other_ids_in = take(5)
    weights = take(groups)
    saved = [dict(zip(BACK_NAMES, take(8))) for _ in range(layers)]
    for layer in range(layers):
        for kind in range(kinds):
            saved[layer][f"w{kind}"] = weights[kinds * layer + kind]
    block_out, below_out, vectors_out = take(3)
    outs = take(6)
    box = {"layers": saved}
    names = ("upper", "fc_in", "hid", "slope", "normed", "branch", "source", "grad", "below")
    box.update(zip(names, take(9)))
    names = ("send", "got", "grad_keys", "grad_values", "seg_row", "seg_col", "vectors", "sums")
    box.update(zip(names, take(8)))
    own_ids, other_ids, box["vector_grads"] = take(3)
    small = take(6)
    buffers = [take(7) for _ in range(kinds)]
    (credits,) = take(1)
    move = Mover(*refs)
    clock = Clock(SLACK)
    plan = Plan(clock)
    copies = [
        move.keep(cotangent, box["send"]),
        move.keep(vectors, box["vectors"]),
        move.keep(ids, own_ids),
        move.keep(other_ids_in, other_ids),
    ]
    move.greet()
    finish_above = return_tokens(move, block, block_out)
    for copy in copies:
        copy.wait()
    segment_rows(move, own_ids, other_ids, box["seg_row"], box["seg_col"])

    def body(i):
        rows = at(i, 64)
        box["grad"][rows, :] = box["send"][rows, :].astype(float_type)

    loop(box["grad"].shape[0] // 64, body)
    devices = {
        "x": move.x_side,
        "y": move.y_side,
        "across": move.z_across,
        "near": move.z_near,
    }
    order = list(devices)
    running = {}

    def start_group(kind, layer):
        if kind in running:
            plan.finish(running.pop(kind))
        sent, loaded, *got = buffers[kind]
        first = [None, None]

        def free(name):
            if layer < layers - 1:
                pl.semaphore_wait(credits.at[kind * 4 + order.index(name)], 1)

        def release():
            if layer > 0:
                for i, name in enumerate(order):
                    pl.semaphore_signal(
                        credits.at[kind * 4 + i],
                        inc=1,
                        device_id=devices[name],
                        device_id_type=pl.DeviceIdType.MESH,
                    )

        out = [
            ref.at[layer] for ref in (outs[:3], outs[3:4], outs[4:5], outs[5:6])[kind]
        ]

        def go(side, link):
            name = "y" if side == 0 else "x"
            free(name)
            copy = move.send(sent.at[side], got[0].at[side], devices[name])
            first[side] = (copy, clock.post(size_of(sent.at[side]), link))

        def begin():
            task = collect_stages(move, clock, first, loaded, got, out, free, release)
            plan.add(task)
            running[kind] = task

        return {"sent": sent, "loaded": loaded, "go": go, "begin": begin}

    def compute():
        yield from backward_steps(move, plan, score_scale, layers, box, start_group)
        ends.append(return_tokens(move, box["send"], below_out))
        plan.add(vector_sum_stages(move, clock, box["vector_grads"], *small, vectors_out))

    ends = [finish_above]
    plan.run(compute(), lambda: True)
    for finish in ends:
        finish()


def backward_all(block, cotangent, vectors, ids, other_ids, weights, saved, layers, score_scale):
    tokens, width = cotangent.shape
    units = [w.shape[1] for w in weights[:4]]
    count = len(weights)
    low, high = brain_type, float_type
    small_vectors = (2, 4, vectors.shape[1], vectors.shape[2])
    scratch = [((2 * tokens, units[2]), low)] * 4
    scratch += [((2 * tokens, width), low)] * 2
    scratch += [((tokens, width), high)] * 3
    scratch += [((tokens, width), low)] * 2
    scratch += [((2 * tokens, 128), high)] * 2
    scratch += [((1, 2 * tokens), high), ((2 * tokens, 128), high)]
    scratch += [(vectors.shape, high), ((8, width), high)]
    scratch += [(ids.shape, ids.dtype)] * 2
    scratch += [(small_vectors, high), (small_vectors[1:], high), (small_vectors[1:], high)]
    scratch += [((2, *small_vectors[2:]), high)] + [(small_vectors[2:], high)] * 3
    for wide in units:
        for rows, columns in ((256, 1), (256, 1), (256, 1), (128, 1), (128, 2), (128, 2), (128, 4)):
            scratch.append(((2, rows, wide // columns), low))
    remote = 16 * count + 9 + 4 * layers + 8
    outs = pl.pallas_call(
        partial(backward_kernel, layers, score_scale),
        out_shape=[jax.ShapeDtypeStruct((2, tokens // 2, width), low)] * 2
        + [jax.ShapeDtypeStruct(vectors.shape[1:], high)]
        + [jax.ShapeDtypeStruct((layers, 128, units[0] // 6), low)] * 3
        + [jax.ShapeDtypeStruct((layers, 128, w // 2), low) for w in units[1:]],
        in_specs=hbm(5 + count + 8 * layers),
        out_specs=hbm(2) + [pl.BlockSpec(memory_space=pltpu.VMEM)] + hbm(6),
        scratch_shapes=[pltpu.VMEM(*shape) for shape in scratch]
        + [
            pltpu.SemaphoreType.REGULAR((16,)),
            pltpu.SemaphoreType.DMA((remote,)),
            pltpu.SemaphoreType.DMA((remote,)),
            pltpu.SemaphoreType.DMA((8 + 14 * layers + 2 * count,)),
        ],
        compiler_params=pltpu.CompilerParams(
            collective_id=1, has_side_effects=True, vmem_limit_bytes=62 * 1024 * 1024
        ),
        name="backward",
    )(block, cotangent, vectors, ids, other_ids, *weights, *[a for kept in saved for a in kept])
    return outs[:2], outs[2], outs[3:]


def per_chip(
    inputs,
    segment_ids,
    norm1_gain,
    norm1_shift,
    w_query,
    w_key,
    w_value,
    w_output,
    norm2_gain,
    norm2_shift,
    w_fc_in,
    w_fc_out,
    cotangent,
):
    layers = norm1_gain.shape[0]
    head_width = inputs.shape[3] // HEADS
    score_scale = 1.0 / math.sqrt(head_width)
    vectors = jnp.concatenate([norm1_gain, norm1_shift, norm2_gain, norm2_shift], axis=0)
    grad, vectors, other_ids, block, weights, saved = forward_all(
        inputs[:, 0],
        cotangent[:, 0],
        vectors.astype(float_type),
        segment_ids,
        (w_query, w_key, w_value, w_output.mT, w_fc_in, w_fc_out.mT),
        layers,
        score_scale,
    )
    tokens, vector_grads, outs = backward_all(
        block, grad, vectors, segment_ids, other_ids, weights, saved, layers, score_scale
    )
    block_output, input_grad = (part.astype(float_type) for part in tokens)
    grad_query, grad_key, grad_value, grad_output, grad_fc_in, grad_fc_out = outs
    grad_output, grad_fc_out = grad_output.mT, grad_fc_out.mT
    gain_one, shift_one, gain_two, shift_two = (
        vector_grads[i * layers : (i + 1) * layers] for i in range(4)
    )
    return (
        block_output[:, None],
        input_grad[:, None],
        gain_one,
        shift_one,
        grad_query.astype(float_type),
        grad_key.astype(float_type),
        grad_value.astype(float_type),
        grad_output.astype(float_type),
        gain_two,
        shift_two,
        grad_fc_in.astype(float_type),
        grad_fc_out.astype(float_type),
    )


def layer_norm(token_rows, gain_vec, shift_vec):
    center = token_rows - jnp.mean(token_rows, axis=-1, keepdims=True)
    spread = jnp.mean(center * center, axis=-1, keepdims=True)
    return center * lax.rsqrt(spread + 1e-05) * gain_vec + shift_vec


def normed_local(token_rows, gain_vec, shift_vec):
    return layer_norm(token_rows, gain_vec.astype(float_type), shift_vec.astype(float_type)).astype(
        brain_type
    )


def normed_send(token_rows, gain_vec, shift_vec):
    return lax.all_gather(
        normed_local(token_rows, gain_vec, shift_vec), "tensor", axis=0, tiled=True
    )


def normed_resend(token_rows, gain_vec, shift_vec):
    return lax.all_gather(
        normed_local(token_rows, gain_vec, shift_vec), "tensor", axis=0, tiled=True
    )


def branch_total(partial_sum):
    return lax.psum_scatter(
        partial_sum.astype(jnp.bfloat16), "tensor", scatter_dimension=0, tiled=True
    ).astype(jnp.float32)


def branch_cotangent(grad_rows):
    return lax.all_gather(grad_rows.astype(brain_type), "tensor", axis=0, tiled=True)


def input_total(partial_sum):
    return lax.psum_scatter(
        partial_sum.astype(jnp.bfloat16), "tensor", scatter_dimension=0, tiled=True
    ).astype(jnp.float32)


def norm_backward(token_rows, gain_vec, shift_vec, grad_normed):
    _, norm_pull = jax.vjp(
        layer_norm, token_rows, gain_vec.astype(float_type), shift_vec.astype(float_type)
    )
    return norm_pull(grad_normed)


def masked_scores(query_part, segment_part, key_heads, segment, score_scale):
    raw_scores = jnp.einsum(
        "qhd,khd->hqk", query_part, key_heads, preferred_element_type=float_type
    )
    same_scene = segment_part[:, None] == segment[None, :]
    return jnp.where(same_scene[None], raw_scores * score_scale, -1e30)


def attend_forward(queries, key_heads, values, segment, block_rows):
    seq_len, head_count, head_width = queries.shape
    score_scale = 1.0 / math.sqrt(head_width)
    block_count = seq_len // block_rows

    def one_block(block_pair):
        query_part, segment_part = block_pair
        scores = masked_scores(query_part, segment_part, key_heads, segment, score_scale)
        row_max = jnp.max(scores, axis=-1, keepdims=True)
        exp_scores = jnp.exp(scores - row_max)
        row_total = jnp.sum(exp_scores, axis=-1, keepdims=True)
        probabilities = (exp_scores / row_total).astype(brain_type)
        block_out = jnp.einsum(
            "hqk,khd->qhd", probabilities, values, preferred_element_type=float_type
        )
        log_total = (row_max + jnp.log(row_total))[..., 0]
        return (block_out.astype(brain_type), log_total)

    query_blocks = queries.reshape(block_count, block_rows, head_count, head_width)
    segment_blocks = segment.reshape(block_count, block_rows)
    outputs, log_totals = lax.map(one_block, (query_blocks, segment_blocks))
    return (outputs.reshape(seq_len, head_count * head_width), log_totals)


def attend_backward(queries, key_heads, values, segment, log_totals, grad_out, block_rows):
    seq_len, head_count, head_width = queries.shape
    score_scale = 1.0 / math.sqrt(head_width)
    block_count = seq_len // block_rows

    def one_block(carry_pair, block_items):
        grad_keys, grad_values = carry_pair
        query_part, segment_part, log_part, grad_part = block_items
        scores = masked_scores(query_part, segment_part, key_heads, segment, score_scale)
        probabilities = jnp.exp(scores - log_part[..., None])
        grad_probs = jnp.einsum(
            "qhd,khd->hqk", grad_part, values, preferred_element_type=float_type
        )
        row_inner = jnp.sum(probabilities * grad_probs, axis=-1, keepdims=True)
        grad_raw = (probabilities * (grad_probs - row_inner) * score_scale).astype(brain_type)
        grad_query = jnp.einsum(
            "hqk,khd->qhd", grad_raw, key_heads, preferred_element_type=float_type
        )
        grad_keys = grad_keys + jnp.einsum(
            "hqk,qhd->khd", grad_raw, query_part, preferred_element_type=float_type
        )
        grad_values = grad_values + jnp.einsum(
            "hqk,qhd->khd",
            probabilities.astype(brain_type),
            grad_part,
            preferred_element_type=float_type,
        )
        return ((grad_keys, grad_values), grad_query.astype(brain_type))

    zero_heads = jnp.zeros((seq_len, head_count, head_width), float_type)
    block_items = (
        queries.reshape(block_count, block_rows, head_count, head_width),
        segment.reshape(block_count, block_rows),
        log_totals,
        grad_out.reshape(block_count, block_rows, head_count, head_width),
    )
    (grad_keys, grad_values), grad_queries = lax.scan(
        one_block, (zero_heads, zero_heads), block_items
    )
    flat_shape = (seq_len, head_count * head_width)
    return (
        grad_queries.reshape(flat_shape),
        grad_keys.astype(brain_type).reshape(flat_shape),
        grad_values.astype(brain_type).reshape(flat_shape),
    )


def fresh_totals(layers, attn_width, hidden_width):
    vector_zero = jnp.zeros((layers, D), float_type)
    column_zero = jnp.zeros((layers, D, attn_width), float_type)
    return [
        vector_zero,
        vector_zero,
        column_zero,
        column_zero,
        column_zero,
        jnp.zeros((layers, attn_width, D), float_type),
        vector_zero,
        vector_zero,
        jnp.zeros((layers, D, hidden_width), float_type),
        jnp.zeros((layers, hidden_width, D), float_type),
    ]


def add_into(grad_totals, position, layer_index, term):
    grad_totals[position] = grad_totals[position].at[layer_index].add(term)


def per_device(
    inputs,
    segment_ids,
    norm1_gain,
    norm1_shift,
    w_query,
    w_key,
    w_value,
    w_output,
    norm2_gain,
    norm2_shift,
    w_fc_in,
    w_fc_out,
    cotangent,
):
    micro_count = inputs.shape[0]
    layers = norm1_gain.shape[0]
    seq_len = segment_ids.shape[2]
    block_rows = min(512, seq_len)
    head_width = D // HEADS
    attn_width = w_query.shape[2]
    hidden_width = w_fc_in.shape[2]
    grad_totals = fresh_totals(layers, attn_width, hidden_width)
    reduced = None
    output_list = []
    input_grad_list = []
    for micro_index in range(micro_count):
        token_rows = inputs[micro_index, 0].astype(float_type)
        segment = segment_ids[micro_index, 0]
        saved_state = []
        for layer_index in range(layers):
            weights = (
                lax.all_gather(norm1_gain[layer_index], "dp", axis=0, tiled=True),
                lax.all_gather(norm1_shift[layer_index], "dp", axis=0, tiled=True),
                lax.all_gather(w_query[layer_index], "dp", axis=0, tiled=True),
                lax.all_gather(w_key[layer_index], "dp", axis=0, tiled=True),
                lax.all_gather(w_value[layer_index], "dp", axis=0, tiled=True),
                lax.all_gather(w_output[layer_index], "dp", axis=1, tiled=True),
                lax.all_gather(norm2_gain[layer_index], "dp", axis=0, tiled=True),
                lax.all_gather(norm2_shift[layer_index], "dp", axis=0, tiled=True),
                lax.all_gather(w_fc_in[layer_index], "dp", axis=0, tiled=True),
                lax.all_gather(w_fc_out[layer_index], "dp", axis=1, tiled=True),
            )
            (
                gain_one,
                shift_one,
                query_w,
                key_w,
                value_w,
                output_w,
                gain_two,
                shift_two,
                fc_in_w,
                fc_out_w,
            ) = weights
            whole_weights = None
            normed = normed_send(token_rows, gain_one, shift_one)
            queries = jnp.dot(normed, query_w, preferred_element_type=float_type).astype(brain_type)
            key_heads = jnp.dot(normed, key_w, preferred_element_type=float_type).astype(brain_type)
            values = jnp.dot(normed, value_w, preferred_element_type=float_type).astype(brain_type)
            attended, log_totals = attend_forward(
                queries.reshape(seq_len, -1, head_width),
                key_heads.reshape(seq_len, -1, head_width),
                values.reshape(seq_len, -1, head_width),
                segment,
                block_rows,
            )
            mid_rows = token_rows + branch_total(
                jnp.dot(attended, output_w, preferred_element_type=float_type)
            )
            normed_two = normed_send(mid_rows, gain_two, shift_two)
            pre_act = jnp.dot(normed_two, fc_in_w, preferred_element_type=float_type)
            hidden = jax.nn.gelu(pre_act, approximate=False).astype(brain_type)
            next_rows = mid_rows + branch_total(
                jnp.dot(hidden, fc_out_w, preferred_element_type=float_type)
            )
            saved_state.append(
                (
                    token_rows,
                    mid_rows,
                    weights,
                    normed,
                    normed_two,
                    queries,
                    key_heads,
                    values,
                    attended,
                    log_totals,
                    pre_act,
                    hidden,
                    whole_weights,
                )
            )
            token_rows = next_rows
        output_list.append(token_rows)
        grad_rows = cotangent[micro_index, 0].astype(float_type)
        for layer_index in reversed(range(layers)):
            (
                layer_rows,
                mid_rows,
                weights,
                normed,
                normed_two,
                queries,
                key_heads,
                values,
                attended,
                log_totals,
                pre_act,
                hidden,
                whole_weights,
            ) = saved_state[layer_index]
            weights = (
                lax.all_gather(norm1_gain[layer_index], "dp", axis=0, tiled=True),
                lax.all_gather(norm1_shift[layer_index], "dp", axis=0, tiled=True),
                lax.all_gather(w_query[layer_index], "dp", axis=0, tiled=True),
                lax.all_gather(w_key[layer_index], "dp", axis=0, tiled=True),
                lax.all_gather(w_value[layer_index], "dp", axis=0, tiled=True),
                lax.all_gather(w_output[layer_index], "dp", axis=1, tiled=True),
                lax.all_gather(norm2_gain[layer_index], "dp", axis=0, tiled=True),
                lax.all_gather(norm2_shift[layer_index], "dp", axis=0, tiled=True),
                lax.all_gather(w_fc_in[layer_index], "dp", axis=0, tiled=True),
                lax.all_gather(w_fc_out[layer_index], "dp", axis=1, tiled=True),
            )
            (
                gain_one,
                shift_one,
                query_w,
                key_w,
                value_w,
                output_w,
                gain_two,
                shift_two,
                fc_in_w,
                fc_out_w,
            ) = weights
            normed = normed_resend(layer_rows, gain_one, shift_one)
            normed_two = normed_resend(mid_rows, gain_two, shift_two)
            grad_branch = branch_cotangent(grad_rows)
            add_into(
                grad_totals,
                9,
                layer_index,
                jnp.einsum("sf,sd->fd", hidden, grad_branch, preferred_element_type=float_type),
            )
            grad_hidden = jnp.einsum(
                "sd,fd->sf", grad_branch, fc_out_w, preferred_element_type=float_type
            )
            _, gelu_pull = jax.vjp(partial(jax.nn.gelu, approximate=False), pre_act)
            grad_pre = gelu_pull(grad_hidden)[0].astype(brain_type)
            add_into(
                grad_totals,
                8,
                layer_index,
                jnp.einsum("sd,sf->df", normed_two, grad_pre, preferred_element_type=float_type),
            )
            grad_normed = input_total(
                jnp.einsum("sf,df->sd", grad_pre, fc_in_w, preferred_element_type=float_type)
            )
            grad_mid_part, grad_gain, grad_shift = norm_backward(
                mid_rows, gain_two, shift_two, grad_normed
            )
            add_into(grad_totals, 6, layer_index, grad_gain)
            add_into(grad_totals, 7, layer_index, grad_shift)
            grad_mid = grad_rows + grad_mid_part
            grad_branch = branch_cotangent(grad_mid)
            add_into(
                grad_totals,
                5,
                layer_index,
                jnp.einsum("sa,sd->ad", attended, grad_branch, preferred_element_type=float_type),
            )
            grad_attended = jnp.einsum(
                "sd,ad->sa", grad_branch, output_w, preferred_element_type=float_type
            ).astype(brain_type)
            grad_queries, grad_keys, grad_values = attend_backward(
                queries.reshape(seq_len, -1, head_width),
                key_heads.reshape(seq_len, -1, head_width),
                values.reshape(seq_len, -1, head_width),
                segment,
                log_totals,
                grad_attended.reshape(seq_len, -1, head_width),
                block_rows,
            )
            add_into(
                grad_totals,
                2,
                layer_index,
                jnp.einsum("sd,sa->da", normed, grad_queries, preferred_element_type=float_type),
            )
            add_into(
                grad_totals,
                3,
                layer_index,
                jnp.einsum("sd,sa->da", normed, grad_keys, preferred_element_type=float_type),
            )
            add_into(
                grad_totals,
                4,
                layer_index,
                jnp.einsum("sd,sa->da", normed, grad_values, preferred_element_type=float_type),
            )
            grad_input_part = jnp.einsum(
                "sa,da->sd", grad_queries, query_w, preferred_element_type=float_type
            )
            grad_input_part = grad_input_part + jnp.einsum(
                "sa,da->sd", grad_keys, key_w, preferred_element_type=float_type
            )
            grad_input_part = grad_input_part + jnp.einsum(
                "sa,da->sd", grad_values, value_w, preferred_element_type=float_type
            )
            grad_normed = input_total(grad_input_part)
            grad_below, grad_gain, grad_shift = norm_backward(
                layer_rows, gain_one, shift_one, grad_normed
            )
            add_into(grad_totals, 0, layer_index, grad_gain)
            add_into(grad_totals, 1, layer_index, grad_shift)
            grad_rows = grad_mid + grad_below
        input_grad_list.append(grad_rows)
    reduced = (
        lax.psum_scatter(
            grad_totals[0].astype(jnp.bfloat16), "dp", scatter_dimension=1, tiled=True
        ).astype(jnp.float32),
        lax.psum_scatter(
            grad_totals[1].astype(jnp.bfloat16), "dp", scatter_dimension=1, tiled=True
        ).astype(jnp.float32),
        lax.psum_scatter(
            grad_totals[2].astype(jnp.bfloat16), "dp", scatter_dimension=1, tiled=True
        ).astype(jnp.float32),
        lax.psum_scatter(
            grad_totals[3].astype(jnp.bfloat16), "dp", scatter_dimension=1, tiled=True
        ).astype(jnp.float32),
        lax.psum_scatter(
            grad_totals[4].astype(jnp.bfloat16), "dp", scatter_dimension=1, tiled=True
        ).astype(jnp.float32),
        lax.psum_scatter(
            grad_totals[5].astype(jnp.bfloat16), "dp", scatter_dimension=2, tiled=True
        ).astype(jnp.float32),
        lax.psum_scatter(
            grad_totals[6].astype(jnp.bfloat16), "dp", scatter_dimension=1, tiled=True
        ).astype(jnp.float32),
        lax.psum_scatter(
            grad_totals[7].astype(jnp.bfloat16), "dp", scatter_dimension=1, tiled=True
        ).astype(jnp.float32),
        lax.psum_scatter(
            grad_totals[8].astype(jnp.bfloat16), "dp", scatter_dimension=1, tiled=True
        ).astype(jnp.float32),
        lax.psum_scatter(
            grad_totals[9].astype(jnp.bfloat16), "dp", scatter_dimension=2, tiled=True
        ).astype(jnp.float32),
    )
    norm_sums = lax.psum((reduced[0], reduced[1], reduced[6], reduced[7]), "tensor")
    block_output = jnp.stack(output_list)[:, None]
    input_grad = jnp.stack(input_grad_list)[:, None]
    return (
        block_output,
        input_grad,
        norm_sums[0],
        norm_sums[1],
        reduced[2],
        reduced[3],
        reduced[4],
        reduced[5],
        norm_sums[2],
        norm_sums[3],
        reduced[8],
        reduced[9],
    )


def solution(mesh):
    placed = (
        P(None, "dp", "tensor", None),
        P(None, "dp", None),
        P(None, "dp"),
        P(None, "dp"),
        P(None, "dp", "tensor"),
        P(None, "dp", "tensor"),
        P(None, "dp", "tensor"),
        P(None, "tensor", "dp"),
        P(None, "dp"),
        P(None, "dp"),
        P(None, "dp", "tensor"),
        P(None, "tensor", "dp"),
        P(None, "dp", "tensor", None),
    )
    line, plane = mesh.shape["tensor"], mesh.shape["dp"]
    fits = line == 4 and plane == 8 and 2 * line == plane
    return jax.shard_map(
        per_chip if fits else per_device,
        mesh=mesh,
        in_specs=placed,
        out_specs=(
            P(None, "dp", "tensor", None),
            P(None, "dp", "tensor", None),
            P(None, "dp"),
            P(None, "dp"),
            P(None, "dp", "tensor"),
            P(None, "dp", "tensor"),
            P(None, "dp", "tensor"),
            P(None, "tensor", "dp"),
            P(None, "dp"),
            P(None, "dp"),
            P(None, "dp", "tensor"),
            P(None, "tensor", "dp"),
        ),
        check_vma=False,
    )
```
